32 devices in a mesh: wide: 8 (over z, x), narrow: 4 (over y, core).
Axes of the slice: x: 2, y: 2, z: 4, core: 2. Of those that a mesh axis runs over, the one named last changes fastest.
Arguments:
- frames: bfloat16 [32768, 1024], P(('wide', 'narrow')), may hold values from -6 to 6
- skip: bfloat16 [32768, 1024], P(('wide', 'narrow')), may hold values from -6 to 6
- lengths: int32 [32, 8], P(('wide', 'narrow')), may hold values from 0 to 1024, as said below
- key_mask: int32 [32768], P(('wide', 'narrow')), may hold values 0 or 1
- cotangent: bfloat16 [32768, 1024], P(('wide', 'narrow')), may hold values from -6 to 6
- w_skip: bfloat16 [2048, 1024], P(('wide', 'narrow')), may hold values from -0.125 to 0.125
- b_skip: bfloat16 [1024], P(('wide', 'narrow')), may hold values from -2 to 2
- pre_attn_gain: bfloat16 [1024], P(('wide', 'narrow')), may hold values from 0.5 to 1.5
- pre_attn_bias: bfloat16 [1024], P(('wide', 'narrow')), may hold values from -1.5 to 1.5
- w_qkv: bfloat16 [1024, 3072], P(('wide', 'narrow')), may hold values from -0.1875 to 0.1875
- b_query: bfloat16 [1024], P(('wide', 'narrow')), may hold values from -2 to 2
- b_value: bfloat16 [1024], P(('wide', 'narrow')), may hold values from -2 to 2
- w_out: bfloat16 [1024, 1024], P(('wide', 'narrow')), may hold values from -0.75 to 0.75
- b_out: bfloat16 [1024], P(('wide', 'narrow')), may hold values from -2 to 2
- pre_ffn_gain: bfloat16 [1024], P(('wide', 'narrow')), may hold values from 0.5 to 1.5
- pre_ffn_bias: bfloat16 [1024], P(('wide', 'narrow')), may hold values from -1.5 to 1.5
- w_up: bfloat16 [1024, 4096], P(('wide', 'narrow')), may hold values from -0.1875 to 0.1875
- b_up: bfloat16 [4096], P(('wide', 'narrow')), may hold values from -2 to 2
- w_down: bfloat16 [4096, 1024], P(('wide', 'narrow')), may hold values from -0.09375 to 0.09375
- b_down: bfloat16 [1024], P(('wide', 'narrow')), may hold values from -2 to 2
Outputs:
- layer_out: bfloat16 [32768, 1024], P(('wide', 'narrow'))
- grad_frames: bfloat16 [32768, 1024], P(('wide', 'narrow'))
- grad_skip: bfloat16 [32768, 1024], P(('wide', 'narrow'))
- grad_w_skip: float32 [2048, 1024], P(('wide', 'narrow'))
- grad_b_skip: float32 [1024], P(('wide', 'narrow'))
- grad_pre_attn_gain: float32 [1024], P(('wide', 'narrow'))
- grad_pre_attn_bias: float32 [1024], P(('wide', 'narrow'))
- grad_w_qkv: float32 [1024, 3072], P(('wide', 'narrow'))
- grad_b_query: float32 [1024], P(('wide', 'narrow'))
- grad_b_value: float32 [1024], P(('wide', 'narrow'))
- grad_w_out: float32 [1024, 1024], P(('wide', 'narrow'))
- grad_b_out: float32 [1024], P(('wide', 'narrow'))
- grad_pre_ffn_gain: float32 [1024], P(('wide', 'narrow'))
- grad_pre_ffn_bias: float32 [1024], P(('wide', 'narrow'))
- grad_w_up: float32 [1024, 4096], P(('wide', 'narrow'))
- grad_b_up: float32 [4096], P(('wide', 'narrow'))
- grad_w_down: float32 [4096, 1024], P(('wide', 'narrow'))
- grad_b_down: float32 [1024], P(('wide', 'narrow'))
The draws below stay inside these ranges and needn't reach their ends.
Inputs may be any that keep to these rules, and one draw needn't show every extreme that they name: `lengths`: each row sums to at most 1024; zeros stand only after the last utterance of a row; every row holds at least one utterance, and in every draw some row holds one utterance of exactly 1024 frames.
All inputs are finite; a program needn't handle non-finite values. No bound on the sum of `key_mask` on one device may be relied on, other than what follows from the above.
Results may differ from the reference program's by a relative error of at most 0.014.
Values may be sent and summed in bfloat16 or wider, within the bound.
No kernel may reach another device: no remote copies, remote signals or barrier semaphores. Data moves between devices by JAX's collectives and lax.ppermute only.
A program may use at most 320 MiB of HBM per device.

```python
import jax
import jax.numpy as jnp
from jax import lax

D = 1024
HEADS = 16
FF = 4096
TOK_DEV = 1024
UTT = 8
HEAD_DIM = 64
TOKENS = 32768


def draw_lengths(key, part):
    key = jax.random.fold_in(key, 11)
    key_short, key_pick, key_forced = jax.random.split(key, 3)
    row_count = TOKENS // TOK_DEV
    short_len = jax.random.randint(key_short, (row_count, UTT), 1 + TOK_DEV // 32, 1 + TOK_DEV // 4)
    running = jnp.cumsum(short_len, axis=1)
    short_len = jnp.where(running <= TOK_DEV, short_len, 0)
    picked = jax.random.randint(key_pick, (row_count,), 0, 8) == 0
    forced_row = jax.random.randint(key_forced, (), 0, row_count)
    long_rows = picked | (jnp.arange(row_count) == forced_row)
    long_len = jnp.where(jnp.arange(UTT) == 0, TOK_DEV, 0)
    return jnp.where(long_rows[:, None], long_len[None, :], short_len).astype(jnp.int32)


def plant(entries, rng, least, largest):
    place = [jax.random.randint(jax.random.fold_in(rng, axis), (), 0, length) for axis, length in enumerate(entries.shape)]
    main_axis = entries.shape.index(max(entries.shape))
    neighbour = place[:main_axis] + [(place[main_axis] + 1) % entries.shape[main_axis]] + place[main_axis + 1:]
    return entries.at[tuple(place)].set(least).at[tuple(neighbour)].set(largest)


def raised(values, own_key, source, target, parts, factor):
    owner, partner = [(jnp.arange(values.shape[axis_at]) // (values.shape[axis_at] // parts)).reshape([-1 if axis == axis_at else 1 for axis in range(values.ndim)]) for axis_at in (source, target)]
    chosen = jax.random.permutation(own_key, parts)[partner]
    strong = (owner == chosen) | (owner == (partner + parts // 2) % parts)
    return jnp.where(strong, factor * values, values)


def level_of(own_key, dims, shards, low, high):
    level, own = 1.0, jax.random.fold_in(own_key, 6)
    for axis_at, shards_of in shards:
        steps = jnp.exp(jax.random.uniform(jax.random.fold_in(own, axis_at), (shards_of,), jnp.float32, low / len(shards), high / len(shards)))
        level = level * jnp.repeat(steps, dims[axis_at] // shards_of).reshape([-1 if axis == axis_at else 1 for axis in range(len(dims))])
    return level


def centred(stream_key, shape, scale, most, cuts=(), kind=jnp.bfloat16):
    factor_of = level_of(stream_key, shape, cuts, -0.22, 0.18) if cuts else 1.0
    array = jax.random.normal(stream_key, shape, jnp.float32) * scale * factor_of
    return jnp.minimum(jnp.maximum(array, -most), most).astype(kind)


def gaussian_with(rng, dims, scale, most, pieces, heavy, kind=jnp.bfloat16):
    array = scale * jax.random.normal(rng, dims, jnp.float32)
    if pieces:
        array = array * level_of(rng, dims, pieces, -0.22, 0.18)
    return jnp.clip(raised(array, jax.random.fold_in(rng, 3), *heavy), -most, most).astype(kind)


def setup_inputs(seed: int = 0) -> dict:
    key_list = jax.random.split(jax.random.key(seed), 21)
    return {
        "frames": gaussian_with(key_list[0], (TOKENS, D), 1.0, 6.0, ((0, 32),), (0, 1, 32, 2.75)),
        "skip": gaussian_with(key_list[1], (TOKENS, D), 1.0, 6.0, ((0, 32),), (0, 1, 32, 2.75)),
        "lengths": draw_lengths(jax.random.fold_in(key_list[20], 71), 0),
        "key_mask": plant((jax.random.randint(key_list[3], (TOKENS,), 0, 8) < 7).astype(jnp.int32), jax.random.fold_in(key_list[3], 1), 0, 1),
        "cotangent": gaussian_with(key_list[4], (TOKENS, D), 1.0, 6.0, ((0, 32),), (0, 1, 32, 2.75)),
        "w_skip": centred(key_list[5], (2 * D, D), (2 * D) ** -0.5, 0.125, ((0, 32),)),
        "b_skip": centred(key_list[6], (D,), 0.3, 2.0, ((0, 32),)),
        "pre_attn_gain": jnp.clip(1.0 + 0.1 * jax.random.normal(key_list[7], (D,), jnp.float32), 0.5, 1.5).astype(jnp.bfloat16),
        "pre_attn_bias": centred(key_list[8], (D,), 0.2, 1.5, ((0, 32),)),
        "w_qkv": centred(key_list[9], (D, 3 * D), D ** -0.5, 0.1875, ((0, 32),)),
        "b_query": centred(key_list[10], (D,), 0.3, 2.0, ((0, 32),)),
        "b_value": centred(key_list[11], (D,), 0.3, 2.0, ((0, 32),)),
        "w_out": centred(key_list[12], (D, D), (D // 16) ** -0.5, 0.75, ((0, 32),)),
        "b_out": centred(key_list[13], (D,), 0.3, 2.0, ((0, 32),)),
        "pre_ffn_gain": jnp.clip(1.0 + 0.1 * jax.random.normal(key_list[14], (D,), jnp.float32), 0.5, 1.5).astype(jnp.bfloat16),
        "pre_ffn_bias": centred(key_list[15], (D,), 0.2, 1.5, ((0, 32),)),
        "w_up": centred(key_list[16], (D, FF), D ** -0.5, 0.1875, ((0, 32),)),
        "b_up": centred(key_list[17], (FF,), 0.3, 2.0, ((0, 32),)),
        "w_down": centred(key_list[18], (FF, D), FF ** -0.5, 0.09375, ((0, 32),)),
        "b_down": centred(key_list[19], (D,), 0.3, 2.0, ((0, 32),)),
    }


@jax.custom_vjp
def low(v):
    return lax.optimization_barrier(v.astype(jnp.bfloat16)).astype(jnp.float32)

@jax.custom_vjp
def low_back(v):
    return v

def low_keep(v):
    return (low(v), None)

def low_pass(kept, grad):
    return (grad,)

def back_keep(v):
    return (v, None)

def back_low(kept, grad):
    return (low(grad),)
low.defvjp(low_keep, low_pass)
low_back.defvjp(back_keep, back_low)
EPSILON = 1e-05
MASKED = -1e+30

def matmul(left_op, right_op):
    return jnp.dot(left_op, right_op, precision=lax.Precision.HIGHEST, preferred_element_type=jnp.float32)

def norm_apply(hidden, gain_vec, shift_vec):
    center = hidden - lax.optimization_barrier(jnp.mean(hidden, axis=1, keepdims=True))
    spread = lax.optimization_barrier(jnp.mean(center * center, axis=1, keepdims=True))
    return center * lax.rsqrt(spread + EPSILON) * gain_vec + shift_vec

def gelu_tanh(v):
    return 0.5 * v * (1.0 + jnp.tanh(0.7978845608 * (v + 0.044715 * v * v * v)))

def segment_layout(length_row, mask_row):
    utter_ends = jnp.cumsum(length_row).astype(jnp.int32)
    slot_ids = jnp.arange(TOK_DEV, dtype=jnp.int32)
    segment = lax.optimization_barrier(jnp.sum((slot_ids[:, None] >= utter_ends[None, :]).astype(jnp.int32), axis=1))
    in_use = slot_ids < utter_ends[-1]
    key_live = in_use & (mask_row == 1)
    return (segment, in_use, key_live)

def attend_pack(queries, keys_all, values, segment, in_use, key_live):
    block_rows = min(512, TOK_DEV)
    block_count = TOK_DEV // block_rows
    slopes = jnp.exp2(-8.0 * (jnp.arange(HEADS, dtype=jnp.float32) + 1.0) / HEADS)
    col_ids = jnp.arange(TOK_DEV, dtype=jnp.int32)

    def block_fn(inputs):
        query_block, offset = inputs
        row_ids = offset + jnp.arange(block_rows, dtype=jnp.int32)
        raw = jnp.einsum('qhd,khd->hqk', query_block, keys_all, precision=lax.Precision.HIGHEST) * HEAD_DIM ** (-0.5)
        distance = jnp.abs(row_ids[:, None] - col_ids[None, :]).astype(jnp.float32)
        scores = low_back(raw - slopes[:, None, None] * distance[None])
        row_segment = lax.dynamic_slice_in_dim(segment, offset, block_rows)
        row_use = lax.dynamic_slice_in_dim(in_use, offset, block_rows)
        allowed = (row_segment[:, None] == segment[None, :]) & row_use[:, None] & key_live[None, :] | (row_ids[:, None] == col_ids[None, :])
        masked = jnp.where(allowed[None], scores, MASKED)
        top_val = lax.optimization_barrier(jnp.max(masked, axis=2, keepdims=True))
        expo = jnp.exp(masked - top_val)
        probs = low(expo / lax.optimization_barrier(jnp.sum(expo, axis=2, keepdims=True)))
        return jnp.einsum('hqk,khd->qhd', probs, values, precision=lax.Precision.HIGHEST)
    query_blocks = queries.reshape(block_count, block_rows, HEADS, HEAD_DIM)
    offsets = jnp.arange(block_count, dtype=jnp.int32) * block_rows
    result = lax.map(jax.checkpoint(block_fn), (query_blocks, offsets))
    return result.reshape(TOK_DEV, D)

def forward_pack(frames, skip, weights, segment, in_use, key_live):
    w_skip, b_skip, gain_one, shift_one, w_qkv, b_query, b_value, w_out, b_out, gain_two, shift_two, w_up, b_up, w_down, b_down = weights
    joined = jnp.concatenate([frames, skip], axis=1)
    first_proj = low_back(matmul(joined, w_skip) + b_skip)
    normed = low(norm_apply(first_proj, gain_one, shift_one))
    qkv_bias = jnp.concatenate([b_query, jnp.zeros_like(b_query), b_value])
    qkv = low_back(low(matmul(normed, w_qkv) + qkv_bias))
    queries = qkv[:, :D].reshape(TOK_DEV, HEADS, HEAD_DIM)
    keys_all = qkv[:, D:2 * D].reshape(TOK_DEV, HEADS, HEAD_DIM)
    values = qkv[:, 2 * D:].reshape(TOK_DEV, HEADS, HEAD_DIM)
    mixed = low_back(low(attend_pack(queries, keys_all, values, segment, in_use, key_live)))
    attn_out = low_back(matmul(mixed, w_out) + b_out)
    second = first_proj + attn_out
    normed_two = low(norm_apply(second, gain_two, shift_two))
    hidden = low_back(matmul(normed_two, w_up) + b_up)
    activated = low(gelu_tanh(hidden))
    return second + matmul(activated, w_down) + b_down

def reference(frames, skip, lengths, key_mask, cotangent, w_skip, b_skip, pre_attn_gain, pre_attn_bias, w_qkv, b_query, b_value, w_out, b_out, pre_ffn_gain, pre_ffn_bias, w_up, b_up, w_down, b_down):
    pack_count = TOKENS // TOK_DEV
    weights = tuple((w.astype(jnp.float32) for w in (w_skip, b_skip, pre_attn_gain, pre_attn_bias, w_qkv, b_query, b_value, w_out, b_out, pre_ffn_gain, pre_ffn_bias, w_up, b_up, w_down, b_down)))
    pack_items = (frames.astype(jnp.float32).reshape(pack_count, TOK_DEV, D), skip.astype(jnp.float32).reshape(pack_count, TOK_DEV, D), lengths, key_mask.reshape(pack_count, TOK_DEV), cotangent.astype(jnp.float32).reshape(pack_count, TOK_DEV, D))
    zero_grads = tuple((jnp.zeros_like(w) for w in weights))

    def one_pack(summed, inputs):
        frame_pack, skip_pack, length_row, mask_row, cot_pack = inputs
        segment, in_use, key_live = segment_layout(length_row, mask_row)

        def run_pack(frame_in, skip_in, weight_in):
            return forward_pack(frame_in, skip_in, weight_in, segment, in_use, key_live)
        out_rows, pullback = jax.vjp(run_pack, frame_pack, skip_pack, weights)
        grad_frame, grad_skip_pack, grad_weights = pullback(cot_pack)
        summed = tuple((a + b for a, b in zip(summed, grad_weights)))
        return (summed, (out_rows, grad_frame, grad_skip_pack))
    grads, (out_rows, grad_frame, grad_skip_pack) = lax.scan(one_pack, zero_grads, pack_items)
    layer_out = out_rows.reshape(TOKENS, D).astype(jnp.bfloat16)
    grad_frames = grad_frame.reshape(TOKENS, D).astype(jnp.bfloat16)
    grad_skip = grad_skip_pack.reshape(TOKENS, D).astype(jnp.bfloat16)
    return (layer_out, grad_frames, grad_skip, grads[0], grads[1], grads[2], grads[3], grads[4], grads[5], grads[6], grads[7], grads[8], grads[9], grads[10], grads[11], grads[12], grads[13], grads[14])
```

```python
import functools
import math

import jax
import jax.numpy as jnp
from jax import lax
from jax.experimental import pallas as pl
from jax.experimental.pallas import tpu as pltpu
from jax.sharding import PartitionSpec as P

HEADS = 16
EPSILON = 1e-05
FAR = 1e32
AXES = ("wide", "narrow")
BF = jnp.bfloat16
F32 = jnp.float32
VMEM_LIMIT = 56 * 1024 * 1024

ANY = pl.BlockSpec(memory_space=pl.ANY)
SMEM = pl.BlockSpec(memory_space=pltpu.SMEM)


def params():
    return pltpu.CompilerParams(vmem_limit_bytes=VMEM_LIMIT)


def cost(flops, nbytes, trans=0):
    return pl.CostEstimate(flops=int(flops), bytes_accessed=int(nbytes), transcendentals=int(trans))


class Net:
    def __init__(self, size, rows_min):
        self.size = size
        self.bits = size.bit_length() - 1
        self.high = self.bits - 3
        self.groups = 1 << self.high
        self.fast = size == 1 << self.bits and self.bits >= 3 and rows_min % 16 == 0
        self.shards = size if self.fast else 1

    def pp(self, x, mask):
        pairs = [(d, d ^ mask(d & 1)) for d in range(self.size)]
        return lax.ppermute(x, AXES, pairs)


def first_bit(core):
    return 2 + 2 * core


def second_bit(core):
    return 4 - 2 * core


def gather(net, shard):
    if not net.fast:
        return [lax.all_gather(shard, AXES, axis=0, tiled=True)[None]]
    block = shard[None]
    for bit in range(3, net.bits):
        block = jnp.concatenate([block, net.pp(block, lambda c: 1 << bit)], axis=0)
    one = net.pp(block, first_bit)
    own = [block, one, net.pp(block, second_bit), net.pp(one, second_bit)]
    return own + [net.pp(piece, lambda c: 1) for piece in own]


def piece_masks(core):
    a, b = first_bit(core), second_bit(core)
    return [0, a, b, 6, 1, 1 ^ b, 1 ^ a, 7]


def gather_vector(net, row):
    if not net.fast:
        return lax.all_gather(row, AXES, axis=0, tiled=True)
    me = lax.axis_index(AXES)
    for bit in range(net.bits):
        other = net.pp(row, lambda c: 1 << bit)
        row = jnp.where(
            (me >> bit) & 1 == 1,
            jnp.concatenate([other, row], axis=0),
            jnp.concatenate([row, other], axis=0),
        )
    return row


def scatter_vector(net, rows):
    if not net.fast:
        return lax.psum_scatter(rows, AXES, scatter_dimension=0, tiled=True)[0]
    me = lax.axis_index(AXES)
    for bit in reversed(range(net.bits)):
        half = 1 << bit
        up = (me >> bit) & 1 == 1
        keep = jnp.where(up, rows[half:], rows[:half])
        send = jnp.where(up, rows[:half], rows[half:])
        rows = keep + net.pp(send, lambda c: 1 << bit)
    return rows[0]


def scatter(net, parts):
    if not net.fast:
        return lax.psum_scatter(parts[0][0].astype(F32), AXES, scatter_dimension=0, tiled=True)
    keep, send = parts
    got = [net.pp(send, lambda c: 1)]
    masks = [second_bit, first_bit] + [
        (lambda c, bit=bit: 1 << bit) for bit in reversed(range(3, net.bits))
    ]
    half = keep.shape[0] // 2

    def summed(lo, hi):
        total = keep[lo:hi].astype(F32)
        for arr in got:
            total = total + arr[lo:hi].astype(F32)
        return total

    for mask in masks:
        got.append(net.pp(summed(half, 2 * half).astype(BF), mask))
        half //= 2
    return summed(0, 1)[0]


def load_start(net, me, pieces, dst, sems):
    copies = []
    if len(pieces) == 1:
        copies.append(pltpu.make_async_copy(pieces[0].at[0], dst, sems.at[0]))
    else:
        masks = piece_masks(me & 1)
        rows = dst.shape[0] // net.size
        for i, piece in enumerate(pieces):
            for j in range(net.groups):
                source = me ^ (masks[i] ^ (j << 3))
                at = pl.multiple_of(source * rows, rows)
                copies.append(
                    pltpu.make_async_copy(
                        piece.at[j], dst.at[pl.ds(at, rows), :], sems.at[len(copies)]
                    )
                )
    for copy in copies:
        copy.start()
    return copies


def relative(net, rel, core):
    bit_one, bit_two, group = (rel >> 1) & 1, (rel >> 2) & 1, rel >> 3
    top = jnp.where(core == 0, bit_two, bit_one)
    low = jnp.where(core == 0, bit_one, bit_two)
    return (top << (net.high + 1)) | (low << net.high) | group


def grad_out_shapes(net, rows, cols):
    if not net.fast:
        return [jax.ShapeDtypeStruct((1, rows, cols), BF)]
    shape = jax.ShapeDtypeStruct((net.size // 2, rows // net.size, cols), BF)
    return [shape, shape]


def store_start(net, me, src, base, rows, total_rows, outs, sems, first_sem):
    copies = []
    if not net.fast:
        copies.append(
            pltpu.make_async_copy(
                src.at[pl.ds(base, rows), :],
                outs[0].at[0, pl.ds(base, rows), :],
                sems.at[first_sem],
            )
        )
    else:
        shard = total_rows // net.size
        core = me & 1
        for i in range(0, rows // shard, 2):
            even = base // shard + i
            for k, out in enumerate(outs):
                owner_core = core if k == 0 else 1 - core
                target = even | owner_core
                rel = (me if k == 0 else me ^ 1) ^ target
                at = pl.multiple_of(target * shard, shard)
                copies.append(
                    pltpu.make_async_copy(
                        src.at[pl.ds(at, shard), :],
                        out.at[relative(net, rel, owner_core)],
                        sems.at[first_sem + i + k],
                    )
                )
    for copy in copies:
        copy.start()
    return copies


def dot(a, b):
    return jnp.dot(a, b, preferred_element_type=F32)


def dot_t(a, b):
    return lax.dot_general(a, b, (((1,), (1,)), ((), ())), preferred_element_type=F32)


def norm_parts(x):
    center = x - jnp.mean(x, axis=1, keepdims=True)
    spread = jnp.mean(center * center, axis=1, keepdims=True)
    rstd = lax.rsqrt(spread + EPSILON)
    return center * rstd, rstd


def sums(x):
    return jnp.sum(x, axis=0, keepdims=True)


def add_to(ref, value, step):
    @pl.when(step == 0)
    def _():
        ref[...] = value

    @pl.when(step > 0)
    def _():
        ref[...] += value


def row_block(tok):
    return min(512, tok)


def weight_scratch(net, *shapes):
    out = []
    for shape in shapes:
        out += [pltpu.VMEM(shape, BF), pltpu.SemaphoreType.DMA((net.shards,))]
    return out


def n_pieces(net):
    return 8 if net.fast else 1


def skip_kernel(net, me_ref, frames, skip, bias, gain, shift, *rest):
    np_ = n_pieces(net)
    pieces, (first_ref, normed_ref, w, sems) = rest[:np_], rest[np_:]

    @pl.when(pl.program_id(0) == 0)
    def _():
        for copy in load_start(net, me_ref[0], pieces, w, sems):
            copy.wait()

    width = frames.shape[1]
    first = dot(frames[...], w[:width, :]) + dot(skip[...], w[width:, :]) + bias[...]
    first_ref[...] = first
    xhat, _ = norm_parts(first)
    normed_ref[...] = (xhat * gain[...] + shift[...]).astype(BF)


def skip_forward(net, me, frames, skip, pieces, bias, gain, shift):
    tok, width = frames.shape
    blk = row_block(tok)
    rows = pl.BlockSpec((blk, width), lambda i: (i, 0))
    vec = pl.BlockSpec((1, width), lambda i: (0, 0))
    return pl.pallas_call(
        functools.partial(skip_kernel, net),
        grid=(tok // blk,),
        in_specs=[SMEM, rows, rows, vec, vec, vec] + [ANY] * len(pieces),
        out_specs=[rows, rows],
        out_shape=[jax.ShapeDtypeStruct((tok, width), F32), jax.ShapeDtypeStruct((tok, width), BF)],
        scratch_shapes=weight_scratch(net, (2 * width, width)),
        compiler_params=params(),
        cost_estimate=cost(4 * tok * width * width, tok * width * 10 + 4 * width * width),
        name="skip_forward",
    )(me, frames, skip, bias, gain, shift, *pieces)


def qkv_kernel(net, me_ref, normed, bias, *rest):
    np_ = n_pieces(net)
    pieces, (out_ref, w, sems) = rest[:np_], rest[np_:]

    @pl.when(pl.program_id(0) == 0)
    def _():
        for copy in load_start(net, me_ref[0], pieces, w, sems):
            copy.wait()

    chunk = 1024
    for at in range(0, w.shape[1], chunk):
        part = slice(at, at + chunk)
        out_ref[:, part] = (dot(normed[...], w[:, part]) + bias[:, part]).astype(BF)


def qkv_forward(net, me, normed, pieces, bias):
    tok, width = normed.shape
    cols = bias.shape[1]
    blk = row_block(tok)
    return pl.pallas_call(
        functools.partial(qkv_kernel, net),
        grid=(tok // blk,),
        in_specs=[
            SMEM,
            pl.BlockSpec((blk, width), lambda i: (i, 0)),
            pl.BlockSpec((1, cols), lambda i: (0, 0)),
        ]
        + [ANY] * len(pieces),
        out_specs=pl.BlockSpec((blk, cols), lambda i: (i, 0)),
        out_shape=jax.ShapeDtypeStruct((tok, cols), BF),
        scratch_shapes=weight_scratch(net, (width, cols)),
        compiler_params=params(),
        cost_estimate=cost(2 * tok * width * cols, tok * width * 8 + 6 * width * width),
        name="qkv_forward",
    )(me, normed, bias, *pieces)


def gelu_both(v):
    square = v * v
    th = jnp.tanh(0.7978845608 * v * (1.0 + 0.044715 * square))
    half = 0.5 * (1.0 + th)
    slope = half + 0.5 * v * (1.0 - th * th) * (0.7978845608 + 3 * 0.7978845608 * 0.044715 * square)
    return v * half, slope


def up_kernel(net, me_ref, first, mixed, b_out, gain, shift, b_up, *rest):
    np_ = n_pieces(net)
    out_pieces, up_pieces, rest = rest[:np_], rest[np_ : 2 * np_], rest[2 * np_ :]
    second_ref, normed_ref, act_ref, pull_ref, w_out, sems_out, w_up, sems_up = rest

    @pl.when(pl.program_id(0) == 0)
    def _():
        copies = load_start(net, me_ref[0], out_pieces, w_out, sems_out)
        copies += load_start(net, me_ref[0], up_pieces, w_up, sems_up)
        for copy in copies:
            copy.wait()

    second = first[...] + dot(mixed[...], w_out[...]) + b_out[...]
    second_ref[...] = second
    xhat, _ = norm_parts(second)
    normed = (xhat * gain[...] + shift[...]).astype(BF)
    normed_ref[...] = normed
    chunk = 1024
    for at in range(0, w_up.shape[1], chunk):
        part = slice(at, at + chunk)
        hidden = dot(normed, w_up[:, part]) + b_up[:, part]
        act, pull = gelu_both(hidden)
        act_ref[:, part] = act.astype(BF)
        pull_ref[:, part] = pull.astype(BF)


def up_forward(net, me, first, mixed, out_pieces, up_pieces, b_out, gain, shift, b_up):
    tok, width = first.shape
    ff = b_up.shape[1]
    blk = min(256, tok)
    rows = pl.BlockSpec((blk, width), lambda i: (i, 0))
    wide = pl.BlockSpec((blk, ff), lambda i: (i, 0))
    vec = pl.BlockSpec((1, width), lambda i: (0, 0))
    vec_ff = pl.BlockSpec((1, ff), lambda i: (0, 0))
    return pl.pallas_call(
        functools.partial(up_kernel, net),
        grid=(tok // blk,),
        in_specs=[SMEM, rows, rows, vec, vec, vec, vec_ff] + [ANY] * (2 * len(out_pieces)),
        out_specs=[rows, rows, wide, wide],
        out_shape=[
            jax.ShapeDtypeStruct((tok, width), F32),
            jax.ShapeDtypeStruct((tok, width), BF),
            jax.ShapeDtypeStruct((tok, ff), BF),
            jax.ShapeDtypeStruct((tok, ff), BF),
        ],
        scratch_shapes=weight_scratch(net, (width, width), (width, ff)),
        compiler_params=params(),
        cost_estimate=cost(
            2 * tok * width * (width + ff), tok * (width * 12 + ff * 4) + 2 * width * (width + ff)
        ),
        name="up_forward",
    )(me, first, mixed, b_out, gain, shift, b_up, *out_pieces, *up_pieces)


def down_kernel(net, me_ref, second, act, pull, cot, b_down, *rest):
    np_ = n_pieces(net)
    pieces, (out_ref, gh_ref, bsum_ref, csum_ref, w, sems) = rest[:np_], rest[np_:]
    step = pl.program_id(0)

    @pl.when(step == 0)
    def _():
        for copy in load_start(net, me_ref[0], pieces, w, sems):
            copy.wait()

    out_ref[...] = (second[...] + dot(act[...], w[...]) + b_down[...]).astype(BF)
    chunk = 1024
    for at in range(0, w.shape[0], chunk):
        part = slice(at, at + chunk)
        gh = (dot_t(cot[...], w[part, :]) * pull[:, part].astype(F32)).astype(BF)
        gh_ref[:, part] = gh
        add_to(bsum_ref.at[:, part], sums(gh.astype(F32)), step)
    add_to(csum_ref, sums(cot[...].astype(F32)), step)


def down_both(net, me, second, act, pull, cot, pieces, b_down):
    tok, width = second.shape
    ff = act.shape[1]
    blk = min(256, tok)
    rows = pl.BlockSpec((blk, width), lambda i: (i, 0))
    wide = pl.BlockSpec((blk, ff), lambda i: (i, 0))
    vec = pl.BlockSpec((1, width), lambda i: (0, 0))
    vec_ff = pl.BlockSpec((1, ff), lambda i: (0, 0))
    return pl.pallas_call(
        functools.partial(down_kernel, net),
        grid=(tok // blk,),
        in_specs=[SMEM, rows, wide, wide, rows, vec] + [ANY] * len(pieces),
        out_specs=[rows, wide, vec_ff, vec],
        out_shape=[
            jax.ShapeDtypeStruct((tok, width), BF),
            jax.ShapeDtypeStruct((tok, ff), BF),
            jax.ShapeDtypeStruct((1, ff), F32),
            jax.ShapeDtypeStruct((1, width), F32),
        ],
        scratch_shapes=weight_scratch(net, (ff, width)),
        compiler_params=params(),
        cost_estimate=cost(4 * tok * width * ff, tok * (width * 8 + ff * 6) + 2 * width * ff),
        name="down_both",
    )(me, second, act, pull, cot, b_down, *pieces)


def grad_kernel(net, lefts, blk, me_ref, *rest):
    left_refs, right, rest = rest[:lefts], rest[lefts], rest[lefts + 1 :]
    outs, (acc, sems) = rest[:-2], rest[-2:]
    step = pl.program_id(0)
    total = acc.shape[0]
    per_left = total // lefts // blk
    cols = acc.shape[1]
    chunk = 1024
    for k in range(lefts):

        @pl.when((step >= k * per_left) & (step < (k + 1) * per_left))
        def _():
            left = left_refs[k][...].T
            for at in range(0, cols, chunk):
                part = slice(at, at + chunk)
                acc[pl.ds(pl.multiple_of(step * blk, blk), blk), part] = dot(
                    left, right[:, part]
                ).astype(BF)

    steps = total // blk
    per_step = sems.shape[0] // steps
    for s in range(steps):

        @pl.when(step == s)
        def _():
            store_start(net, me_ref[0], acc, s * blk, blk, total, outs, sems, s * per_step)

    @pl.when(step == steps - 1)
    def _():
        for s in range(steps):
            for copy in store_list(
                net, me_ref[0], acc, s * blk, blk, total, outs, sems, s * per_step
            ):
                copy.wait()


def store_list(net, me, src, base, rows, total_rows, outs, sems, first_sem):
    copies = []
    if not net.fast:
        return [
            pltpu.make_async_copy(
                src.at[pl.ds(base, rows), :],
                outs[0].at[0, pl.ds(base, rows), :],
                sems.at[first_sem],
            )
        ]
    shard = total_rows // net.size
    core = me & 1
    for i in range(0, rows // shard, 2):
        even = base // shard + i
        for k, out in enumerate(outs):
            owner_core = core if k == 0 else 1 - core
            target = even | owner_core
            rel = (me if k == 0 else me ^ 1) ^ target
            at = pl.multiple_of(target * shard, shard)
            copies.append(
                pltpu.make_async_copy(
                    src.at[pl.ds(at, shard), :],
                    out.at[relative(net, rel, owner_core)],
                    sems.at[first_sem + i + k],
                )
            )
    return copies


def weight_grad(net, me, lefts, right, name):
    tok, cols = right.shape
    each = lefts[0].shape[1]
    total = each * len(lefts)
    blk = min(512, each)
    per_left = each // blk
    steps = total // blk
    per_step = blk // (total // net.size) if net.fast else 1

    def index(k):
        return lambda i: (0, jnp.clip(i - k * per_left, 0, per_left - 1))

    shapes = grad_out_shapes(net, total, cols)
    return pl.pallas_call(
        functools.partial(grad_kernel, net, len(lefts), blk),
        grid=(steps,),
        in_specs=[SMEM]
        + [pl.BlockSpec((tok, blk), index(k)) for k in range(len(lefts))]
        + [pl.BlockSpec((tok, cols), lambda i: (0, 0), pipeline_mode=pl.Buffered(1))],
        out_specs=[ANY] * len(shapes),
        out_shape=shapes,
        scratch_shapes=[
            pltpu.VMEM((total, cols), BF),
            pltpu.SemaphoreType.DMA((steps * per_step,)),
        ],
        compiler_params=params(),
        cost_estimate=cost(
            2 * tok * total * cols, 2 * tok * (total + cols) + 2 * total * cols
        ),
        name=name,
    )(me, *lefts, right)


def norm_back(dn, x, gain):
    xhat, rstd = norm_parts(x)
    scaled = dn * gain
    mean_one = jnp.mean(scaled, axis=1, keepdims=True)
    mean_two = jnp.mean(scaled * xhat, axis=1, keepdims=True)
    return (scaled - mean_one - xhat * mean_two) * rstd, dn * xhat


def second_kernel(net, me_ref, gh, second, cot, gain, *rest):
    np_ = n_pieces(net)
    up_pieces, out_pieces, rest = rest[:np_], rest[np_ : 2 * np_], rest[2 * np_ :]
    gsec_ref, gattn_ref, gmix_ref, ggain_ref, gshift_ref, gbout_ref = rest[:6]
    w_up, sems_up, w_out, sems_out = rest[6:]
    step = pl.program_id(0)

    @pl.when(step == 0)
    def _():
        copies = load_start(net, me_ref[0], up_pieces, w_up, sems_up)
        copies += load_start(net, me_ref[0], out_pieces, w_out, sems_out)
        for copy in copies:
            copy.wait()

    dn = dot_t(gh[...], w_up[...])
    pulled, dx = norm_back(dn, second[...], gain[...])
    gsec = cot[...].astype(F32) + pulled
    gsec_ref[...] = gsec
    gattn = gsec.astype(BF)
    gattn_ref[...] = gattn
    gmix_ref[...] = dot_t(gattn, w_out[...]).astype(BF)
    add_to(ggain_ref, sums(dx), step)
    add_to(gshift_ref, sums(dn), step)
    add_to(gbout_ref, sums(gattn.astype(F32)), step)


def second_back(net, me, gh, second, cot, up_pieces, out_pieces, gain):
    tok, width = second.shape
    ff = gh.shape[1]
    blk = min(256, tok)
    rows = pl.BlockSpec((blk, width), lambda i: (i, 0))
    wide = pl.BlockSpec((blk, ff), lambda i: (i, 0))
    vec = pl.BlockSpec((1, width), lambda i: (0, 0))
    vec_shape = jax.ShapeDtypeStruct((1, width), F32)
    return pl.pallas_call(
        functools.partial(second_kernel, net),
        grid=(tok // blk,),
        in_specs=[SMEM, wide, rows, rows, vec] + [ANY] * (2 * len(up_pieces)),
        out_specs=[rows, rows, rows, vec, vec, vec],
        out_shape=[
            jax.ShapeDtypeStruct((tok, width), F32),
            jax.ShapeDtypeStruct((tok, width), BF),
            jax.ShapeDtypeStruct((tok, width), BF),
            vec_shape,
            vec_shape,
            vec_shape,
        ],
        scratch_shapes=weight_scratch(net, (width, ff), (width, width)),
        compiler_params=params(),
        cost_estimate=cost(
            2 * tok * width * (width + ff), tok * (width * 14 + ff * 2) + 2 * width * (width + ff)
        ),
        name="second_back",
    )(me, gh, second, cot, gain, *up_pieces, *out_pieces)


def first_kernel(net, me_ref, gqkv, first, gsec, gain, *rest):
    np_ = n_pieces(net)
    pieces, rest = rest[:np_], rest[np_:]
    gfirst_ref, ggain_ref, gshift_ref, gbskip_ref, gbqkv_ref, w, sems = rest
    step = pl.program_id(0)

    @pl.when(step == 0)
    def _():
        for copy in load_start(net, me_ref[0], pieces, w, sems):
            copy.wait()

    dn = dot_t(gqkv[...], w[...])
    pulled, dx = norm_back(dn, first[...], gain[...])
    gfirst = (gsec[...] + pulled).astype(BF)
    gfirst_ref[...] = gfirst
    add_to(ggain_ref, sums(dx), step)
    add_to(gshift_ref, sums(dn), step)
    add_to(gbskip_ref, sums(gfirst.astype(F32)), step)
    add_to(gbqkv_ref, sums(gqkv[...].astype(F32)), step)


def first_back(net, me, gqkv, first, gsec, pieces, gain):
    tok, width = first.shape
    cols = gqkv.shape[1]
    blk = min(256, tok)
    rows = pl.BlockSpec((blk, width), lambda i: (i, 0))
    wide = pl.BlockSpec((blk, cols), lambda i: (i, 0))
    vec = pl.BlockSpec((1, width), lambda i: (0, 0))
    vec_wide = pl.BlockSpec((1, cols), lambda i: (0, 0))
    vec_shape = jax.ShapeDtypeStruct((1, width), F32)
    return pl.pallas_call(
        functools.partial(first_kernel, net),
        grid=(tok // blk,),
        in_specs=[SMEM, wide, rows, rows, vec] + [ANY] * len(pieces),
        out_specs=[rows, vec, vec, vec, vec_wide],
        out_shape=[
            jax.ShapeDtypeStruct((tok, width), BF),
            vec_shape,
            vec_shape,
            vec_shape,
            jax.ShapeDtypeStruct((1, cols), F32),
        ],
        scratch_shapes=weight_scratch(net, (width, cols)),
        compiler_params=params(),
        cost_estimate=cost(2 * tok * width * cols, tok * (width * 10 + cols * 2) + 2 * width * cols),
        name="first_back",
    )(me, gqkv, first, gsec, gain, *pieces)


def joined_kernel(net, me_ref, gfirst, *rest):
    np_ = n_pieces(net)
    pieces, (gframes_ref, gskip_ref, w, sems) = rest[:np_], rest[np_:]

    @pl.when(pl.program_id(0) == 0)
    def _():
        for copy in load_start(net, me_ref[0], pieces, w, sems):
            copy.wait()

    width = gframes_ref.shape[1]
    gframes_ref[...] = dot_t(gfirst[...], w[:width, :]).astype(BF)
    gskip_ref[...] = dot_t(gfirst[...], w[width:, :]).astype(BF)


def joined_back(net, me, gfirst, pieces):
    tok, width = gfirst.shape
    blk = row_block(tok)
    rows = pl.BlockSpec((blk, width), lambda i: (i, 0))
    out = jax.ShapeDtypeStruct((tok, width), BF)
    return pl.pallas_call(
        functools.partial(joined_kernel, net),
        grid=(tok // blk,),
        in_specs=[SMEM, rows] + [ANY] * len(pieces),
        out_specs=[rows, rows],
        out_shape=[out, out],
        scratch_shapes=weight_scratch(net, (2 * width, width)),
        compiler_params=params(),
        cost_estimate=cost(4 * tok * width * width, tok * width * 6 + 4 * width * width),
        name="joined_back",
    )(me, gfirst, *pieces)


def far_apart(row_tag, col_tag, row_at):
    shape = (row_tag.shape[0], col_tag.shape[1])
    i = row_at + lax.broadcasted_iota(jnp.int32, shape, 0)
    j = lax.broadcasted_iota(jnp.int32, shape, 1)
    ok = (row_tag == col_tag) | (i == j)
    return jnp.where(ok, jnp.abs(i - j).astype(F32), FAR)


def head_slope(head):
    return jnp.exp2((jnp.full((1, 1), head, jnp.int32).astype(F32) + 1.0) * (-8.0 / HEADS))


def attend_kernel(size, blk, q, k, v, tag_q, tag_k, out_ref, lse_ref, far):
    pair = pl.program_id(0)
    tok = q.shape[0]
    steps = tok // blk

    @pl.when(pair == 0)
    def _():
        lse_ref[...] = jnp.zeros_like(lse_ref)
        for i in range(steps):
            at = slice(i * blk, (i + 1) * blk)
            far[at, :] = far_apart(tag_q[at, :], tag_k[...], i * blk)

    lane = lax.broadcasted_iota(jnp.int32, (1, 2 * size), 1)
    lse_lane = lax.broadcasted_iota(jnp.int32, (1, lse_ref.shape[1]), 1)
    scale = size**-0.5
    for i in range(steps):
        at = slice(i * blk, (i + 1) * blk)
        q_blk = q[at, :] * scale
        outs, lse = [], lse_ref[at, :]
        for h in range(2):
            mine = (lane >= h * size) & (lane < (h + 1) * size)
            scores = dot_t(jnp.where(mine, q_blk, 0), k[...]) - head_slope(2 * pair + h) * far[at, :]
            top = jnp.max(scores, axis=1, keepdims=True)
            expo = jnp.exp(scores - top)
            denom = jnp.sum(expo, axis=1, keepdims=True)
            outs.append(dot(expo.astype(BF), v[...]) / denom)
            lse = jnp.where(lse_lane == 2 * pair + h, top + jnp.log(denom), lse)
        out_ref[at, :] = jnp.where(lane < size, outs[0], outs[1]).astype(BF)
        lse_ref[at, :] = lse


def attend(qkv, tag_q, tag_k, heads):
    tok = qkv.shape[0]
    width = qkv.shape[1] // 3
    size = width // heads
    pairs = heads // 2
    blk = min(256, tok)

    def cols(k):
        return pl.BlockSpec((tok, 2 * size), lambda p: (0, k * pairs + p))

    return pl.pallas_call(
        functools.partial(attend_kernel, size, blk),
        grid=(pairs,),
        in_specs=[
            cols(0),
            cols(1),
            cols(2),
            pl.BlockSpec((tok, 1), lambda p: (0, 0)),
            pl.BlockSpec((1, tok), lambda p: (0, 0)),
        ],
        out_specs=[
            pl.BlockSpec((tok, 2 * size), lambda p: (0, p)),
            pl.BlockSpec((tok, 128), lambda p: (0, 0)),
        ],
        out_shape=[
            jax.ShapeDtypeStruct((tok, width), BF),
            jax.ShapeDtypeStruct((tok, 128), F32),
        ],
        scratch_shapes=[pltpu.VMEM((tok, tok), F32)],
        compiler_params=params(),
        cost_estimate=cost(16 * heads * tok * tok * size, tok * width * 8, heads * tok * tok),
        name="attend",
    )(qkv, qkv, qkv, tag_q.reshape(tok, 1), tag_k.reshape(1, tok))


def attend_back_kernel(size, blk, q, k, v, g, o, lse, tag_k, tag_q, gq_ref, gk_ref, gv_ref, far, lse_t):
    pair = pl.program_id(0)
    tok = q.shape[0]
    steps = tok // blk

    @pl.when(pair == 0)
    def _():
        lse_t[...] = lse[...].T
        for i in range(steps):
            at = slice(i * blk, (i + 1) * blk)
            far[at, :] = far_apart(tag_k[at, :], tag_q[...], i * blk)

    lane = lax.broadcasted_iota(jnp.int32, (1, 2 * size), 1)
    scale = size**-0.5
    q_all = q[...] * scale
    g_all = g[...]
    products = (g_all.astype(F32) * o[...].astype(F32)).T
    k_t = (k[...] * scale).astype(F32).T.astype(BF)
    grads_q, kept = [], []
    for h in range(2):
        mine = (lane >= h * size) & (lane < (h + 1) * size)
        q_h = jnp.where(mine, q_all, 0)
        g_h = jnp.where(mine, g_all, 0)
        delta = jnp.sum(products[h * size : (h + 1) * size, :], axis=0, keepdims=True)
        norm = lse_t[pl.ds(2 * pair + h, 1), :]
        slope = head_slope(2 * pair + h)
        grad_q = jnp.zeros((size, tok), F32)
        for i in range(steps):
            at = slice(i * blk, (i + 1) * blk)
            scores = dot_t(k[at, :], q_h) - slope * far[at, :]
            probs = jnp.exp(scores - norm)
            pulled = dot_t(v[at, :], g_h)
            ds = (probs * (pulled - delta)).astype(BF)
            gv = dot(probs.astype(BF), g_all)
            gk = dot(ds, q_all)
            grad_q = grad_q + dot(k_t[h * size : (h + 1) * size, at], ds)
            if h == 0:
                gv_ref[at, :] = gv.astype(BF)
                gk_ref[at, :] = gk.astype(BF)
            else:
                gv_ref[at, :] = jnp.where(mine, gv.astype(BF), gv_ref[at, :])
                gk_ref[at, :] = jnp.where(mine, gk.astype(BF), gk_ref[at, :])
        grads_q.append(grad_q)
    gq_ref[...] = jnp.concatenate(grads_q, axis=0).T.astype(BF)


def attend_back(qkv, grad_mixed, mixed, lse, tag_q, tag_k, heads):
    tok = qkv.shape[0]
    width = qkv.shape[1] // 3
    size = width // heads
    pairs = heads // 2
    blk = min(256, tok)

    def cols(k):
        return pl.BlockSpec((tok, 2 * size), lambda p: (0, k * pairs + p))

    out = jax.ShapeDtypeStruct((tok, width), BF)
    return pl.pallas_call(
        functools.partial(attend_back_kernel, size, blk),
        grid=(pairs,),
        in_specs=[
            cols(0),
            cols(1),
            cols(2),
            cols(0),
            cols(0),
            pl.BlockSpec((tok, 128), lambda p: (0, 0)),
            pl.BlockSpec((tok, 1), lambda p: (0, 0)),
            pl.BlockSpec((1, tok), lambda p: (0, 0)),
        ],
        out_specs=[cols(0)] * 3,
        out_shape=[out] * 3,
        scratch_shapes=[pltpu.VMEM((tok, tok), F32), pltpu.VMEM((128, tok), F32)],
        compiler_params=params(),
        cost_estimate=cost(40 * heads * tok * tok * size, tok * width * 16, heads * tok * tok),
        name="attend_back",
    )(qkv, qkv, qkv, grad_mixed, mixed, lse, tag_k.reshape(tok, 1), tag_q.reshape(1, tok))


def tags(length_row, mask_row, tok):
    order = jnp.arange(length_row.shape[0])
    ends = jnp.sum(jnp.where(order[:, None] <= order[None, :], length_row[:, None], 0), axis=0)
    slots = jnp.arange(tok, dtype=jnp.int32)
    segment = jnp.sum((slots[:, None] >= ends[None, :]).astype(jnp.int32), axis=1)
    used = slots < jnp.sum(length_row)
    return jnp.where(used, segment, -1), jnp.where(used & (mask_row == 1), segment, -2)


def body(size, frames, skip, lengths, key_mask, cotangent, *weights):
    (
        w_skip, b_skip, pre_attn_gain, pre_attn_bias, w_qkv, b_query, b_value, w_out, b_out,
        pre_ffn_gain, pre_ffn_bias, w_up, b_up, w_down, b_down,
    ) = weights
    tok, width = frames.shape
    net = Net(size, min(w.shape[0] for w in (w_skip, w_qkv, w_out, w_up, w_down)))
    me = lax.axis_index(AXES).astype(jnp.int32).reshape(1)

    small = (
        b_skip, pre_attn_gain, pre_attn_bias, b_query, b_value, b_out, pre_ffn_gain, pre_ffn_bias, b_up, b_down,
    )
    vectors = gather_vector(net, jnp.concatenate(small).reshape(1, -1)).astype(F32)
    whole, at = [], 0
    for vec in small:
        whole.append(vectors[:, at : at + vec.shape[0]].reshape(1, -1))
        at += vec.shape[0]
    bskip, gain1, shift1, bquery, bvalue, bout, gain2, shift2, bup, bdown = whole

    skip_w = gather(net, w_skip)
    qkv_w = gather(net, w_qkv)
    out_w = gather(net, w_out)
    up_w = gather(net, w_up)
    down_w = gather(net, w_down)

    tag_q, tag_k = tags(lengths[0], key_mask, tok)

    first, normed = skip_forward(net, me, frames, skip, skip_w, bskip, gain1, shift1)
    qkv_bias = jnp.concatenate([bquery, jnp.zeros_like(bquery), bvalue], axis=1)
    qkv = qkv_forward(net, me, normed, qkv_w, qkv_bias)
    mixed, lse = attend(qkv, tag_q, tag_k, HEADS)
    second, normed2, act, pull = up_forward(
        net, me, first, mixed, out_w, up_w, bout, gain2, shift2, bup
    )
    down_parts = weight_grad(net, me, [act], cotangent, "grad_down")
    layer_out, gh, gbup, gbdown = down_both(net, me, second, act, pull, cotangent, down_w, bdown)
    up_parts = weight_grad(net, me, [normed2], gh, "grad_up")
    gsec, gattn, gmixed, ggain2, gshift2, gbout = second_back(
        net, me, gh, second, cotangent, up_w, out_w, gain2
    )
    out_parts = weight_grad(net, me, [mixed], gattn, "grad_out")
    gq, gk, gv = attend_back(qkv, gmixed, mixed, lse, tag_q, tag_k, HEADS)
    gqkv = jnp.concatenate([gq, gk, gv], axis=1)
    qkv_parts = weight_grad(net, me, [normed], gqkv, "grad_qkv")
    gfirst, ggain1, gshift1, gbskip, gbqkv = first_back(net, me, gqkv, first, gsec, qkv_w, gain1)
    skip_parts = weight_grad(net, me, [frames, skip], gfirst, "grad_skip")
    gframes, gskip = joined_back(net, me, gfirst, skip_w)

    grads_small = (
        gbskip, ggain1, gshift1, gbqkv[:, :width], gbqkv[:, 2 * width :], gbout, ggain2, gshift2, gbup, gbdown,
    )
    rows = jnp.concatenate([g.reshape(size, -1) for g in grads_small], axis=1)
    row = scatter_vector(net, rows)
    vec_out, at = [], 0
    for vec in small:
        vec_out.append(row[at : at + vec.shape[0]])
        at += vec.shape[0]
    obskip, ogain1, oshift1, obq, obv, obout, ogain2, oshift2, obup, obdown = vec_out
    return (
        layer_out,
        gframes,
        gskip,
        scatter(net, skip_parts),
        obskip,
        ogain1,
        oshift1,
        scatter(net, qkv_parts),
        obq,
        obv,
        scatter(net, out_parts),
        obout,
        ogain2,
        oshift2,
        scatter(net, up_parts),
        obup,
        scatter(net, down_parts),
        obdown,
    )


def solution(mesh):
    mat, vec = P(AXES, None), P(AXES)
    size = math.prod(mesh.shape.values())
    return jax.shard_map(
        functools.partial(body, size),
        mesh=mesh,
        in_specs=(
            mat, mat, mat, vec, mat,
            mat, vec, vec, vec, mat, vec, vec, mat, vec, vec, vec, mat, vec, mat, vec,
        ),
        out_specs=(
            mat, mat, mat,
            mat, vec, vec, vec, mat, vec, vec, mat, vec, vec, vec, mat, vec, mat, vec,
        ),
        check_vma=False,
    )
```

```python
import functools
import math

import jax
import jax.numpy as jnp
from jax import lax
from jax.experimental import pallas as pl
from jax.experimental.pallas import tpu as pltpu
from jax.sharding import PartitionSpec as P

HEADS = 16
EPSILON = 1e-05
FAR = 1e32
AXES = ("wide", "narrow")
BF = jnp.bfloat16
F32 = jnp.float32
VMEM_LIMIT = 36 * 1024 * 1024

ANY = pl.BlockSpec(memory_space=pl.ANY)
SMEM = pl.BlockSpec(memory_space=pltpu.SMEM)


def params():
    return pltpu.CompilerParams(vmem_limit_bytes=VMEM_LIMIT)


def cost(flops, nbytes, trans=0):
    return pl.CostEstimate(flops=int(flops), bytes_accessed=int(nbytes), transcendentals=int(trans))


class Net:
    def __init__(self, size, rows_min, vec_rows):
        self.size = size
        self.bits = size.bit_length() - 1
        self.high = self.bits - 3
        self.groups = 1 << self.high
        self.fast = size == 1 << self.bits and self.bits >= 3 and rows_min % 16 == 0 and vec_rows == (32, 128)
        self.shards = size if self.fast else 1

    def pp(self, x, mask):
        if not self.fast:
            return x
        pairs = [(d, d ^ mask(d & 1)) for d in range(self.size)]
        return lax.ppermute(x, AXES, pairs)


def first_bit(core):
    return 2 + 2 * core


def second_bit(core):
    return 4 - 2 * core


def other_core(core):
    return 1


def piece_masks(core):
    a, b = first_bit(core), second_bit(core)
    return [0, a, b, 6, 1, 1 ^ b, 1 ^ a, 7]


def bar(*values):
    return lax.optimization_barrier(values)


class Flow:
    def __init__(self, net):
        self.net, self.data = net, {}

    def end(self, values, *prefixes):
        names = [n for n in self.data if n.startswith(prefixes)] if prefixes else []
        values, arrays = bar(values, [self.data[n] for n in names])
        self.data.update(zip(names, arrays))
        return values

    def send(self, name, x, mask):
        self.data[name] = self.net.pp(x, mask)

    def own(self, p, shard):
        if self.net.fast:
            self.data[p + "z0"] = shard
        else:
            self.data[p + "m0"] = lax.all_gather(shard, AXES, axis=0, tiled=True)

    def z(self, p, *steps):
        if self.net.fast:
            for j in steps:
                self.send(f"{p}z{j}", self.data[p + "z0"], lambda c, j=j: j << 3)

    def near(self, p):
        if not self.net.fast:
            return
        block = jnp.stack([self.data.pop(f"{p}z{j}") for j in range(self.net.groups)])
        self.data[p + "m0"] = block
        self.send(p + "m1", block, first_bit)
        self.send(p + "m2", block, second_bit)

    def far(self, p):
        if self.net.fast:
            self.send(p + "m3", self.data[p + "m1"], second_bit)

    def core(self, p, *which):
        if self.net.fast:
            for i in which:
                self.send(f"{p}o{i}", self.data[f"{p}m{i}"], other_core)

    def pieces(self, p):
        if not self.net.fast:
            return [self.data.pop(p + "m0")]
        return [self.data.pop(p + k + str(i)) for k in "mo" for i in range(4)]


BSKIP, GAIN1, SHIFT1, BQUERY, BVALUE, BOUT, GAIN2, SHIFT2, BDOWN = range(9)


def packed_vectors(vectors, wide, rows):
    narrow = jnp.pad(jnp.stack(vectors), ((0, 0), (0, 128 - vectors[0].shape[0])))
    return jnp.pad(
        jnp.concatenate([narrow, wide.reshape(1, 128)], axis=0),
        ((0, rows - len(vectors) - 1), (0, 0)),
    )


def unpack_kernel(net, col, me_ref, *rest):
    pieces, (rows_ref, wide_ref, held, sems) = rest[:8], rest[8:]
    me = me_ref[0]
    masks = piece_masks(me & 1)
    copies = []
    for i, piece in enumerate(pieces):
        for j in range(net.groups):
            source = me ^ (masks[i] ^ (j << 3))
            copies.append(
                pltpu.make_async_copy(
                    piece.at[j, pl.ds(0, 16), pl.ds(col, 128)], held.at[source], sems.at[len(copies)]
                )
            )
    for copy in copies:
        copy.start()
    for copy in copies:
        copy.wait()
    for d in range(0, net.size, 4):
        tile = held[d].astype(F32)
        for k in range(1, 4):
            tile = tile + pltpu.roll(held[d + k].astype(F32), 32 * k, 1)
        rows_ref[:, 32 * d : 32 * d + 128] = tile
    for d in range(net.size):
        wide_ref[:, 128 * d : 128 * d + 128] = held[d].astype(F32)[9:10, :]


def unpack_vectors(net, me, pieces, col):
    return pl.pallas_call(
        functools.partial(unpack_kernel, net, col),
        in_specs=[SMEM] + [ANY] * len(pieces),
        out_shape=[
            jax.ShapeDtypeStruct((16, 32 * net.size), F32),
            jax.ShapeDtypeStruct((1, 128 * net.size), F32),
        ],
        scratch_shapes=[pltpu.VMEM((net.size, 16, 128), BF), pltpu.SemaphoreType.DMA((net.size,))],
        compiler_params=params(),
        cost_estimate=cost(1000, 200000),
        name="unpack_vectors",
    )(me, *pieces)


def sum_vectors(net, rows, start, stop):
    if not net.fast:
        return rows if start else lax.psum(rows, AXES)
    for bit in range(start, stop):
        rows = rows + net.pp(rows, lambda c: 1 << bit)
    return rows


class Scatter:
    def __init__(self, net, parts):
        self.net, self.keep, self.got = net, parts[0], []
        self.send = parts[-1]

    def summed(self, lo, hi, cols=slice(None)):
        total = self.keep[lo:hi, :, cols].astype(F32)
        for arr in self.got:
            total = total + arr[lo:hi, :, cols].astype(F32)
        return total

    def core(self):
        if not self.net.fast:
            total = self.keep[0].astype(F32)
            return lax.psum_scatter(total, AXES, scatter_dimension=0, tiled=True)
        return self.net.pp(self.send, other_core)

    def next(self, got, mask, lo):
        self.got.append(got)
        if not self.net.fast:
            return got
        return self.net.pp(self.summed(lo, 2 * lo).astype(BF), mask)

    def b(self, got):
        return self.next(got, second_bit, 2 * self.net.groups)

    def a(self, got):
        return self.next(got, first_bit, self.net.groups)

    def z(self, got):
        self.got.append(got)
        if not self.net.fast:
            return [got]
        return [
            self.net.pp(self.summed(j, j + 1)[0].astype(BF), lambda c, j=j: j << 3)
            for j in range(1, self.net.groups)
        ]

    def done(self, last, cols=slice(None)):
        if not self.net.fast:
            return last[0][:, cols]
        total = self.summed(0, 1, cols)[0]
        for arr in last:
            total = total + arr[:, cols].astype(F32)
        return total


def load_start(net, me, pieces, dst, sems, which=0, col=0):
    copies = []
    if not net.fast:
        copies.append(pltpu.make_async_copy(pieces[which], dst, sems.at[0]))
    else:
        masks = piece_masks(me & 1)
        rows, cols = dst.shape[0] // net.size, dst.shape[1]
        for i, piece in enumerate(pieces):
            for j in range(net.groups):
                source = me ^ (masks[i] ^ (j << 3))
                at = pl.multiple_of(source * rows, rows)
                copies.append(
                    pltpu.make_async_copy(
                        piece.at[j, :, pl.ds(col, cols)],
                        dst.at[pl.ds(at, rows), :],
                        sems.at[len(copies)],
                    )
                )
    for copy in copies:
        copy.start()
    return copies


def relative(net, rel, core):
    bit_one, bit_two, group = (rel >> 1) & 1, (rel >> 2) & 1, rel >> 3
    top = jnp.where(core == 0, bit_two, bit_one)
    low = jnp.where(core == 0, bit_one, bit_two)
    return (top << (net.high + 1)) | (low << net.high) | group


def store_copies(net, me, src, base, rows, total_rows, outs, col, sems, first_sem):
    cols = pl.ds(col, src.shape[1])
    if not net.fast:
        rows = pl.ds(base, rows)
        return [
            pltpu.make_async_copy(
                src.at[rows, :], outs[0].at[0, rows, cols], sems.at[first_sem]
            )
        ]
    copies = []
    shard = total_rows // net.size
    core = me & 1
    for i in range(0, rows // shard, 2):
        even = base // shard + i
        for k, out in enumerate(outs):
            owner_core = core if k == 0 else 1 - core
            target = even | owner_core
            rel = (me if k == 0 else me ^ 1) ^ target
            at = pl.multiple_of(target * shard, shard)
            copies.append(
                pltpu.make_async_copy(
                    src.at[pl.ds(at, shard), :],
                    out.at[relative(net, rel, owner_core), :, cols],
                    sems.at[first_sem + i + k],
                )
            )
    return copies


def dot(a, b):
    return jnp.dot(a, b, preferred_element_type=F32)


def dot_t(a, b):
    return lax.dot_general(a, b, (((1,), (1,)), ((), ())), preferred_element_type=F32)


def norm_parts(x):
    center = x - jnp.mean(x, axis=1, keepdims=True)
    spread = jnp.mean(center * center, axis=1, keepdims=True)
    rstd = lax.rsqrt(spread + EPSILON)
    return center * rstd, rstd


def sums(x):
    return jnp.sum(x, axis=0, keepdims=True)


def add_to(ref, value, step):
    @pl.when(step == 0)
    def _():
        ref[...] = value

    @pl.when(step > 0)
    def _():
        ref[...] += value


def row_block(tok):
    return min(512, tok)


def weight_scratch(net, *shapes):
    out = []
    for shape in shapes:
        out += [pltpu.VMEM(shape, BF), pltpu.SemaphoreType.DMA((net.shards,))]
    return out


def n_pieces(net, whole=1):
    return 8 if net.fast else whole


def skip_kernel(net, me_ref, frames, skip, *rest):
    np_ = n_pieces(net)
    pieces, (raw_ref, w, sems) = rest[:np_], rest[np_:]

    @pl.when(pl.program_id(0) == 0)
    def _():
        for copy in load_start(net, me_ref[0], pieces, w, sems):
            copy.wait()

    width = frames.shape[1]
    raw_ref[...] = dot(frames[...], w[:width, :]) + dot(skip[...], w[width:, :])


def skip_forward(net, me, frames, skip, pieces):
    tok, width = frames.shape
    blk = row_block(tok)
    rows = pl.BlockSpec((blk, width), lambda i: (i, 0))
    return pl.pallas_call(
        functools.partial(skip_kernel, net),
        grid=(tok // blk,),
        in_specs=[SMEM, rows, rows] + [ANY] * len(pieces),
        out_specs=rows,
        out_shape=jax.ShapeDtypeStruct((tok, width), F32),
        scratch_shapes=weight_scratch(net, (2 * width, width)),
        compiler_params=params(),
        cost_estimate=cost(4 * tok * width * width, tok * width * 8 + 4 * width * width),
        name="skip_forward",
    )(me, frames, skip, *pieces)


def vec_row(vecs, k):
    return vecs[k : k + 1, :]


def qkv_kernel(net, me_ref, raw, vecs, *rest):
    np_ = n_pieces(net)
    pieces, (normed_ref, out_ref, w, sems) = rest[:np_], rest[np_:]

    @pl.when(pl.program_id(0) == 0)
    def _():
        copies = load_start(net, me_ref[0], pieces, w, sems)
        for copy in copies:
            copy.wait()

    xhat, _ = norm_parts(raw[...] + vec_row(vecs, BSKIP))
    normed = (xhat * vec_row(vecs, GAIN1) + vec_row(vecs, SHIFT1)).astype(BF)
    normed_ref[...] = normed
    width = raw.shape[1]
    out_ref[:, :width] = (dot(normed, w[:, :width]) + vec_row(vecs, BQUERY)).astype(BF)
    out_ref[:, width : 2 * width] = dot(normed, w[:, width : 2 * width]).astype(BF)
    out_ref[:, 2 * width :] = (dot(normed, w[:, 2 * width :]) + vec_row(vecs, BVALUE)).astype(BF)


def qkv_forward(net, me, raw, vecs, pieces):
    tok, width = raw.shape
    cols = 3 * width
    blk = row_block(tok)
    return pl.pallas_call(
        functools.partial(qkv_kernel, net),
        grid=(tok // blk,),
        in_specs=[
            SMEM,
            pl.BlockSpec((blk, width), lambda i: (i, 0)),
            pl.BlockSpec((16, width), lambda i: (0, 0)),
        ]
        + [ANY] * len(pieces),
        out_specs=[
            pl.BlockSpec((blk, width), lambda i: (i, 0)),
            pl.BlockSpec((blk, cols), lambda i: (i, 0)),
        ],
        out_shape=[jax.ShapeDtypeStruct((tok, width), BF), jax.ShapeDtypeStruct((tok, cols), BF)],
        scratch_shapes=weight_scratch(net, (width, cols)),
        compiler_params=params(),
        cost_estimate=cost(2 * tok * width * cols, tok * width * 12 + 6 * width * width),
        name="qkv_forward",
    )(me, raw, vecs, *pieces)


def gelu_both(v):
    lead, cubic = 0.7978845608, 0.7978845608 * 0.044715
    square = v * v
    half = 0.5 + 0.5 * jnp.tanh(v * (lead + cubic * square))
    slope = half + (half - half * half) * (v * (2 * lead + (6 * cubic) * square))
    return v * half, slope


def up_kernel(net, me_ref, raw, mixed, vecs, b_up, *rest):
    np_ = n_pieces(net, 2)
    pieces, rest = rest[:np_], rest[np_:]
    second_ref, normed_ref, act_ref, pull_ref, w_out, sems_out, w_up, sems_up = rest

    @pl.when(pl.program_id(0) == 0)
    def _():
        copies = load_start(net, me_ref[0], pieces, w_out, sems_out, 0, 0)
        copies += load_start(net, me_ref[0], pieces, w_up, sems_up, 1, w_out.shape[1])
        for copy in copies:
            copy.wait()

    bias = vec_row(vecs, BSKIP) + vec_row(vecs, BOUT)
    second = raw[...] + dot(mixed[...], w_out[...]) + bias
    second_ref[...] = second
    xhat, _ = norm_parts(second)
    normed = (xhat * vec_row(vecs, GAIN2) + vec_row(vecs, SHIFT2)).astype(BF)
    normed_ref[...] = normed
    chunk = 1024
    for at in range(0, w_up.shape[1], chunk):
        part = slice(at, at + chunk)
        hidden = dot(normed, w_up[:, part]) + b_up[:, part]
        act, pull = gelu_both(hidden)
        act_ref[:, part] = act.astype(BF)
        pull_ref[:, part] = pull.astype(BF)


def up_forward(net, me, raw, mixed, pieces, vecs, b_up):
    tok, width = raw.shape
    ff = b_up.shape[1]
    blk = min(256, tok)
    rows = pl.BlockSpec((blk, width), lambda i: (i, 0))
    wide = pl.BlockSpec((blk, ff), lambda i: (i, 0))
    vec = pl.BlockSpec((16, width), lambda i: (0, 0))
    vec_ff = pl.BlockSpec((1, ff), lambda i: (0, 0))
    return pl.pallas_call(
        functools.partial(up_kernel, net),
        grid=(tok // blk,),
        in_specs=[SMEM, rows, rows, vec, vec_ff] + [ANY] * len(pieces),
        out_specs=[rows, rows, wide, wide],
        out_shape=[
            jax.ShapeDtypeStruct((tok, width), F32),
            jax.ShapeDtypeStruct((tok, width), BF),
            jax.ShapeDtypeStruct((tok, ff), BF),
            jax.ShapeDtypeStruct((tok, ff), BF),
        ],
        scratch_shapes=weight_scratch(net, (width, width), (width, ff)),
        compiler_params=params(),
        cost_estimate=cost(
            2 * tok * width * (width + ff), tok * (width * 12 + ff * 4) + 2 * width * (width + ff)
        ),
        name="up_forward",
    )(me, raw, mixed, vecs, b_up, *pieces)


def down_kernel(net, me_ref, second, act, vecs, *rest):
    pieces, (out_ref, w, sems) = rest[: n_pieces(net)], rest[-3:]

    @pl.when(pl.program_id(0) == 0)
    def _():
        for copy in load_start(net, me_ref[0], pieces, w, sems):
            copy.wait()

    out_ref[...] = (second[...] + dot(act[...], w[...]) + vec_row(vecs, BDOWN)).astype(BF)


def down_forward(net, me, second, act, pieces, vecs, part, parts, before=()):
    tok, width = second.shape
    ff = act.shape[1]
    blk = min(256, tok)
    steps = tok // blk // parts
    start = part * steps
    rows = pl.BlockSpec((blk, width), lambda i: (start + i, 0))
    wide = pl.BlockSpec((blk, ff), lambda i: (start + i, 0))
    vec = pl.BlockSpec((16, width), lambda i: (0, 0))
    return pl.pallas_call(
        functools.partial(down_kernel, net),
        grid=(steps,),
        in_specs=[SMEM, rows, wide, vec] + [ANY] * (len(pieces) + len(before)),
        out_specs=rows,
        out_shape=jax.ShapeDtypeStruct((tok, width), BF),
        input_output_aliases={4 + len(pieces): 0} if before else {},
        scratch_shapes=weight_scratch(net, (ff, width)),
        compiler_params=params(),
        cost_estimate=cost(
            2 * tok * width * ff // parts, tok * (width * 6 + ff * 2) // parts + 2 * width * ff
        ),
        name="down_forward",
    )(me, second, act, vecs, *pieces, *before)


def hidden_kernel(net, me_ref, pull, cot, *rest):
    np_ = n_pieces(net)
    pieces, (gh_ref, bsum_ref, csum_ref, w, sems) = rest[:np_], rest[np_:]
    step = pl.program_id(0)

    @pl.when(step == 0)
    def _():
        for copy in load_start(net, me_ref[0], pieces, w, sems):
            copy.wait()

    chunk = 1024
    for at in range(0, w.shape[0], chunk):
        part = slice(at, at + chunk)
        gh = (dot_t(cot[...], w[part, :]) * pull[:, part].astype(F32)).astype(BF)
        gh_ref[:, part] = gh
        add_to(bsum_ref.at[:, part], sums(gh.astype(F32)), step)
    add_to(csum_ref, sums(cot[...].astype(F32)), step)


def hidden_back(net, me, pull, cot, pieces):
    tok, width = cot.shape
    ff = pull.shape[1]
    blk = row_block(tok)
    rows = pl.BlockSpec((blk, width), lambda i: (i, 0))
    wide = pl.BlockSpec((blk, ff), lambda i: (i, 0))
    vec = pl.BlockSpec((1, width), lambda i: (0, 0))
    vec_ff = pl.BlockSpec((1, ff), lambda i: (0, 0))
    return pl.pallas_call(
        functools.partial(hidden_kernel, net),
        grid=(tok // blk,),
        in_specs=[SMEM, wide, rows] + [ANY] * len(pieces),
        out_specs=[wide, vec_ff, vec],
        out_shape=[
            jax.ShapeDtypeStruct((tok, ff), BF),
            jax.ShapeDtypeStruct((1, ff), F32),
            jax.ShapeDtypeStruct((1, width), F32),
        ],
        scratch_shapes=weight_scratch(net, (ff, width)),
        compiler_params=params(),
        cost_estimate=cost(2 * tok * width * ff, tok * (width * 2 + ff * 4) + 2 * width * ff),
        name="hidden_back",
    )(me, pull, cot, *pieces)


def grad_kernel(net, lefts, rights, blk, col, outs_n, into_n, me_ref, *rest):
    left_refs, right_refs = rest[:lefts], rest[lefts : lefts + rights]
    rest = rest[lefts + rights + into_n :]
    outs, (acc, sems) = rest[:outs_n], rest[outs_n:]
    step = pl.program_id(0)
    total, cols = acc.shape
    steps = total // blk
    per_left = steps // lefts
    per_step = sems.shape[0] // steps
    for s in range(steps):

        @pl.when(step == s)
        def _():
            left = left_refs[s // per_left][...].T
            at = 0
            for right in right_refs:
                chunk = min(1024, right.shape[1])
                for i in range(0, right.shape[1], chunk):
                    acc[s * blk : (s + 1) * blk, at : at + chunk] = dot(
                        left, right[:, i : i + chunk]
                    ).astype(BF)
                    at += chunk
            for copy in store_copies(
                net, me_ref[0], acc, s * blk, blk, total, outs, col, sems, s * per_step
            ):
                copy.start()

    @pl.when(step == steps - 1)
    def _():
        for s in range(steps):
            for copy in store_copies(
                net, me_ref[0], acc, s * blk, blk, total, outs, col, sems, s * per_step
            ):
                copy.wait()


def weight_grad(net, me, lefts, rights, name, into=(), col=0, all_cols=0):
    tok = lefts[0].shape[0]
    cols = sum(right.shape[1] for right in rights)
    each = lefts[0].shape[1]
    total = each * len(lefts)
    blk = min(512, each)
    per_left = each // blk
    steps = total // blk
    all_cols = all_cols or cols
    if net.fast:
        per_step = blk // (total // net.size)
        shapes = [jax.ShapeDtypeStruct((net.size // 2, total // net.size, all_cols), BF)] * 2
    else:
        per_step = 1
        shapes = [jax.ShapeDtypeStruct((1, total, all_cols), BF)]

    def index(k):
        return lambda i: (0, jnp.clip(i - k * per_left, 0, per_left - 1))

    first_into = 1 + len(lefts) + len(rights)
    return pl.pallas_call(
        functools.partial(
            grad_kernel, net, len(lefts), len(rights), blk, col, len(shapes), len(into)
        ),
        grid=(steps,),
        in_specs=[SMEM]
        + [pl.BlockSpec((tok, blk), index(k)) for k in range(len(lefts))]
        + [
            pl.BlockSpec(right.shape, lambda i: (0, 0), pipeline_mode=pl.Buffered(1))
            for right in rights
        ]
        + [ANY] * len(into),
        out_specs=[ANY] * len(shapes),
        out_shape=shapes,
        input_output_aliases={first_into + k: k for k in range(len(into))},
        scratch_shapes=[
            pltpu.VMEM((total, cols), BF),
            pltpu.SemaphoreType.DMA((steps * per_step,)),
        ],
        compiler_params=params(),
        cost_estimate=cost(
            2 * tok * total * cols, 2 * tok * (total + cols) + 2 * total * cols
        ),
        name=name,
    )(me, *lefts, *rights, *into)


def norm_back(dn, x, gain):
    xhat, rstd = norm_parts(x)
    scaled = dn * gain
    mean_one = jnp.mean(scaled, axis=1, keepdims=True)
    mean_two = jnp.mean(scaled * xhat, axis=1, keepdims=True)
    return (scaled - mean_one - xhat * mean_two) * rstd, dn * xhat


def second_kernel(net, me_ref, gh, second, cot, vecs, *rest):
    np_ = n_pieces(net, 2)
    pieces, rest = rest[:np_], rest[np_:]
    gsec_ref, gattn_ref, gmix_ref, ggain_ref, gshift_ref, gbout_ref = rest[:6]
    w_up, sems_up, w_out, sems_out = rest[6:]
    step = pl.program_id(0)

    @pl.when(step == 0)
    def _():
        copies = load_start(net, me_ref[0], pieces, w_up, sems_up, 1, w_out.shape[1])
        copies += load_start(net, me_ref[0], pieces, w_out, sems_out, 0, 0)
        for copy in copies:
            copy.wait()

    dn = dot_t(gh[...], w_up[...])
    pulled, dx = norm_back(dn, second[...], vec_row(vecs, GAIN2))
    gsec = cot[...].astype(F32) + pulled
    gsec_ref[...] = gsec
    gattn = gsec.astype(BF)
    gattn_ref[...] = gattn
    gmix_ref[...] = dot_t(gattn, w_out[...]).astype(BF)
    add_to(ggain_ref, sums(dx), step)
    add_to(gshift_ref, sums(dn), step)
    add_to(gbout_ref, sums(gattn.astype(F32)), step)


def second_back(net, me, gh, second, cot, pieces, vecs):
    tok, width = second.shape
    ff = gh.shape[1]
    blk = min(256, tok)
    rows = pl.BlockSpec((blk, width), lambda i: (i, 0))
    wide = pl.BlockSpec((blk, ff), lambda i: (i, 0))
    vec = pl.BlockSpec((1, width), lambda i: (0, 0))
    vec_shape = jax.ShapeDtypeStruct((1, width), F32)
    return pl.pallas_call(
        functools.partial(second_kernel, net),
        grid=(tok // blk,),
        in_specs=[SMEM, wide, rows, rows, pl.BlockSpec((16, width), lambda i: (0, 0))]
        + [ANY] * len(pieces),
        out_specs=[rows, rows, rows, vec, vec, vec],
        out_shape=[
            jax.ShapeDtypeStruct((tok, width), F32),
            jax.ShapeDtypeStruct((tok, width), BF),
            jax.ShapeDtypeStruct((tok, width), BF),
            vec_shape,
            vec_shape,
            vec_shape,
        ],
        scratch_shapes=weight_scratch(net, (width, ff), (width, width)),
        compiler_params=params(),
        cost_estimate=cost(
            2 * tok * width * (width + ff), tok * (width * 14 + ff * 2) + 2 * width * (width + ff)
        ),
        name="second_back",
    )(me, gh, second, cot, vecs, *pieces)


def first_kernel(net, me_ref, gq, gk, gv, raw, gsec, vecs, *rest):
    np_ = n_pieces(net)
    pieces, rest = rest[:np_], rest[np_:]
    gfirst_ref, ggain_ref, gshift_ref, gbskip_ref, gbq_ref, gbv_ref, w, sems = rest
    step = pl.program_id(0)

    @pl.when(step == 0)
    def _():
        for copy in load_start(net, me_ref[0], pieces, w, sems):
            copy.wait()

    width = gq.shape[1]
    dn = dot_t(gq[...], w[:, :width])
    dn = dn + dot_t(gk[...], w[:, width : 2 * width])
    dn = dn + dot_t(gv[...], w[:, 2 * width :])
    pulled, dx = norm_back(dn, raw[...] + vec_row(vecs, BSKIP), vec_row(vecs, GAIN1))
    gfirst = (gsec[...] + pulled).astype(BF)
    gfirst_ref[...] = gfirst
    add_to(ggain_ref, sums(dx), step)
    add_to(gshift_ref, sums(dn), step)
    add_to(gbskip_ref, sums(gfirst.astype(F32)), step)
    add_to(gbq_ref, sums(gq[...].astype(F32)), step)
    add_to(gbv_ref, sums(gv[...].astype(F32)), step)


def first_back(net, me, gq, gk, gv, raw, gsec, pieces, vecs):
    tok, width = raw.shape
    blk = min(256, tok)
    rows = pl.BlockSpec((blk, width), lambda i: (i, 0))
    vec = pl.BlockSpec((1, width), lambda i: (0, 0))
    vec_shape = jax.ShapeDtypeStruct((1, width), F32)
    return pl.pallas_call(
        functools.partial(first_kernel, net),
        grid=(tok // blk,),
        in_specs=[SMEM, rows, rows, rows, rows, rows, pl.BlockSpec((16, width), lambda i: (0, 0))]
        + [ANY] * len(pieces),
        out_specs=[rows] + [vec] * 5,
        out_shape=[jax.ShapeDtypeStruct((tok, width), BF)] + [vec_shape] * 5,
        scratch_shapes=weight_scratch(net, (width, 3 * width)),
        compiler_params=params(),
        cost_estimate=cost(6 * tok * width * width, tok * width * 16 + 6 * width * width),
        name="first_back",
    )(me, gq, gk, gv, raw, gsec, vecs, *pieces)


def joined_kernel(net, me_ref, gfirst, *rest):
    np_ = n_pieces(net)
    pieces, (gframes_ref, gskip_ref, w, sems) = rest[:np_], rest[np_:]

    @pl.when(pl.program_id(0) == 0)
    def _():
        for copy in load_start(net, me_ref[0], pieces, w, sems):
            copy.wait()

    width = gframes_ref.shape[1]
    gframes_ref[...] = dot_t(gfirst[...], w[:width, :]).astype(BF)
    gskip_ref[...] = dot_t(gfirst[...], w[width:, :]).astype(BF)


def joined_back(net, me, gfirst, pieces):
    tok, width = gfirst.shape
    blk = row_block(tok)
    rows = pl.BlockSpec((blk, width), lambda i: (i, 0))
    out = jax.ShapeDtypeStruct((tok, width), BF)
    return pl.pallas_call(
        functools.partial(joined_kernel, net),
        grid=(tok // blk,),
        in_specs=[SMEM, rows] + [ANY] * len(pieces),
        out_specs=[rows, rows],
        out_shape=[out, out],
        scratch_shapes=weight_scratch(net, (2 * width, width)),
        compiler_params=params(),
        cost_estimate=cost(4 * tok * width * width, tok * width * 6 + 4 * width * width),
        name="joined_back",
    )(me, gfirst, *pieces)


def far_apart(row_tag, col_tag, row_at):
    shape = (row_tag.shape[0], col_tag.shape[1])
    i = row_at + lax.broadcasted_iota(jnp.int32, shape, 0)
    j = lax.broadcasted_iota(jnp.int32, shape, 1)
    ok = (row_tag == col_tag) | (i == j)
    return jnp.where(ok, jnp.abs(i - j).astype(F32), FAR)


def head_slope(head):
    return jnp.exp2((jnp.full((1, 1), head, jnp.int32).astype(F32) + 1.0) * (-8.0 / HEADS))


def far_kernel(blk, tag_q, tag_k, out_ref):
    out_ref[...] = far_apart(tag_q[...], tag_k[...], pl.program_id(0) * blk)


def far_matrix(row_tag, col_tag):
    tok = row_tag.shape[0]
    blk = min(256, tok)
    return pl.pallas_call(
        functools.partial(far_kernel, blk),
        grid=(tok // blk,),
        in_specs=[pl.BlockSpec((blk, 1), lambda i: (i, 0)), pl.BlockSpec((1, tok), lambda i: (0, 0))],
        out_specs=pl.BlockSpec((blk, tok), lambda i: (i, 0)),
        out_shape=jax.ShapeDtypeStruct((tok, tok), F32),
        compiler_params=params(),
        cost_estimate=cost(8 * tok * tok, 4 * tok * tok),
        name="far_matrix",
    )(row_tag.reshape(tok, 1), col_tag.reshape(1, tok))


def attend_kernel(size, blk, first_pair, q, k, v, far, *rest):
    out_ref, lse_ref, columns = rest[-3:]
    pair = first_pair + pl.program_id(0)
    tok = q.shape[0]
    lane = lax.broadcasted_iota(jnp.int32, (1, 2 * size), 1)
    scale = size**-0.5
    for i in range(tok // blk):
        at = slice(i * blk, (i + 1) * blk)
        q_blk = q[at, :] * scale
        outs, lse = [], []
        for h in range(2):
            mine = (lane >= h * size) & (lane < (h + 1) * size)
            scores = dot_t(jnp.where(mine, q_blk, 0), k[...]) - head_slope(2 * pair + h) * far[at, :]
            top = jnp.max(scores, axis=1, keepdims=True)
            expo = jnp.exp(scores - top)
            denom = jnp.sum(expo, axis=1, keepdims=True)
            outs.append(dot(expo.astype(BF), v[...]) / denom)
            lse.append(top + jnp.log(denom))
        out_ref[at, :] = jnp.where(lane < size, outs[0], outs[1]).astype(BF)
        columns[at, :] = jnp.where(lane < size, lse[0], lse[1])
    rows = columns[...].T
    lse_ref[0, 0:1, :] = rows[0:1, :]
    lse_ref[0, 1:2, :] = rows[size : size + 1, :]


def attend(qkv, far, heads, part, parts, before=()):
    tok = qkv.shape[0]
    width = qkv.shape[1] // 3
    size = width // heads
    pairs = heads // 2
    here = pairs // parts
    start = part * here
    blk = min(256, tok)

    def cols(k):
        return pl.BlockSpec((tok, 2 * size), lambda p: (0, k * pairs + start + p))

    return pl.pallas_call(
        functools.partial(attend_kernel, size, blk, start),
        grid=(here,),
        in_specs=[
            cols(0),
            cols(1),
            cols(2),
            pl.BlockSpec((tok, tok), lambda p: (0, 0), pipeline_mode=pl.Buffered(1)),
        ]
        + [ANY] * len(before),
        out_specs=[cols(0), pl.BlockSpec((1, 8, tok), lambda p: (start + p, 0, 0))],
        out_shape=[
            jax.ShapeDtypeStruct((tok, width), BF),
            jax.ShapeDtypeStruct((pairs, 8, tok), F32),
        ],
        input_output_aliases={4 + k: k for k in range(len(before))},
        scratch_shapes=[pltpu.VMEM((tok, 2 * size), F32)],
        compiler_params=params(),
        cost_estimate=cost(
            16 * here * 2 * tok * tok * size, tok * width * 8 // parts, here * 2 * tok * tok
        ),
        name="attend",
    )(qkv, qkv, qkv, far, *before)


def attend_back_kernel(size, blk, first_pair, q, k, v, g, o, lse, far, *rest):
    gq_ref, gk_ref, gv_ref = rest[-3:]
    pair = first_pair + pl.program_id(0)
    tok = q.shape[0]
    lane = lax.broadcasted_iota(jnp.int32, (1, 2 * size), 1)
    scale = size**-0.5
    q_all = q[...] * scale
    g_all = g[...]
    products = (g_all.astype(F32) * o[...].astype(F32)).T
    k_t = (k[...] * scale).astype(F32).T.astype(BF)
    grads_q = []
    for h in range(2):
        mine = (lane >= h * size) & (lane < (h + 1) * size)
        q_h = jnp.where(mine, q_all, 0)
        g_h = jnp.where(mine, g_all, 0)
        delta = jnp.sum(products[h * size : (h + 1) * size, :], axis=0, keepdims=True)
        norm = lse[0, h : h + 1, :]
        slope = head_slope(2 * pair + h)
        grad_q = jnp.zeros((size, tok), F32)
        for i in range(tok // blk):
            at = slice(i * blk, (i + 1) * blk)
            scores = dot_t(k[at, :], q_h) - slope * far[at, :]
            probs = jnp.exp(scores - norm)
            pulled = dot_t(v[at, :], g_h)
            ds = (probs * (pulled - delta)).astype(BF)
            gv = dot(probs.astype(BF), g_all)
            gk = dot(ds, q_all)
            grad_q = grad_q + dot(k_t[h * size : (h + 1) * size, at], ds)
            if h == 0:
                gv_ref[at, :] = gv.astype(BF)
                gk_ref[at, :] = gk.astype(BF)
            else:
                gv_ref[at, :] = jnp.where(mine, gv.astype(BF), gv_ref[at, :])
                gk_ref[at, :] = jnp.where(mine, gk.astype(BF), gk_ref[at, :])
        grads_q.append(grad_q)
    gq_ref[...] = jnp.concatenate(grads_q, axis=0).T.astype(BF)


def attend_back(qkv, grad_mixed, mixed, lse, far, heads, part, parts, before=()):
    tok = qkv.shape[0]
    width = qkv.shape[1] // 3
    size = width // heads
    pairs = heads // 2
    here = pairs // parts
    start = part * here
    blk = min(256, tok)

    def cols(k):
        return pl.BlockSpec((tok, 2 * size), lambda p: (0, k * pairs + start + p))

    out = jax.ShapeDtypeStruct((tok, width), BF)
    return pl.pallas_call(
        functools.partial(attend_back_kernel, size, blk, start),
        grid=(here,),
        in_specs=[
            cols(0),
            cols(1),
            cols(2),
            cols(0),
            cols(0),
            pl.BlockSpec((1, 8, tok), lambda p: (start + p, 0, 0)),
            pl.BlockSpec((tok, tok), lambda p: (0, 0), pipeline_mode=pl.Buffered(1)),
        ]
        + [ANY] * len(before),
        out_specs=[cols(0)] * 3,
        out_shape=[out] * 3,
        input_output_aliases={7 + k: k for k in range(len(before))},
        compiler_params=params(),
        cost_estimate=cost(
            40 * here * 2 * tok * tok * size, tok * width * 16 // parts, here * 2 * tok * tok
        ),
        name="attend_back",
    )(qkv, qkv, qkv, grad_mixed, mixed, lse, far, *before)


def tags(length_row, mask_row, tok):
    order = jnp.arange(length_row.shape[0])
    ends = jnp.sum(jnp.where(order[:, None] <= order[None, :], length_row[:, None], 0), axis=0)
    slots = jnp.arange(tok, dtype=jnp.int32)
    segment = jnp.sum((slots[:, None] >= ends[None, :]).astype(jnp.int32), axis=1)
    used = slots < jnp.sum(length_row)
    return jnp.where(used, segment, -1), jnp.where(used & (mask_row == 1), segment, -2)


def body(size, frames, skip, lengths, key_mask, cotangent, *weights):
    (
        w_skip, b_skip, pre_attn_gain, pre_attn_bias, w_qkv, b_query, b_value, w_out, b_out,
        pre_ffn_gain, pre_ffn_bias, w_up, b_up, w_down, b_down,
    ) = weights
    tok, width = frames.shape
    net = Net(
        size,
        min(w.shape[0] for w in (w_skip, w_qkv, w_out, w_up, w_down)),
        (b_skip.shape[0], b_up.shape[0]),
    )
    index = lax.axis_index(AXES).astype(jnp.int32)
    me = index.reshape(1)
    narrow = (
        b_skip, pre_attn_gain, pre_attn_bias, b_query, b_value, b_out, pre_ffn_gain, pre_ffn_bias, b_down,
    )

    def stacked(arrays):
        return jnp.stack(arrays) if net.fast else arrays[0]

    flow = Flow(net)
    flow.own("s", w_skip)
    flow.z("s", 1, 2, 3)
    w_two, w_three = w_qkv, [w_out, w_up]
    if net.fast:
        w_two = jnp.concatenate([w_qkv, packed_vectors(narrow, b_up, w_qkv.shape[0])], axis=1)
        w_three = [jnp.concatenate(w_three, axis=1)]
    w_two, w_three, w_down = flow.end((w_two, w_three, w_down), "s")
    flow.own("q", w_two)
    flow.own("u", w_three[-1])
    flow.own("o", w_three[0])
    flow.own("d", w_down)
    flow.near("s")
    flow.z("q", 1, 2)
    tag_q, tag_k = tags(lengths[0], key_mask, tok)
    tag_q, tag_k = flow.end((tag_q, tag_k), "s", "q")
    flow.far("s")
    flow.core("s", 0, 1)
    flow.z("q", 3)
    far = far_matrix(tag_q, tag_k)
    far, tag_q = flow.end((far, tag_q), "s", "q", "u")
    flow.core("s", 2, 3)
    flow.near("q")
    flow.z("u", 2)
    far_t = far_matrix(tag_k, tag_q)
    frames, far_t = flow.end((frames, far_t), "s")
    pieces_s = flow.pieces("s")
    raw = skip_forward(net, me, frames, skip, pieces_s)
    raw = flow.end(raw, "q", "u")
    flow.far("q")
    flow.core("q", 0)
    flow.z("u", 1, 3)
    raw = flow.end(raw, "q")
    flow.core("q", 1, 2, 3)
    raw = flow.end(raw, "q", "u")
    flow.near("u")
    pieces_q = flow.pieces("q")
    if net.fast:
        vecs, bup = unpack_vectors(net, me, pieces_q, 3 * width)
    else:
        every = [lax.all_gather(v, AXES, axis=0, tiled=True).astype(F32) for v in (*narrow, b_up)]
        vecs, bup = jnp.pad(jnp.stack(every[:-1]), ((0, 16 - len(narrow)), (0, 0))), every[-1][None]
    normed, qkv = qkv_forward(net, me, raw, vecs, pieces_q)
    qkv = flow.end(qkv, "d")
    flow.z("d", 1, 2)
    attended = attend(qkv, far, HEADS, 0, 2)
    attended = flow.end(attended, "u", "d")
    flow.far("u")
    flow.core("u", 0, 1, 2)
    flow.z("d", 3)
    attended = attend(qkv, far, HEADS, 1, 2, attended)
    attended = flow.end(attended, "u", "d")
    flow.core("u", 3)
    attended = flow.end(attended, "u", "d")
    flow.near("d")
    mixed, lse = attended
    pieces_u = ([] if net.fast else flow.pieces("o")) + flow.pieces("u")
    second, normed2, act, pull = up_forward(net, me, raw, mixed, pieces_u, vecs, bup)
    act = flow.end(act, "d")
    flow.far("d")
    flow.core("d", 0, 1, 2)
    down = Scatter(net, weight_grad(net, me, [act], [cotangent], "grad_down"))
    down.keep, down.send = flow.end((down.keep, down.send), "d")
    flow.core("d", 3)
    pieces_d = flow.pieces("d")

    down.keep, down.send, pieces_d = bar(down.keep, down.send, pieces_d)
    down_got = down.core()
    gh, gbup, gbdown = hidden_back(net, me, pull, cotangent, pieces_d)
    gh, down_got = bar(gh, down_got)
    down_got = down.b(down_got)
    up_cols = 4 * width + width if net.fast else 0
    up_parts = weight_grad(net, me, [normed2], [gh], "grad_up", all_cols=up_cols)
    gh, up_parts = bar(gh, up_parts)
    gsec, gattn, gmixed, ggain2, gshift2, gbout = second_back(
        net, me, gh, second, cotangent, pieces_u, vecs
    )
    gattn, gmixed, down_got = bar(gattn, gmixed, down_got)
    down_got = down.a(down_got)
    if net.fast:
        up = Scatter(
            net,
            weight_grad(net, me, [mixed], [gattn], "grad_out", up_parts, 4 * width, up_cols),
        )
        out = None
    else:
        up = Scatter(net, up_parts)
        out = Scatter(net, weight_grad(net, me, [mixed], [gattn], "grad_out"))
    gmixed, up.keep, up.send = bar(gmixed, up.keep, up.send)
    up_got = up.core()
    back = (qkv, gmixed, mixed, lse, far_t, HEADS)
    grads = attend_back(*back, 0, 4)
    grads, down_got, up_got = bar(grads, down_got, up_got)
    down_got = down.z(down_got)
    up_got = up.b(up_got)
    grads = attend_back(*back, 1, 4, grads)
    grads = attend_back(*back, 2, 4, grads)
    grads, down_got, up_got = bar(grads, down_got, up_got)
    up_got = up.a(up_got)
    grads = attend_back(*back, 3, 4, grads)
    (gq, gk, gv), up_got = bar(grads, up_got)
    up_got = up.z(up_got)
    gqkv = Scatter(net, weight_grad(net, me, [normed], [gq, gk, gv], "grad_qkv"))
    gq, gqkv.keep, gqkv.send, up_got = bar(gq, gqkv.keep, gqkv.send, up_got)
    qkv_got = gqkv.core()
    gfirst, ggain1, gshift1, gbskip, gbq, gbv = first_back(
        net, me, gq, gk, gv, raw, gsec, pieces_q, vecs
    )
    gfirst, qkv_got, ggain1 = bar(gfirst, qkv_got, ggain1)
    qkv_got = gqkv.b(qkv_got)
    rows = [gbskip, ggain1, gshift1, gbq, gbv, gbout, ggain2, gshift2, gbdown, gbup.reshape(-1, width)]
    rows = sum_vectors(net, jnp.concatenate(rows, axis=0), 0, 1)
    gskip_w = Scatter(net, weight_grad(net, me, [frames, skip], [gfirst], "grad_skip"))
    gfirst, gskip_w.keep, gskip_w.send, rows, qkv_got = bar(
        gfirst, gskip_w.keep, gskip_w.send, rows, qkv_got
    )
    qkv_got = gqkv.a(qkv_got)
    skip_got = gskip_w.core()
    rows = sum_vectors(net, rows, 1, 2)
    gframes, gskip = joined_back(net, me, gfirst, pieces_s)
    gframes, qkv_got, skip_got, second, rows = bar(gframes, qkv_got, skip_got, second, rows)
    skip_got = gskip_w.b(skip_got)
    qkv_got = gqkv.z(qkv_got)
    rows = sum_vectors(net, rows, 2, 3)
    layer_out = down_forward(net, me, second, act, pieces_d, vecs, 0, 2)
    layer_out, qkv_got, skip_got, rows = bar(layer_out, qkv_got, skip_got, rows)
    skip_got = gskip_w.a(skip_got)
    rows = sum_vectors(net, rows, 3, 4)
    layer_out = down_forward(net, me, second, act, pieces_d, vecs, 1, 2, [layer_out])
    layer_out, skip_got, rows = bar(layer_out, skip_got, rows)
    skip_got = gskip_w.z(skip_got)
    rows = sum_vectors(net, rows, 4, net.bits)

    def mine(row):
        each = width // size
        return lax.dynamic_slice(rows[row], (index * each,), (each,))

    wide = rows[9:].reshape(-1)
    each = wide.shape[0] // size
    o_bup = lax.dynamic_slice(wide, (index * each,), (each,))
    up_out = up.done(up_got, slice(0, 4 * width) if net.fast else slice(None))
    if net.fast:
        out_out = up.done(up_got, slice(4 * width, 5 * width))
    else:
        out_out = out.core()
    return (
        layer_out,
        gframes,
        gskip,
        gskip_w.done(skip_got),
        mine(0),
        mine(1),
        mine(2),
        gqkv.done(qkv_got),
        mine(3),
        mine(4),
        out_out,
        mine(5),
        mine(6),
        mine(7),
        up_out,
        o_bup,
        down.done(down_got),
        mine(8),
    )


def solution(mesh):
    mat, vec = P(AXES, None), P(AXES)
    size = math.prod(mesh.shape.values())
    return jax.shard_map(
        functools.partial(body, size),
        mesh=mesh,
        in_specs=(
            mat, mat, mat, vec, mat,
            mat, vec, vec, vec, mat, vec, vec, mat, vec, vec, vec, mat, vec, mat, vec,
        ),
        out_specs=(
            mat, mat, mat,
            mat, vec, vec, vec, mat, vec, vec, mat, vec, vec, vec, mat, vec, mat, vec,
        ),
        check_vma=False,
    )
```

```python
import functools
import math

import jax
import jax.numpy as jnp
from jax import lax
from jax.experimental import pallas as pl
from jax.experimental.pallas import tpu as pltpu
from jax.sharding import PartitionSpec as P

HEADS = 16
EPSILON = 1e-05
FAR = 1e32
AXES = ("wide", "narrow")
BF = jnp.bfloat16
F32 = jnp.float32
VMEM_LIMIT = 36 * 1024 * 1024
VMEM_MOST = 58 * 1024 * 1024

ANY = pl.BlockSpec(memory_space=pl.ANY)
SMEM = pl.BlockSpec(memory_space=pltpu.SMEM)


def params(limit=VMEM_LIMIT):
    return pltpu.CompilerParams(vmem_limit_bytes=limit)


def cost(flops, nbytes, trans=0):
    return pl.CostEstimate(flops=int(flops), bytes_accessed=int(nbytes), transcendentals=int(trans))


class Net:
    def __init__(self, size, rows_min, vec_rows):
        self.size = size
        self.bits = size.bit_length() - 1
        self.high = self.bits - 3
        self.groups = 1 << self.high
        self.fast = size == 1 << self.bits and self.bits >= 3 and rows_min % 16 == 0 and vec_rows == (32, 128)
        self.shards = size if self.fast else 1

    def pp(self, x, mask):
        if not self.fast:
            return x
        pairs = [(d, d ^ mask(d & 1)) for d in range(self.size)]
        return lax.ppermute(x, AXES, pairs)


def first_bit(core):
    return 2 + 2 * core


def second_bit(core):
    return 4 - 2 * core


def other_core(core):
    return 1


def piece_masks(core):
    a, b = first_bit(core), second_bit(core)
    return [0, a, b, 6, 1, 1 ^ b, 1 ^ a, 7]


def bar(*values):
    return lax.optimization_barrier(values)


class Flow:
    def __init__(self, net):
        self.net, self.data = net, {}

    def end(self, values, *prefixes):
        names = [n for n in self.data if n.startswith(prefixes)] if prefixes else []
        values, arrays = bar(values, [self.data[n] for n in names])
        self.data.update(zip(names, arrays))
        return values

    def send(self, name, x, mask):
        self.data[name] = self.net.pp(x, mask)

    def own(self, p, shard):
        if self.net.fast:
            self.data[p + "z0"] = shard
        else:
            self.data[p + "m0"] = lax.all_gather(shard, AXES, axis=0, tiled=True)

    def z(self, p, *steps):
        if self.net.fast:
            for j in steps:
                self.send(f"{p}z{j}", self.data[p + "z0"], lambda c, j=j: j << 3)

    def near(self, p):
        if not self.net.fast:
            return
        block = jnp.stack([self.data.pop(f"{p}z{j}") for j in range(self.net.groups)])
        self.data[p + "m0"] = block
        self.send(p + "m1", block, first_bit)
        self.send(p + "m2", block, second_bit)

    def far(self, p):
        if self.net.fast:
            self.send(p + "m3", self.data[p + "m1"], second_bit)

    def core(self, p, *which):
        if self.net.fast:
            for i in which:
                self.send(f"{p}o{i}", self.data[f"{p}m{i}"], other_core)

    def pieces(self, p):
        if not self.net.fast:
            return [self.data.pop(p + "m0")]
        return [self.data.pop(p + k + str(i)) for k in "mo" for i in range(4)]


BSKIP, GAIN1, SHIFT1, BQUERY, BVALUE, BOUT, GAIN2, SHIFT2, BDOWN = range(9)


def packed_vectors(vectors, wide, rows):
    narrow = jnp.pad(jnp.stack(vectors), ((0, 0), (0, 128 - vectors[0].shape[0])))
    return jnp.pad(
        jnp.concatenate([narrow, wide.reshape(1, 128)], axis=0),
        ((0, rows - len(vectors) - 1), (0, 0)),
    )


def unpack_kernel(net, col, me_ref, *rest):
    pieces, (rows_ref, wide_ref, held, sems) = rest[:8], rest[8:]
    me = me_ref[0]
    masks = piece_masks(me & 1)
    copies = []
    for i, piece in enumerate(pieces):
        for j in range(net.groups):
            source = me ^ (masks[i] ^ (j << 3))
            copies.append(
                pltpu.make_async_copy(
                    piece.at[j, pl.ds(0, 16), pl.ds(col, 128)], held.at[source], sems.at[len(copies)]
                )
            )
    for copy in copies:
        copy.start()
    for copy in copies:
        copy.wait()
    for d in range(0, net.size, 4):
        tile = held[d].astype(F32)
        for k in range(1, 4):
            tile = tile + pltpu.roll(held[d + k].astype(F32), 32 * k, 1)
        rows_ref[:, 32 * d : 32 * d + 128] = tile
    for d in range(net.size):
        wide_ref[:, 128 * d : 128 * d + 128] = held[d].astype(F32)[9:10, :]


def unpack_vectors(net, me, pieces, col):
    return pl.pallas_call(
        functools.partial(unpack_kernel, net, col),
        in_specs=[SMEM] + [ANY] * len(pieces),
        out_shape=[
            jax.ShapeDtypeStruct((16, 32 * net.size), F32),
            jax.ShapeDtypeStruct((1, 128 * net.size), F32),
        ],
        scratch_shapes=[pltpu.VMEM((net.size, 16, 128), BF), pltpu.SemaphoreType.DMA((net.size,))],
        compiler_params=params(),
        cost_estimate=cost(1000, 200000),
        name="unpack_vectors",
    )(me, *pieces)


def sum_vectors(net, rows, start, stop):
    if not net.fast:
        return rows if start else lax.psum(rows, AXES)
    for bit in range(start, stop):
        rows = rows + net.pp(rows, lambda c: 1 << bit)
    return rows


class Scatter:
    def __init__(self, net, parts):
        self.net, self.keep, self.got = net, parts[0], []
        self.send = parts[-1]

    def summed(self, lo, hi, cols=slice(None)):
        total = self.keep[lo:hi, :, cols].astype(F32)
        for arr in self.got:
            total = total + arr[lo:hi, :, cols].astype(F32)
        return total

    def core(self):
        if not self.net.fast:
            total = self.keep[0].astype(F32)
            return lax.psum_scatter(total, AXES, scatter_dimension=0, tiled=True)
        return self.net.pp(self.send, other_core)

    def next(self, got, mask, lo):
        self.got.append(got)
        if not self.net.fast:
            return got
        return self.net.pp(self.summed(lo, 2 * lo).astype(BF), mask)

    def b(self, got):
        return self.next(got, second_bit, 2 * self.net.groups)

    def a(self, got):
        return self.next(got, first_bit, self.net.groups)

    def z(self, got, *steps):
        if got is not None:
            self.got.append(got)
        if not self.net.fast:
            return [] if got is None else [got]
        return [
            self.net.pp(self.summed(j, j + 1)[0].astype(BF), lambda c, j=j: j << 3) for j in steps
        ]

    def done(self, last, cols=slice(None)):
        if not self.net.fast:
            return last[0][:, cols]
        total = self.summed(0, 1, cols)[0]
        for arr in last:
            total = total + arr[:, cols].astype(F32)
        return total


def load_list(net, me, pieces, dst, sems, which=0, col=0):
    copies = []
    if not net.fast:
        copies.append(pltpu.make_async_copy(pieces[which], dst, sems.at[0]))
    else:
        masks = piece_masks(me & 1)
        rows, cols = dst.shape[0] // net.size, dst.shape[1]
        for i, piece in enumerate(pieces):
            for j in range(net.groups):
                source = me ^ (masks[i] ^ (j << 3))
                at = pl.multiple_of(source * rows, rows)
                copies.append(
                    pltpu.make_async_copy(
                        piece.at[j, :, pl.ds(col, cols)],
                        dst.at[pl.ds(at, rows), :],
                        sems.at[len(copies)],
                    )
                )
    return copies


def load_start(*args):
    copies = load_list(*args)
    for copy in copies:
        copy.start()
    return copies


def relative(net, rel, core):
    bit_one, bit_two, group = (rel >> 1) & 1, (rel >> 2) & 1, rel >> 3
    top = jnp.where(core == 0, bit_two, bit_one)
    low = jnp.where(core == 0, bit_one, bit_two)
    return (top << (net.high + 1)) | (low << net.high) | group


def store_copies(net, me, src, base, rows, total_rows, outs, col, sems, first_sem):
    cols = pl.ds(col, src.shape[1])
    if not net.fast:
        rows = pl.ds(base, rows)
        return [
            pltpu.make_async_copy(
                src.at[rows, :], outs[0].at[0, rows, cols], sems.at[first_sem]
            )
        ]
    copies = []
    shard = total_rows // net.size
    core = me & 1
    for i in range(0, rows // shard, 2):
        even = base // shard + i
        for k, out in enumerate(outs):
            owner_core = core if k == 0 else 1 - core
            target = even | owner_core
            rel = (me if k == 0 else me ^ 1) ^ target
            at = pl.multiple_of(target * shard, shard)
            copies.append(
                pltpu.make_async_copy(
                    src.at[pl.ds(at, shard), :],
                    out.at[relative(net, rel, owner_core), :, cols],
                    sems.at[first_sem + i + k],
                )
            )
    return copies


def dot(a, b):
    return jnp.dot(a, b, preferred_element_type=F32)


def dot_t(a, b):
    return lax.dot_general(a, b, (((1,), (1,)), ((), ())), preferred_element_type=F32)


def norm_parts(x):
    center = x - jnp.mean(x, axis=1, keepdims=True)
    spread = jnp.mean(center * center, axis=1, keepdims=True)
    rstd = lax.rsqrt(spread + EPSILON)
    return center * rstd, rstd


def sums(x):
    return jnp.sum(x, axis=0, keepdims=True)


def add_to(ref, value, step):
    @pl.when(step == 0)
    def _():
        ref[...] = value

    @pl.when(step > 0)
    def _():
        ref[...] += value


def row_block(tok):
    return min(512, tok)


def weight_scratch(net, *shapes):
    out = []
    for shape in shapes:
        out += [pltpu.VMEM(shape, BF), pltpu.SemaphoreType.DMA((net.shards,))]
    return out


def n_pieces(net, whole=1):
    return 8 if net.fast else whole


def skip_kernel(net, me_ref, frames, skip, *rest):
    np_ = n_pieces(net)
    pieces, (raw_ref, w, sems) = rest[:np_], rest[np_:]

    @pl.when(pl.program_id(0) == 0)
    def _():
        for copy in load_start(net, me_ref[0], pieces, w, sems):
            copy.wait()

    width = frames.shape[1]
    raw_ref[...] = dot(frames[...], w[:width, :]) + dot(skip[...], w[width:, :])


def skip_forward(net, me, frames, skip, pieces):
    tok, width = frames.shape
    blk = row_block(tok)
    rows = pl.BlockSpec((blk, width), lambda i: (i, 0))
    return pl.pallas_call(
        functools.partial(skip_kernel, net),
        grid=(tok // blk,),
        in_specs=[SMEM, rows, rows] + [ANY] * len(pieces),
        out_specs=rows,
        out_shape=jax.ShapeDtypeStruct((tok, width), F32),
        scratch_shapes=weight_scratch(net, (2 * width, width)),
        compiler_params=params(),
        cost_estimate=cost(4 * tok * width * width, tok * width * 8 + 4 * width * width),
        name="skip_forward",
    )(me, frames, skip, *pieces)


def vec_row(vecs, k):
    return vecs[k : k + 1, :]


def qkv_kernel(net, me_ref, raw, vecs, *rest):
    np_ = n_pieces(net)
    pieces, (normed_ref, out_ref, w, sems) = rest[:np_], rest[np_:]

    @pl.when(pl.program_id(0) == 0)
    def _():
        copies = load_start(net, me_ref[0], pieces, w, sems)
        for copy in copies:
            copy.wait()

    xhat, _ = norm_parts(raw[...] + vec_row(vecs, BSKIP))
    normed = (xhat * vec_row(vecs, GAIN1) + vec_row(vecs, SHIFT1)).astype(BF)
    normed_ref[...] = normed
    width = raw.shape[1]
    out_ref[:, :width] = (dot(normed, w[:, :width]) + vec_row(vecs, BQUERY)).astype(BF)
    out_ref[:, width : 2 * width] = dot(normed, w[:, width : 2 * width]).astype(BF)
    out_ref[:, 2 * width :] = (dot(normed, w[:, 2 * width :]) + vec_row(vecs, BVALUE)).astype(BF)


def qkv_forward(net, me, raw, vecs, pieces):
    tok, width = raw.shape
    cols = 3 * width
    blk = row_block(tok)
    return pl.pallas_call(
        functools.partial(qkv_kernel, net),
        grid=(tok // blk,),
        in_specs=[
            SMEM,
            pl.BlockSpec((blk, width), lambda i: (i, 0)),
            pl.BlockSpec((16, width), lambda i: (0, 0)),
        ]
        + [ANY] * len(pieces),
        out_specs=[
            pl.BlockSpec((blk, width), lambda i: (i, 0)),
            pl.BlockSpec((blk, cols), lambda i: (i, 0)),
        ],
        out_shape=[jax.ShapeDtypeStruct((tok, width), BF), jax.ShapeDtypeStruct((tok, cols), BF)],
        scratch_shapes=weight_scratch(net, (width, cols)),
        compiler_params=params(),
        cost_estimate=cost(2 * tok * width * cols, tok * width * 12 + 6 * width * width),
        name="qkv_forward",
    )(me, raw, vecs, *pieces)


def gelu_both(v):
    lead, cubic = 0.7978845608, 0.7978845608 * 0.044715
    square = v * v
    half = 0.5 + 0.5 * jnp.tanh(v * (lead + cubic * square))
    slope = half + (half - half * half) * (v * (2 * lead + (6 * cubic) * square))
    return v * half, slope


def up_kernel(net, me_ref, raw, mixed, vecs, b_up, *rest):
    np_ = n_pieces(net, 2)
    pieces, rest = rest[:np_], rest[np_:]
    second_ref, normed_ref, act_ref, pull_ref, w_out, sems_out, w_up, sems_up = rest

    @pl.when(pl.program_id(0) == 0)
    def _():
        copies = load_start(net, me_ref[0], pieces, w_out, sems_out, 0, 0)
        copies += load_start(net, me_ref[0], pieces, w_up, sems_up, 1, w_out.shape[1])
        for copy in copies:
            copy.wait()

    bias = vec_row(vecs, BSKIP) + vec_row(vecs, BOUT)
    second = raw[...] + dot(mixed[...], w_out[...]) + bias
    second_ref[...] = second
    xhat, _ = norm_parts(second)
    normed = (xhat * vec_row(vecs, GAIN2) + vec_row(vecs, SHIFT2)).astype(BF)
    normed_ref[...] = normed
    chunk = 1024
    for at in range(0, w_up.shape[1], chunk):
        part = slice(at, at + chunk)
        hidden = dot(normed, w_up[:, part]) + b_up[:, part]
        act, pull = gelu_both(hidden)
        act_ref[:, part] = act.astype(BF)
        pull_ref[:, part] = pull.astype(BF)


def up_forward(net, me, raw, mixed, pieces, vecs, b_up):
    tok, width = raw.shape
    ff = b_up.shape[1]
    blk = min(256, tok)
    rows = pl.BlockSpec((blk, width), lambda i: (i, 0))
    wide = pl.BlockSpec((blk, ff), lambda i: (i, 0))
    vec = pl.BlockSpec((16, width), lambda i: (0, 0))
    vec_ff = pl.BlockSpec((1, ff), lambda i: (0, 0))
    return pl.pallas_call(
        functools.partial(up_kernel, net),
        grid=(tok // blk,),
        in_specs=[SMEM, rows, rows, vec, vec_ff] + [ANY] * len(pieces),
        out_specs=[rows, rows, wide, wide],
        out_shape=[
            jax.ShapeDtypeStruct((tok, width), F32),
            jax.ShapeDtypeStruct((tok, width), BF),
            jax.ShapeDtypeStruct((tok, ff), BF),
            jax.ShapeDtypeStruct((tok, ff), BF),
        ],
        scratch_shapes=weight_scratch(net, (width, width), (width, ff)),
        compiler_params=params(),
        cost_estimate=cost(
            2 * tok * width * (width + ff), tok * (width * 12 + ff * 4) + 2 * width * (width + ff)
        ),
        name="up_forward",
    )(me, raw, mixed, vecs, b_up, *pieces)


def down_kernel(net, me_ref, second, act, vecs, *rest):
    pieces, (out_ref, w, sems) = rest[: n_pieces(net)], rest[-3:]

    @pl.when(pl.program_id(0) == 0)
    def _():
        for copy in load_start(net, me_ref[0], pieces, w, sems):
            copy.wait()

    out_ref[...] = (second[...] + dot(act[...], w[...]) + vec_row(vecs, BDOWN)).astype(BF)


def down_forward(net, me, second, act, pieces, vecs, part, parts, before=()):
    tok, width = second.shape
    ff = act.shape[1]
    blk = min(256, tok)
    steps = tok // blk // parts
    start = part * steps
    rows = pl.BlockSpec((blk, width), lambda i: (start + i, 0))
    wide = pl.BlockSpec((blk, ff), lambda i: (start + i, 0))
    vec = pl.BlockSpec((16, width), lambda i: (0, 0))
    return pl.pallas_call(
        functools.partial(down_kernel, net),
        grid=(steps,),
        in_specs=[SMEM, rows, wide, vec] + [ANY] * (len(pieces) + len(before)),
        out_specs=rows,
        out_shape=jax.ShapeDtypeStruct((tok, width), BF),
        input_output_aliases={4 + len(pieces): 0} if before else {},
        scratch_shapes=weight_scratch(net, (ff, width)),
        compiler_params=params(),
        cost_estimate=cost(
            2 * tok * width * ff // parts, tok * (width * 6 + ff * 2) // parts + 2 * width * ff
        ),
        name="down_forward",
    )(me, second, act, vecs, *pieces, *before)


def hidden_kernel(net, me_ref, pull, cot, *rest):
    np_ = n_pieces(net)
    pieces, (gh_ref, bsum_ref, csum_ref, w, sems) = rest[:np_], rest[np_:]
    step = pl.program_id(0)

    @pl.when(step == 0)
    def _():
        for copy in load_start(net, me_ref[0], pieces, w, sems):
            copy.wait()

    chunk = 1024
    for at in range(0, w.shape[0], chunk):
        part = slice(at, at + chunk)
        gh = (dot_t(cot[...], w[part, :]) * pull[:, part].astype(F32)).astype(BF)
        gh_ref[:, part] = gh
        add_to(bsum_ref.at[:, part], sums(gh.astype(F32)), step)
    add_to(csum_ref, sums(cot[...].astype(F32)), step)


def hidden_back(net, me, pull, cot, pieces):
    tok, width = cot.shape
    ff = pull.shape[1]
    blk = row_block(tok)
    rows = pl.BlockSpec((blk, width), lambda i: (i, 0))
    wide = pl.BlockSpec((blk, ff), lambda i: (i, 0))
    vec = pl.BlockSpec((1, width), lambda i: (0, 0))
    vec_ff = pl.BlockSpec((1, ff), lambda i: (0, 0))
    return pl.pallas_call(
        functools.partial(hidden_kernel, net),
        grid=(tok // blk,),
        in_specs=[SMEM, wide, rows] + [ANY] * len(pieces),
        out_specs=[wide, vec_ff, vec],
        out_shape=[
            jax.ShapeDtypeStruct((tok, ff), BF),
            jax.ShapeDtypeStruct((1, ff), F32),
            jax.ShapeDtypeStruct((1, width), F32),
        ],
        scratch_shapes=weight_scratch(net, (ff, width)),
        compiler_params=params(),
        cost_estimate=cost(2 * tok * width * ff, tok * (width * 2 + ff * 4) + 2 * width * ff),
        name="hidden_back",
    )(me, pull, cot, *pieces)


def grad_kernel(net, lefts, rights, blk, col, outs_n, into_n, me_ref, *rest):
    left_refs, right_refs = rest[:lefts], rest[lefts : lefts + rights]
    rest = rest[lefts + rights + into_n :]
    outs, (acc, sems) = rest[:outs_n], rest[outs_n:]
    step = pl.program_id(0)
    total, cols = acc.shape
    steps = total // blk
    per_left = steps // lefts
    per_step = sems.shape[0] // steps
    for s in range(steps):

        @pl.when(step == s)
        def _():
            left = left_refs[s // per_left][...].T
            at = 0
            for right in right_refs:
                chunk = min(1024, right.shape[1])
                for i in range(0, right.shape[1], chunk):
                    acc[s * blk : (s + 1) * blk, at : at + chunk] = dot(
                        left, right[:, i : i + chunk]
                    ).astype(BF)
                    at += chunk
            for copy in store_copies(
                net, me_ref[0], acc, s * blk, blk, total, outs, col, sems, s * per_step
            ):
                copy.start()

    @pl.when(step == steps - 1)
    def _():
        for s in range(steps):
            for copy in store_copies(
                net, me_ref[0], acc, s * blk, blk, total, outs, col, sems, s * per_step
            ):
                copy.wait()


def weight_grad(net, me, lefts, rights, name, into=(), col=0, all_cols=0):
    tok = lefts[0].shape[0]
    cols = sum(right.shape[1] for right in rights)
    each = lefts[0].shape[1]
    total = each * len(lefts)
    blk = min(512, each)
    per_left = each // blk
    steps = total // blk
    all_cols = all_cols or cols
    if net.fast:
        per_step = blk // (total // net.size)
        shapes = [jax.ShapeDtypeStruct((net.size // 2, total // net.size, all_cols), BF)] * 2
    else:
        per_step = 1
        shapes = [jax.ShapeDtypeStruct((1, total, all_cols), BF)]

    def index(k):
        return lambda i: (0, jnp.clip(i - k * per_left, 0, per_left - 1))

    first_into = 1 + len(lefts) + len(rights)
    return pl.pallas_call(
        functools.partial(
            grad_kernel, net, len(lefts), len(rights), blk, col, len(shapes), len(into)
        ),
        grid=(steps,),
        in_specs=[SMEM]
        + [pl.BlockSpec((tok, blk), index(k)) for k in range(len(lefts))]
        + [
            pl.BlockSpec(right.shape, lambda i: (0, 0), pipeline_mode=pl.Buffered(1))
            for right in rights
        ]
        + [ANY] * len(into),
        out_specs=[ANY] * len(shapes),
        out_shape=shapes,
        input_output_aliases={first_into + k: k for k in range(len(into))},
        scratch_shapes=[
            pltpu.VMEM((total, cols), BF),
            pltpu.SemaphoreType.DMA((steps * per_step,)),
        ],
        compiler_params=params(),
        cost_estimate=cost(
            2 * tok * total * cols, 2 * tok * (total + cols) + 2 * total * cols
        ),
        name=name,
    )(me, *lefts, *rights, *into)


def norm_back(dn, x, gain):
    xhat, rstd = norm_parts(x)
    scaled = dn * gain
    mean_one = jnp.mean(scaled, axis=1, keepdims=True)
    mean_two = jnp.mean(scaled * xhat, axis=1, keepdims=True)
    return (scaled - mean_one - xhat * mean_two) * rstd, dn * xhat


def second_kernel(net, blk_w, blk, outs_n, me_ref, gh, normed, mixed, second, cot, vecs, *rest):
    np_ = n_pieces(net, 2)
    pieces, rest = rest[:np_], rest[np_:]
    gsec_ref, gmix_ref, ggain_ref, gshift_ref, gbout_ref = rest[:5]
    outs, rest = rest[5 : 5 + outs_n], rest[5 + outs_n :]
    w_up, sems_up, w_out, sems_out, acc_up, sems_a, acc_out, sems_b, gattn_all = rest
    step = pl.program_id(0)
    me = me_ref[0]
    width, ff = acc_up.shape
    first_steps, mid_steps = width // blk_w, gattn_all.shape[0] // blk
    if net.fast:
        up_outs, out_outs, out_col = outs, outs, ff
    else:
        up_outs, out_outs, out_col = outs[:1], outs[1:], 0
    per_step = sems_a.shape[0] // first_steps

    def stores(acc, targets, col, sems, s):
        return store_copies(net, me, acc, s * blk_w, blk_w, width, targets, col, sems, s * per_step)

    def loads():
        copies = load_list(net, me, pieces, w_up, sems_up, 1, width)
        return copies + load_list(net, me, pieces, w_out, sems_out, 0, 0)

    @pl.when(step == 0)
    def _():
        for copy in loads():
            copy.start()

    for s in range(first_steps):

        @pl.when(step == s)
        def _():
            left = normed[...].T
            for at in range(0, ff, 1024):
                part = slice(at, at + 1024)
                acc_up[s * blk_w : (s + 1) * blk_w, part] = dot(left, gh[:, part]).astype(BF)
            for copy in stores(acc_up, up_outs, 0, sems_a, s):
                copy.start()

    @pl.when(step == first_steps)
    def _():
        for copy in loads():
            copy.wait()

    row = step - first_steps

    @pl.when((row >= 0) & (row < mid_steps))
    def _():
        here = pl.ds(pl.multiple_of(row * blk, blk), blk)
        dn = dot_t(gh[here, :], w_up[...])
        pulled, dx = norm_back(dn, second[...], vec_row(vecs, GAIN2))
        gsec = cot[...].astype(F32) + pulled
        gsec_ref[...] = gsec
        gattn = gsec.astype(BF)
        gattn_all[here, :] = gattn
        gmix_ref[...] = dot_t(gattn, w_out[...]).astype(BF)
        add_to(ggain_ref, sums(dx), row)
        add_to(gshift_ref, sums(dn), row)
        add_to(gbout_ref, sums(gattn.astype(F32)), row)

    for s in range(first_steps):

        @pl.when(row - mid_steps == s)
        def _():
            left = mixed[...].T
            acc_out[s * blk_w : (s + 1) * blk_w, :] = dot(left, gattn_all[...]).astype(BF)
            for copy in stores(acc_out, out_outs, out_col, sems_b, s):
                copy.start()

    @pl.when(row - mid_steps == first_steps - 1)
    def _():
        for s in range(first_steps):
            for copy in stores(acc_up, up_outs, 0, sems_a, s):
                copy.wait()
            for copy in stores(acc_out, out_outs, out_col, sems_b, s):
                copy.wait()


def second_back(net, me, gh, normed, mixed, second, cot, pieces, vecs):
    tok, width = second.shape
    ff = gh.shape[1]
    blk, blk_w = min(256, tok), 512
    first_steps, mid_steps = width // blk_w, tok // blk
    per_step = blk_w // (width // net.size) if net.fast else 1
    if net.fast:
        shard = (net.size // 2, width // net.size, ff + width)
        shapes = [jax.ShapeDtypeStruct(shard, BF)] * 2
    else:
        shapes = [jax.ShapeDtypeStruct((1, width, c), BF) for c in (ff, width)]

    def rows(i):
        return (jnp.clip(i - first_steps, 0, mid_steps - 1), 0)

    def left(start):
        return pl.BlockSpec(
            (tok, blk_w), lambda i: (0, jnp.clip(i - start, 0, first_steps - 1))
        )

    row_spec = pl.BlockSpec((blk, width), rows)
    vec = pl.BlockSpec((1, width), lambda i: (0, 0))
    vec_shape = jax.ShapeDtypeStruct((1, width), F32)
    sems = pltpu.SemaphoreType.DMA((first_steps * per_step,))
    return pl.pallas_call(
        functools.partial(second_kernel, net, blk_w, blk, len(shapes)),
        grid=(2 * first_steps + mid_steps,),
        in_specs=[
            SMEM,
            pl.BlockSpec((tok, ff), lambda i: (0, 0), pipeline_mode=pl.Buffered(1)),
            left(0),
            left(first_steps + mid_steps),
            row_spec,
            row_spec,
            pl.BlockSpec((16, width), lambda i: (0, 0)),
        ]
        + [ANY] * len(pieces),
        out_specs=[row_spec, row_spec, vec, vec, vec] + [ANY] * len(shapes),
        out_shape=[
            jax.ShapeDtypeStruct((tok, width), F32),
            jax.ShapeDtypeStruct((tok, width), BF),
            vec_shape,
            vec_shape,
            vec_shape,
        ]
        + shapes,
        scratch_shapes=weight_scratch(net, (width, ff), (width, width))
        + [
            pltpu.VMEM((width, ff), BF),
            sems,
            pltpu.VMEM((width, width), BF),
            sems,
            pltpu.VMEM((tok, width), BF),
        ],
        compiler_params=params(VMEM_MOST),
        cost_estimate=cost(
            4 * tok * width * (width + ff), tok * (width * 14 + ff * 2) + 4 * width * (width + ff)
        ),
        name="second_back",
    )(me, gh, normed, mixed, second, cot, vecs, *pieces)


def first_kernel(net, me_ref, gq, gk, gv, raw, gsec, vecs, *rest):
    np_ = n_pieces(net)
    pieces, rest = rest[:np_], rest[np_:]
    gfirst_ref, ggain_ref, gshift_ref, gbskip_ref, gbq_ref, gbv_ref, w, sems = rest
    step = pl.program_id(0)

    @pl.when(step == 0)
    def _():
        for copy in load_start(net, me_ref[0], pieces, w, sems):
            copy.wait()

    width = gq.shape[1]
    dn = dot_t(gq[...], w[:, :width])
    dn = dn + dot_t(gk[...], w[:, width : 2 * width])
    dn = dn + dot_t(gv[...], w[:, 2 * width :])
    pulled, dx = norm_back(dn, raw[...] + vec_row(vecs, BSKIP), vec_row(vecs, GAIN1))
    gfirst = (gsec[...] + pulled).astype(BF)
    gfirst_ref[...] = gfirst
    add_to(ggain_ref, sums(dx), step)
    add_to(gshift_ref, sums(dn), step)
    add_to(gbskip_ref, sums(gfirst.astype(F32)), step)
    add_to(gbq_ref, sums(gq[...].astype(F32)), step)
    add_to(gbv_ref, sums(gv[...].astype(F32)), step)


def first_back(net, me, gq, gk, gv, raw, gsec, pieces, vecs):
    tok, width = raw.shape
    blk = min(256, tok)
    rows = pl.BlockSpec((blk, width), lambda i: (i, 0))
    vec = pl.BlockSpec((1, width), lambda i: (0, 0))
    vec_shape = jax.ShapeDtypeStruct((1, width), F32)
    return pl.pallas_call(
        functools.partial(first_kernel, net),
        grid=(tok // blk,),
        in_specs=[SMEM, rows, rows, rows, rows, rows, pl.BlockSpec((16, width), lambda i: (0, 0))]
        + [ANY] * len(pieces),
        out_specs=[rows] + [vec] * 5,
        out_shape=[jax.ShapeDtypeStruct((tok, width), BF)] + [vec_shape] * 5,
        scratch_shapes=weight_scratch(net, (width, 3 * width)),
        compiler_params=params(),
        cost_estimate=cost(6 * tok * width * width, tok * width * 16 + 6 * width * width),
        name="first_back",
    )(me, gq, gk, gv, raw, gsec, vecs, *pieces)


def joined_kernel(net, me_ref, gfirst, *rest):
    np_ = n_pieces(net)
    pieces, (gframes_ref, gskip_ref, w, sems) = rest[:np_], rest[np_:]

    @pl.when(pl.program_id(0) == 0)
    def _():
        for copy in load_start(net, me_ref[0], pieces, w, sems):
            copy.wait()

    width = gframes_ref.shape[1]
    gframes_ref[...] = dot_t(gfirst[...], w[:width, :]).astype(BF)
    gskip_ref[...] = dot_t(gfirst[...], w[width:, :]).astype(BF)


def joined_back(net, me, gfirst, pieces):
    tok, width = gfirst.shape
    blk = row_block(tok)
    rows = pl.BlockSpec((blk, width), lambda i: (i, 0))
    out = jax.ShapeDtypeStruct((tok, width), BF)
    return pl.pallas_call(
        functools.partial(joined_kernel, net),
        grid=(tok // blk,),
        in_specs=[SMEM, rows] + [ANY] * len(pieces),
        out_specs=[rows, rows],
        out_shape=[out, out],
        scratch_shapes=weight_scratch(net, (2 * width, width)),
        compiler_params=params(),
        cost_estimate=cost(4 * tok * width * width, tok * width * 6 + 4 * width * width),
        name="joined_back",
    )(me, gfirst, *pieces)


def far_apart(row_tag, col_tag, row_at):
    shape = (row_tag.shape[0], col_tag.shape[1])
    i = row_at + lax.broadcasted_iota(jnp.int32, shape, 0)
    j = lax.broadcasted_iota(jnp.int32, shape, 1)
    ok = (row_tag == col_tag) | (i == j)
    return jnp.where(ok, jnp.abs(i - j).astype(F32), FAR)


def head_slope(head):
    return jnp.exp2((jnp.full((1, 1), head, jnp.int32).astype(F32) + 1.0) * (-8.0 / HEADS))


def far_kernel(blk, tag_q, tag_k, out_ref):
    out_ref[...] = far_apart(tag_q[...], tag_k[...], pl.program_id(0) * blk)


def far_matrix(row_tag, col_tag):
    tok = row_tag.shape[0]
    blk = min(256, tok)
    return pl.pallas_call(
        functools.partial(far_kernel, blk),
        grid=(tok // blk,),
        in_specs=[pl.BlockSpec((blk, 1), lambda i: (i, 0)), pl.BlockSpec((1, tok), lambda i: (0, 0))],
        out_specs=pl.BlockSpec((blk, tok), lambda i: (i, 0)),
        out_shape=jax.ShapeDtypeStruct((tok, tok), F32),
        compiler_params=params(),
        cost_estimate=cost(8 * tok * tok, 4 * tok * tok),
        name="far_matrix",
    )(row_tag.reshape(tok, 1), col_tag.reshape(1, tok))


def transposed(x):
    return x.astype(F32).T.astype(BF)


def attend_kernel(size, blk, first_pair, q, k, v, far, *rest):
    out_ref, lse_ref, columns = rest[-3:]
    pair = first_pair + pl.program_id(0)
    tok = q.shape[0]
    lane = lax.broadcasted_iota(jnp.int32, (1, 2 * size), 1)

    def score(i, h):
        at = slice(i * blk, (i + 1) * blk)
        mine = (lane >= h * size) & (lane < (h + 1) * size)
        q_h = jnp.where(mine, q[at, :] * size**-0.5, 0)
        scores = dot_t(q_h, k[...]) - head_slope(2 * pair + h) * far[at, :]
        return scores, jnp.max(scores, axis=1, keepdims=True)

    steps = [(i, h) for i in range(tok // blk) for h in range(2)]
    coming = score(*steps[0])
    for n, (i, h) in enumerate(steps):
        scores, top = coming
        if n + 1 < len(steps):
            coming = score(*steps[n + 1])
        expo = jnp.exp(scores - top)
        denom = jnp.sum(expo, axis=1, keepdims=True)
        out, lse = dot(expo.astype(BF), v[...]) / denom, top + jnp.log(denom)
        if h == 0:
            before = out, lse
        else:
            at = slice(i * blk, (i + 1) * blk)
            out_ref[at, :] = jnp.where(lane < size, before[0], out).astype(BF)
            columns[at, :] = jnp.where(lane < size, before[1], lse)
    rows = columns[...].T
    lse_ref[0, 0:1, :] = rows[0:1, :]
    lse_ref[0, 1:2, :] = rows[size : size + 1, :]


def attend(qkv, far, heads, part, parts, before=()):
    tok = qkv.shape[0]
    width = qkv.shape[1] // 3
    size = width // heads
    pairs = heads // 2
    here = pairs // parts
    start = part * here
    blk = min(512, tok)

    def cols(k):
        return pl.BlockSpec((tok, 2 * size), lambda p: (0, k * pairs + start + p))

    return pl.pallas_call(
        functools.partial(attend_kernel, size, blk, start),
        grid=(here,),
        in_specs=[
            cols(0),
            cols(1),
            cols(2),
            pl.BlockSpec((tok, tok), lambda p: (0, 0), pipeline_mode=pl.Buffered(1)),
        ]
        + [ANY] * len(before),
        out_specs=[cols(0), pl.BlockSpec((1, 8, tok), lambda p: (start + p, 0, 0))],
        out_shape=[
            jax.ShapeDtypeStruct((tok, width), BF),
            jax.ShapeDtypeStruct((pairs, 8, tok), F32),
        ],
        input_output_aliases={4 + k: k for k in range(len(before))},
        scratch_shapes=[pltpu.VMEM((tok, 2 * size), F32)],
        compiler_params=params(),
        cost_estimate=cost(
            16 * here * 2 * tok * tok * size, tok * width * 8 // parts, here * 2 * tok * tok
        ),
        name="attend",
    )(qkv, qkv, qkv, far, *before)


def attend_back_kernel(size, blk, first_pair, q, k, v, g, o, lse, far, *rest):
    gq_ref, gk_ref, gv_ref = rest[-3:]
    pair = first_pair + pl.program_id(0)
    tok = q.shape[0]
    lane = lax.broadcasted_iota(jnp.int32, (1, 2 * size), 1)
    scale = size**-0.5
    q_all = q[...] * scale
    g_all = g[...]
    products = (g_all.astype(F32) * o[...].astype(F32)).T
    k_t = transposed(k[...] * scale)
    grads_q = []
    for h in range(2):
        mine = (lane >= h * size) & (lane < (h + 1) * size)
        q_h = jnp.where(mine, q_all, 0)
        g_h = jnp.where(mine, g_all, 0)
        delta = jnp.sum(products[h * size : (h + 1) * size, :], axis=0, keepdims=True)
        norm = lse[0, h : h + 1, :]
        slope = head_slope(2 * pair + h)
        grad_q = jnp.zeros((size, tok), F32)
        for i in range(tok // blk):
            at = slice(i * blk, (i + 1) * blk)
            scores = dot_t(k[at, :], q_h) - slope * far[at, :]
            probs = jnp.exp(scores - norm)
            pulled = dot_t(v[at, :], g_h)
            ds = (probs * (pulled - delta)).astype(BF)
            gv = dot(probs.astype(BF), g_all)
            gk = dot(ds, q_all)
            grad_q = grad_q + dot(k_t[h * size : (h + 1) * size, at], ds)
            if h == 0:
                gv_ref[at, :] = gv.astype(BF)
                gk_ref[at, :] = gk.astype(BF)
            else:
                gv_ref[at, :] = jnp.where(mine, gv.astype(BF), gv_ref[at, :])
                gk_ref[at, :] = jnp.where(mine, gk.astype(BF), gk_ref[at, :])
        grads_q.append(grad_q)
    gq_ref[...] = jnp.concatenate(grads_q, axis=0).T.astype(BF)


def attend_back(qkv, grad_mixed, mixed, lse, far, heads, part, parts, before=()):
    tok = qkv.shape[0]
    width = qkv.shape[1] // 3
    size = width // heads
    pairs = heads // 2
    here = pairs // parts
    start = part * here
    blk = min(512, tok)

    def cols(k):
        return pl.BlockSpec((tok, 2 * size), lambda p: (0, k * pairs + start + p))

    out = jax.ShapeDtypeStruct((tok, width), BF)
    return pl.pallas_call(
        functools.partial(attend_back_kernel, size, blk, start),
        grid=(here,),
        in_specs=[
            cols(0),
            cols(1),
            cols(2),
            cols(0),
            cols(0),
            pl.BlockSpec((1, 8, tok), lambda p: (start + p, 0, 0)),
            pl.BlockSpec((tok, tok), lambda p: (0, 0), pipeline_mode=pl.Buffered(1)),
        ]
        + [ANY] * len(before),
        out_specs=[cols(0)] * 3,
        out_shape=[out] * 3,
        input_output_aliases={7 + k: k for k in range(len(before))},
        compiler_params=params(),
        cost_estimate=cost(
            40 * here * 2 * tok * tok * size, tok * width * 16 // parts, here * 2 * tok * tok
        ),
        name="attend_back",
    )(qkv, qkv, qkv, grad_mixed, mixed, lse, far, *before)


def tags(length_row, mask_row, tok):
    order = jnp.arange(length_row.shape[0])
    ends = jnp.sum(jnp.where(order[:, None] <= order[None, :], length_row[:, None], 0), axis=0)
    slots = jnp.arange(tok, dtype=jnp.int32)
    segment = jnp.sum((slots[:, None] >= ends[None, :]).astype(jnp.int32), axis=1)
    used = slots < jnp.sum(length_row)
    return jnp.where(used, segment, -1), jnp.where(used & (mask_row == 1), segment, -2)


def body(size, frames, skip, lengths, key_mask, cotangent, *weights):
    (
        w_skip, b_skip, pre_attn_gain, pre_attn_bias, w_qkv, b_query, b_value, w_out, b_out,
        pre_ffn_gain, pre_ffn_bias, w_up, b_up, w_down, b_down,
    ) = weights
    tok, width = frames.shape
    net = Net(
        size,
        min(w.shape[0] for w in (w_skip, w_qkv, w_out, w_up, w_down)),
        (b_skip.shape[0], b_up.shape[0]),
    )
    index = lax.axis_index(AXES).astype(jnp.int32)
    me = index.reshape(1)
    narrow = (
        b_skip, pre_attn_gain, pre_attn_bias, b_query, b_value, b_out, pre_ffn_gain, pre_ffn_bias, b_down,
    )

    def stacked(arrays):
        return jnp.stack(arrays) if net.fast else arrays[0]

    flow = Flow(net)
    flow.own("s", w_skip)
    flow.z("s", 1, 2, 3)
    w_two, w_three = w_qkv, [w_out, w_up]
    if net.fast:
        w_two = jnp.concatenate([w_qkv, packed_vectors(narrow, b_up, w_qkv.shape[0])], axis=1)
        w_three = [jnp.concatenate(w_three, axis=1)]
    w_two, w_three, w_down = flow.end((w_two, w_three, w_down), "s")
    flow.own("q", w_two)
    flow.own("u", w_three[-1])
    flow.own("o", w_three[0])
    flow.own("d", w_down)
    flow.near("s")
    flow.z("q", 2)
    tag_q, tag_k = tags(lengths[0], key_mask, tok)
    tag_q, tag_k = flow.end((tag_q, tag_k), "s", "q")
    flow.far("s")
    flow.core("s", 0, 1)
    flow.z("q", 1, 3)
    far_t = far_matrix(tag_k, tag_q)
    frames, far_t, tag_q = flow.end((frames, far_t, tag_q), "s", "q", "u")
    flow.core("s", 2, 3)
    flow.near("q")
    flow.z("u", 2)
    frames = flow.end(frames, "s")
    flow.core("q", 0)
    pieces_s = flow.pieces("s")
    raw = skip_forward(net, me, frames, skip, pieces_s)
    raw, tag_q = flow.end((raw, tag_q), "q", "u")
    flow.far("q")
    flow.core("q", 1, 2)
    flow.z("u", 1, 3)
    far = far_matrix(tag_q, tag_k)
    raw, far = flow.end((raw, far), "q", "u")
    flow.core("q", 3)
    raw = flow.end(raw, "q")
    flow.near("u")
    pieces_q = flow.pieces("q")
    if net.fast:
        vecs, bup = unpack_vectors(net, me, pieces_q, 3 * width)
    else:
        every = [lax.all_gather(v, AXES, axis=0, tiled=True).astype(F32) for v in (*narrow, b_up)]
        vecs, bup = jnp.pad(jnp.stack(every[:-1]), ((0, 16 - len(narrow)), (0, 0))), every[-1][None]
    normed, qkv = qkv_forward(net, me, raw, vecs, pieces_q)
    qkv = flow.end(qkv, "d")
    flow.z("d", 1, 2)
    attended = attend(qkv, far, HEADS, 0, 2)
    attended = flow.end(attended, "u", "d")
    flow.far("u")
    flow.core("u", 0, 1, 2)
    flow.z("d", 3)
    attended = attend(qkv, far, HEADS, 1, 2, attended)
    attended = flow.end(attended, "u", "d")
    flow.core("u", 3)
    attended = flow.end(attended, "u", "d")
    flow.near("d")
    mixed, lse = attended
    pieces_u = ([] if net.fast else flow.pieces("o")) + flow.pieces("u")
    second, normed2, act, pull = up_forward(net, me, raw, mixed, pieces_u, vecs, bup)
    act = flow.end(act, "d")
    flow.far("d")
    flow.core("d", 0, 1, 2)
    down = Scatter(net, weight_grad(net, me, [act], [cotangent], "grad_down"))
    down.keep, down.send = flow.end((down.keep, down.send), "d")
    flow.core("d", 3)
    pieces_d = flow.pieces("d")

    down.keep, down.send, pieces_d = bar(down.keep, down.send, pieces_d)
    down_got = down.core()
    gh, gbup, gbdown = hidden_back(net, me, pull, cotangent, pieces_d)
    gh, down_got = bar(gh, down_got)
    down_got = down.b(down_got)
    gsec, gmixed, ggain2, gshift2, gbout, *up_parts = second_back(
        net, me, gh, normed2, mixed, second, cotangent, pieces_u, vecs
    )
    gmixed, down_got, up_parts = bar(gmixed, down_got, up_parts)
    down_got = down.a(down_got)
    if net.fast:
        up = Scatter(net, up_parts)
    else:
        up, out = Scatter(net, up_parts[:1]), Scatter(net, up_parts[1:])
    gmixed, up.keep, up.send = bar(gmixed, up.keep, up.send)
    up_got = up.core()
    back = (qkv, gmixed, mixed, lse, far_t, HEADS)
    grads = attend_back(*back, 0, 4)
    grads, down_got, up_got = bar(grads, down_got, up_got)
    down_got = down.z(down_got, 1, 2, 3)
    up_got = up.b(up_got)
    grads = attend_back(*back, 1, 4, grads)
    grads = attend_back(*back, 2, 4, grads)
    grads, down_got, up_got = bar(grads, down_got, up_got)
    up_got = up.a(up_got)
    grads = attend_back(*back, 3, 4, grads)
    (gq, gk, gv), up_got = bar(grads, up_got)
    up_got = up.z(up_got, 1, 2)
    gqkv = Scatter(net, weight_grad(net, me, [normed], [gq, gk, gv], "grad_qkv"))
    gq, gqkv.keep, gqkv.send, up_got, up.keep = bar(gq, gqkv.keep, gqkv.send, up_got, up.keep)
    qkv_got = gqkv.core()
    up_got += up.z(None, 3)
    gfirst, ggain1, gshift1, gbskip, gbq, gbv = first_back(
        net, me, gq, gk, gv, raw, gsec, pieces_q, vecs
    )
    gfirst, qkv_got, ggain1, up_got = bar(gfirst, qkv_got, ggain1, up_got)
    qkv_got = gqkv.b(qkv_got)
    rows = [gbskip, ggain1, gshift1, gbq, gbv, gbout, ggain2, gshift2, gbdown, gbup.reshape(-1, width)]
    rows = sum_vectors(net, jnp.concatenate(rows, axis=0), 0, 1)
    gskip_w = Scatter(net, weight_grad(net, me, [frames, skip], [gfirst], "grad_skip"))
    gfirst, gskip_w.keep, gskip_w.send, rows, qkv_got = bar(
        gfirst, gskip_w.keep, gskip_w.send, rows, qkv_got
    )
    qkv_got = gqkv.a(qkv_got)
    skip_got = gskip_w.core()
    rows = sum_vectors(net, rows, 1, 2)
    gframes, gskip = joined_back(net, me, gfirst, pieces_s)
    gframes, qkv_got, skip_got, second, rows = bar(gframes, qkv_got, skip_got, second, rows)
    skip_got = gskip_w.b(skip_got)
    qkv_got = gqkv.z(qkv_got, 1, 2)
    rows = sum_vectors(net, rows, 2, 3)
    layer_out = down_forward(net, me, second, act, pieces_d, vecs, 0, 2)
    layer_out, qkv_got, skip_got, rows, gqkv.keep = bar(layer_out, qkv_got, skip_got, rows, gqkv.keep)
    skip_got = gskip_w.a(skip_got)
    qkv_got += gqkv.z(None, 3)
    rows = sum_vectors(net, rows, 3, 4)
    layer_out = down_forward(net, me, second, act, pieces_d, vecs, 1, 2, [layer_out])
    layer_out, qkv_got, skip_got, rows = bar(layer_out, qkv_got, skip_got, rows)
    skip_got = gskip_w.z(skip_got, 1, 2, 3)
    rows = sum_vectors(net, rows, 4, net.bits)

    def mine(row):
        each = width // size
        return lax.dynamic_slice(rows[row], (index * each,), (each,))

    wide = rows[9:].reshape(-1)
    each = wide.shape[0] // size
    o_bup = lax.dynamic_slice(wide, (index * each,), (each,))
    up_out = up.done(up_got, slice(0, 4 * width) if net.fast else slice(None))
    if net.fast:
        out_out = up.done(up_got, slice(4 * width, 5 * width))
    else:
        out_out = out.core()
    return (
        layer_out,
        gframes,
        gskip,
        gskip_w.done(skip_got),
        mine(0),
        mine(1),
        mine(2),
        gqkv.done(qkv_got),
        mine(3),
        mine(4),
        out_out,
        mine(5),
        mine(6),
        mine(7),
        up_out,
        o_bup,
        down.done(down_got),
        mine(8),
    )


def solution(mesh):
    mat, vec = P(AXES, None), P(AXES)
    size = math.prod(mesh.shape.values())
    return jax.shard_map(
        functools.partial(body, size),
        mesh=mesh,
        in_specs=(
            mat, mat, mat, vec, mat,
            mat, vec, vec, vec, mat, vec, vec, mat, vec, vec, vec, mat, vec, mat, vec,
        ),
        out_specs=(
            mat, mat, mat,
            mat, vec, vec, vec, mat, vec, vec, mat, vec, vec, vec, mat, vec, mat, vec,
        ),
        check_vma=False,
    )
```

```python
import functools
import math

import jax
import jax.numpy as jnp
from jax import lax
from jax.experimental import pallas as pl
from jax.experimental.pallas import tpu as pltpu
from jax.sharding import PartitionSpec as P

HEADS = 16
EPSILON = 1e-05
FAR = 1e32
AXES = ("wide", "narrow")
BF = jnp.bfloat16
F32 = jnp.float32
VMEM_LIMIT = 36 * 1024 * 1024
VMEM_MOST = 58 * 1024 * 1024

ANY = pl.BlockSpec(memory_space=pl.ANY)
SMEM = pl.BlockSpec(memory_space=pltpu.SMEM)


def params(limit=VMEM_LIMIT):
    return pltpu.CompilerParams(vmem_limit_bytes=limit)


def cost(flops, nbytes, trans=0):
    return pl.CostEstimate(flops=int(flops), bytes_accessed=int(nbytes), transcendentals=int(trans))


class Net:
    def __init__(self, size, rows_min, vec_rows):
        self.size = size
        self.bits = size.bit_length() - 1
        self.high = self.bits - 3
        self.groups = 1 << self.high
        self.fast = size == 1 << self.bits and self.bits >= 3 and rows_min % 16 == 0 and vec_rows == (32, 128)
        self.shards = size if self.fast else 1

    def pp(self, x, mask):
        if not self.fast:
            return x
        pairs = [(d, d ^ mask(d & 1)) for d in range(self.size)]
        return lax.ppermute(x, AXES, pairs)


def first_bit(core):
    return 2 + 2 * core


def second_bit(core):
    return 4 - 2 * core


def other_core(core):
    return 1


def piece_masks(core):
    a, b = first_bit(core), second_bit(core)
    return [0, a, b, 6, 1, 1 ^ b, 1 ^ a, 7]


def bar(*values):
    return lax.optimization_barrier(values)


class Flow:
    def __init__(self, net):
        self.net, self.data = net, {}

    def end(self, values, *prefixes):
        names = [n for n in self.data if n.startswith(prefixes)] if prefixes else []
        values, arrays = bar(values, [self.data[n] for n in names])
        self.data.update(zip(names, arrays))
        return values

    def send(self, name, x, mask):
        self.data[name] = self.net.pp(x, mask)

    def own(self, p, shard):
        if self.net.fast:
            self.data[p + "z0"] = shard
        else:
            self.data[p + "m0"] = lax.all_gather(shard, AXES, axis=0, tiled=True)

    def z(self, p, *steps):
        if self.net.fast:
            for j in steps:
                self.send(f"{p}z{j}", self.data[p + "z0"], lambda c, j=j: j << 3)

    def near(self, p):
        if not self.net.fast:
            return
        block = jnp.stack([self.data.pop(f"{p}z{j}") for j in range(self.net.groups)])
        self.data[p + "m0"] = block
        self.send(p + "m1", block, first_bit)
        self.send(p + "m2", block, second_bit)

    def far(self, p):
        if self.net.fast:
            self.send(p + "m3", self.data[p + "m1"], second_bit)

    def core(self, p, *which):
        if self.net.fast:
            for i in which:
                self.send(f"{p}o{i}", self.data[f"{p}m{i}"], other_core)

    def pieces(self, p):
        if not self.net.fast:
            return [self.data.pop(p + "m0")]
        return [self.data.pop(p + k + str(i)) for k in "mo" for i in range(4)]


BSKIP, GAIN1, SHIFT1, BQUERY, BVALUE, BOUT, GAIN2, SHIFT2, BDOWN = range(9)


def packed_vectors(vectors, wide, rows):
    narrow = jnp.pad(jnp.stack(vectors), ((0, 0), (0, 128 - vectors[0].shape[0])))
    return jnp.pad(
        jnp.concatenate([narrow, wide.reshape(1, 128)], axis=0),
        ((0, rows - len(vectors) - 1), (0, 0)),
    )


def unpack_kernel(net, col, me_ref, *rest):
    pieces, (rows_ref, wide_ref, held, sems) = rest[:8], rest[8:]
    me = me_ref[0]
    masks = piece_masks(me & 1)
    copies = []
    for i, piece in enumerate(pieces):
        for j in range(net.groups):
            source = me ^ (masks[i] ^ (j << 3))
            copies.append(
                pltpu.make_async_copy(
                    piece.at[j, pl.ds(0, 16), pl.ds(col, 128)], held.at[source], sems.at[len(copies)]
                )
            )
    for copy in copies:
        copy.start()
    for copy in copies:
        copy.wait()
    for d in range(0, net.size, 4):
        tile = held[d].astype(F32)
        for k in range(1, 4):
            tile = tile + pltpu.roll(held[d + k].astype(F32), 32 * k, 1)
        rows_ref[:, 32 * d : 32 * d + 128] = tile
    for d in range(net.size):
        wide_ref[:, 128 * d : 128 * d + 128] = held[d].astype(F32)[9:10, :]


def unpack_vectors(net, me, pieces, col):
    return pl.pallas_call(
        functools.partial(unpack_kernel, net, col),
        in_specs=[SMEM] + [ANY] * len(pieces),
        out_shape=[
            jax.ShapeDtypeStruct((16, 32 * net.size), F32),
            jax.ShapeDtypeStruct((1, 128 * net.size), F32),
        ],
        scratch_shapes=[pltpu.VMEM((net.size, 16, 128), BF), pltpu.SemaphoreType.DMA((net.size,))],
        compiler_params=params(),
        cost_estimate=cost(1000, 200000),
        name="unpack_vectors",
    )(me, *pieces)


def sum_vectors(net, rows, start, stop):
    if not net.fast:
        return rows if start else lax.psum(rows, AXES)
    for bit in range(start, stop):
        rows = rows + net.pp(rows, lambda c: 1 << bit)
    return rows


class Scatter:
    def __init__(self, net, parts):
        self.net, self.keep, self.got = net, parts[0], []
        self.send = parts[-1]

    def summed(self, lo, hi, cols=slice(None)):
        total = self.keep[lo:hi, :, cols].astype(F32)
        for at, arr in self.got:
            if at <= lo and hi <= at + arr.shape[0]:
                total = total + arr[lo - at : hi - at, :, cols].astype(F32)
        return total

    def take(self, got, at=0):
        if got is not None:
            self.got.append((at, got))

    def core(self):
        if not self.net.fast:
            total = self.keep[0].astype(F32)
            return lax.psum_scatter(total, AXES, scatter_dimension=0, tiled=True)
        return self.net.pp(self.send, other_core)

    def next(self, got, mask, lo, at=0):
        self.take(got, at)
        if not self.net.fast:
            return got
        return self.net.pp(self.summed(lo, 2 * lo).astype(BF), mask)

    def b(self, got):
        return self.next(got, second_bit, 2 * self.net.groups)

    def a(self, got, at=0):
        return self.next(got, first_bit, self.net.groups, at)

    def z(self, got, *steps):
        self.take(got)
        if not self.net.fast:
            return [] if got is None else [got]
        return [
            self.net.pp(self.summed(j, j + 1)[0].astype(BF), lambda c, j=j: j << 3) for j in steps
        ]

    def done(self, last, cols=slice(None)):
        if not self.net.fast:
            return last[0][:, cols]
        total = self.summed(0, 1, cols)[0]
        for arr in last:
            total = total + arr[:, cols].astype(F32)
        return total


def load_list(net, me, pieces, dst, sems, which=0, col=0):
    copies = []
    if not net.fast:
        copies.append(pltpu.make_async_copy(pieces[which], dst, sems.at[0]))
    else:
        masks = piece_masks(me & 1)
        rows, cols = dst.shape[0] // net.size, dst.shape[1]
        for i, piece in enumerate(pieces):
            for j in range(net.groups):
                source = me ^ (masks[i] ^ (j << 3))
                at = pl.multiple_of(source * rows, rows)
                copies.append(
                    pltpu.make_async_copy(
                        piece.at[j, :, pl.ds(col, cols)],
                        dst.at[pl.ds(at, rows), :],
                        sems.at[len(copies)],
                    )
                )
    return copies


def load_start(*args):
    copies = load_list(*args)
    for copy in copies:
        copy.start()
    return copies


def relative(net, rel, core):
    bit_one, bit_two, group = (rel >> 1) & 1, (rel >> 2) & 1, rel >> 3
    top = jnp.where(core == 0, bit_two, bit_one)
    low = jnp.where(core == 0, bit_one, bit_two)
    return (top << (net.high + 1)) | (low << net.high) | group


def store_copies(net, me, src, base, rows, total_rows, outs, col, sems, first_sem):
    cols = pl.ds(col, src.shape[1])
    if not net.fast:
        rows = pl.ds(base, rows)
        return [
            pltpu.make_async_copy(
                src.at[rows, :], outs[0].at[0, rows, cols], sems.at[first_sem]
            )
        ]
    copies = []
    shard = total_rows // net.size
    core = me & 1
    for i in range(0, rows // shard, 2):
        even = base // shard + i
        for k, out in enumerate(outs):
            owner_core = core if k == 0 else 1 - core
            target = even | owner_core
            rel = (me if k == 0 else me ^ 1) ^ target
            at = pl.multiple_of(target * shard, shard)
            copies.append(
                pltpu.make_async_copy(
                    src.at[pl.ds(at, shard), :],
                    out.at[relative(net, rel, owner_core), :, cols],
                    sems.at[first_sem + i + k],
                )
            )
    return copies


def dot(a, b):
    return jnp.dot(a, b, preferred_element_type=F32)


def dot_t(a, b):
    return lax.dot_general(a, b, (((1,), (1,)), ((), ())), preferred_element_type=F32)


def norm_parts(x):
    center = x - jnp.mean(x, axis=1, keepdims=True)
    spread = jnp.mean(center * center, axis=1, keepdims=True)
    rstd = lax.rsqrt(spread + EPSILON)
    return center * rstd, rstd


def sums(x):
    return jnp.sum(x, axis=0, keepdims=True)


def add_to(ref, value, step):
    @pl.when(step == 0)
    def _():
        ref[...] = value

    @pl.when(step > 0)
    def _():
        ref[...] += value


def row_block(tok):
    return min(512, tok)


def weight_scratch(net, *shapes):
    out = []
    for shape in shapes:
        out += [pltpu.VMEM(shape, BF), pltpu.SemaphoreType.DMA((net.shards,))]
    return out


def n_pieces(net, whole=1):
    return 8 if net.fast else whole


def skip_kernel(net, me_ref, frames, skip, *rest):
    np_ = n_pieces(net)
    pieces, (raw_ref, w, sems) = rest[:np_], rest[np_:]

    @pl.when(pl.program_id(0) == 0)
    def _():
        for copy in load_start(net, me_ref[0], pieces, w, sems):
            copy.wait()

    width = frames.shape[1]
    raw_ref[...] = dot(frames[...], w[:width, :]) + dot(skip[...], w[width:, :])


def skip_forward(net, me, frames, skip, pieces):
    tok, width = frames.shape
    blk = row_block(tok)
    rows = pl.BlockSpec((blk, width), lambda i: (i, 0))
    return pl.pallas_call(
        functools.partial(skip_kernel, net),
        grid=(tok // blk,),
        in_specs=[SMEM, rows, rows] + [ANY] * len(pieces),
        out_specs=rows,
        out_shape=jax.ShapeDtypeStruct((tok, width), F32),
        scratch_shapes=weight_scratch(net, (2 * width, width)),
        compiler_params=params(),
        cost_estimate=cost(4 * tok * width * width, tok * width * 8 + 4 * width * width),
        name="skip_forward",
    )(me, frames, skip, *pieces)


def vec_row(vecs, k):
    return vecs[k : k + 1, :]


def qkv_kernel(net, me_ref, raw, vecs, *rest):
    np_ = n_pieces(net)
    pieces, (normed_ref, out_ref, w, sems) = rest[:np_], rest[np_:]

    @pl.when(pl.program_id(0) == 0)
    def _():
        copies = load_start(net, me_ref[0], pieces, w, sems)
        for copy in copies:
            copy.wait()

    xhat, _ = norm_parts(raw[...] + vec_row(vecs, BSKIP))
    normed = (xhat * vec_row(vecs, GAIN1) + vec_row(vecs, SHIFT1)).astype(BF)
    normed_ref[...] = normed
    width = raw.shape[1]
    out_ref[:, :width] = (dot(normed, w[:, :width]) + vec_row(vecs, BQUERY)).astype(BF)
    out_ref[:, width : 2 * width] = dot(normed, w[:, width : 2 * width]).astype(BF)
    out_ref[:, 2 * width :] = (dot(normed, w[:, 2 * width :]) + vec_row(vecs, BVALUE)).astype(BF)


def qkv_forward(net, me, raw, vecs, pieces):
    tok, width = raw.shape
    cols = 3 * width
    blk = row_block(tok)
    return pl.pallas_call(
        functools.partial(qkv_kernel, net),
        grid=(tok // blk,),
        in_specs=[
            SMEM,
            pl.BlockSpec((blk, width), lambda i: (i, 0)),
            pl.BlockSpec((16, width), lambda i: (0, 0)),
        ]
        + [ANY] * len(pieces),
        out_specs=[
            pl.BlockSpec((blk, width), lambda i: (i, 0)),
            pl.BlockSpec((blk, cols), lambda i: (i, 0)),
        ],
        out_shape=[jax.ShapeDtypeStruct((tok, width), BF), jax.ShapeDtypeStruct((tok, cols), BF)],
        scratch_shapes=weight_scratch(net, (width, cols)),
        compiler_params=params(),
        cost_estimate=cost(2 * tok * width * cols, tok * width * 12 + 6 * width * width),
        name="qkv_forward",
    )(me, raw, vecs, *pieces)


def gelu_both(v):
    lead, cubic = 0.7978845608, 0.7978845608 * 0.044715
    square = v * v
    half = 0.5 + 0.5 * jnp.tanh(v * (lead + cubic * square))
    slope = half + (half - half * half) * (v * (2 * lead + (6 * cubic) * square))
    return v * half, slope


def up_kernel(net, me_ref, raw, mixed, vecs, b_up, *rest):
    np_ = n_pieces(net, 2)
    pieces, rest = rest[:np_], rest[np_:]
    second_ref, normed_ref, act_ref, pull_ref, w_out, sems_out, w_up, sems_up = rest

    @pl.when(pl.program_id(0) == 0)
    def _():
        copies = load_start(net, me_ref[0], pieces, w_out, sems_out, 0, 0)
        copies += load_start(net, me_ref[0], pieces, w_up, sems_up, 1, w_out.shape[1])
        for copy in copies:
            copy.wait()

    bias = vec_row(vecs, BSKIP) + vec_row(vecs, BOUT)
    second = raw[...] + dot(mixed[...], w_out[...]) + bias
    second_ref[...] = second
    xhat, _ = norm_parts(second)
    normed = (xhat * vec_row(vecs, GAIN2) + vec_row(vecs, SHIFT2)).astype(BF)
    normed_ref[...] = normed
    chunk = 1024
    for at in range(0, w_up.shape[1], chunk):
        part = slice(at, at + chunk)
        hidden = dot(normed, w_up[:, part]) + b_up[:, part]
        act, pull = gelu_both(hidden)
        act_ref[:, part] = act.astype(BF)
        pull_ref[:, part] = pull.astype(BF)


def up_forward(net, me, raw, mixed, pieces, vecs, b_up):
    tok, width = raw.shape
    ff = b_up.shape[1]
    blk = min(256, tok)
    rows = pl.BlockSpec((blk, width), lambda i: (i, 0))
    wide = pl.BlockSpec((blk, ff), lambda i: (i, 0))
    vec = pl.BlockSpec((16, width), lambda i: (0, 0))
    vec_ff = pl.BlockSpec((1, ff), lambda i: (0, 0))
    return pl.pallas_call(
        functools.partial(up_kernel, net),
        grid=(tok // blk,),
        in_specs=[SMEM, rows, rows, vec, vec_ff] + [ANY] * len(pieces),
        out_specs=[rows, rows, wide, wide],
        out_shape=[
            jax.ShapeDtypeStruct((tok, width), F32),
            jax.ShapeDtypeStruct((tok, width), BF),
            jax.ShapeDtypeStruct((tok, ff), BF),
            jax.ShapeDtypeStruct((tok, ff), BF),
        ],
        scratch_shapes=weight_scratch(net, (width, width), (width, ff)),
        compiler_params=params(),
        cost_estimate=cost(
            2 * tok * width * (width + ff), tok * (width * 12 + ff * 4) + 2 * width * (width + ff)
        ),
        name="up_forward",
    )(me, raw, mixed, vecs, b_up, *pieces)


def down_kernel(net, me_ref, second, act, vecs, *rest):
    pieces, (out_ref, w, sems) = rest[: n_pieces(net)], rest[-3:]

    @pl.when(pl.program_id(0) == 0)
    def _():
        for copy in load_start(net, me_ref[0], pieces, w, sems):
            copy.wait()

    out_ref[...] = (second[...] + dot(act[...], w[...]) + vec_row(vecs, BDOWN)).astype(BF)


def down_forward(net, me, second, act, pieces, vecs, part, parts, before=()):
    tok, width = second.shape
    ff = act.shape[1]
    blk = min(256, tok)
    steps = tok // blk // parts
    start = part * steps
    rows = pl.BlockSpec((blk, width), lambda i: (start + i, 0))
    wide = pl.BlockSpec((blk, ff), lambda i: (start + i, 0))
    vec = pl.BlockSpec((16, width), lambda i: (0, 0))
    return pl.pallas_call(
        functools.partial(down_kernel, net),
        grid=(steps,),
        in_specs=[SMEM, rows, wide, vec] + [ANY] * (len(pieces) + len(before)),
        out_specs=rows,
        out_shape=jax.ShapeDtypeStruct((tok, width), BF),
        input_output_aliases={4 + len(pieces): 0} if before else {},
        scratch_shapes=weight_scratch(net, (ff, width)),
        compiler_params=params(),
        cost_estimate=cost(
            2 * tok * width * ff // parts, tok * (width * 6 + ff * 2) // parts + 2 * width * ff
        ),
        name="down_forward",
    )(me, second, act, vecs, *pieces, *before)


def hidden_kernel(net, me_ref, pull, cot, *rest):
    np_ = n_pieces(net)
    pieces, (gh_ref, bsum_ref, csum_ref, w, sems) = rest[:np_], rest[np_:]
    step = pl.program_id(0)

    @pl.when(step == 0)
    def _():
        for copy in load_start(net, me_ref[0], pieces, w, sems):
            copy.wait()

    chunk = 1024
    for at in range(0, w.shape[0], chunk):
        part = slice(at, at + chunk)
        gh = (dot_t(cot[...], w[part, :]) * pull[:, part].astype(F32)).astype(BF)
        gh_ref[:, part] = gh
        add_to(bsum_ref.at[:, part], sums(gh.astype(F32)), step)
    add_to(csum_ref, sums(cot[...].astype(F32)), step)


def hidden_back(net, me, pull, cot, pieces):
    tok, width = cot.shape
    ff = pull.shape[1]
    blk = row_block(tok)
    rows = pl.BlockSpec((blk, width), lambda i: (i, 0))
    wide = pl.BlockSpec((blk, ff), lambda i: (i, 0))
    vec = pl.BlockSpec((1, width), lambda i: (0, 0))
    vec_ff = pl.BlockSpec((1, ff), lambda i: (0, 0))
    return pl.pallas_call(
        functools.partial(hidden_kernel, net),
        grid=(tok // blk,),
        in_specs=[SMEM, wide, rows] + [ANY] * len(pieces),
        out_specs=[wide, vec_ff, vec],
        out_shape=[
            jax.ShapeDtypeStruct((tok, ff), BF),
            jax.ShapeDtypeStruct((1, ff), F32),
            jax.ShapeDtypeStruct((1, width), F32),
        ],
        scratch_shapes=weight_scratch(net, (ff, width)),
        compiler_params=params(),
        cost_estimate=cost(2 * tok * width * ff, tok * (width * 2 + ff * 4) + 2 * width * ff),
        name="hidden_back",
    )(me, pull, cot, *pieces)


def grad_kernel(net, lefts, rights, blk, col, outs_n, into_n, me_ref, *rest):
    left_refs, right_refs = rest[:lefts], rest[lefts : lefts + rights]
    rest = rest[lefts + rights + into_n :]
    outs, (acc, sems) = rest[:outs_n], rest[outs_n:]
    step = pl.program_id(0)
    total, cols = acc.shape
    steps = total // blk
    per_left = steps // lefts
    per_step = sems.shape[0] // steps
    for s in range(steps):

        @pl.when(step == s)
        def _():
            left = left_refs[s // per_left][...].T
            at = 0
            for right in right_refs:
                chunk = min(1024, right.shape[1])
                for i in range(0, right.shape[1], chunk):
                    acc[s * blk : (s + 1) * blk, at : at + chunk] = dot(
                        left, right[:, i : i + chunk]
                    ).astype(BF)
                    at += chunk
            for copy in store_copies(
                net, me_ref[0], acc, s * blk, blk, total, outs, col, sems, s * per_step
            ):
                copy.start()

    @pl.when(step == steps - 1)
    def _():
        for s in range(steps):
            for copy in store_copies(
                net, me_ref[0], acc, s * blk, blk, total, outs, col, sems, s * per_step
            ):
                copy.wait()


def weight_grad(net, me, lefts, rights, name, into=(), col=0, all_cols=0, most=False):
    tok = lefts[0].shape[0]
    cols = sum(right.shape[1] for right in rights)
    each = lefts[0].shape[1]
    total = each * len(lefts)
    blk = min(512, each)
    per_left = each // blk
    steps = total // blk
    all_cols = all_cols or cols
    if net.fast:
        per_step = blk // (total // net.size)
        shapes = [jax.ShapeDtypeStruct((net.size // 2, total // net.size, all_cols), BF)] * 2
    else:
        per_step = 1
        shapes = [jax.ShapeDtypeStruct((1, total, all_cols), BF)]

    def index(k):
        return lambda i: (0, jnp.clip(i - k * per_left, 0, per_left - 1))

    first_into = 1 + len(lefts) + len(rights)
    return pl.pallas_call(
        functools.partial(
            grad_kernel, net, len(lefts), len(rights), blk, col, len(shapes), len(into)
        ),
        grid=(steps,),
        in_specs=[SMEM]
        + [pl.BlockSpec((tok, blk), index(k)) for k in range(len(lefts))]
        + [
            pl.BlockSpec(right.shape, lambda i: (0, 0), pipeline_mode=pl.Buffered(1))
            for right in rights
        ]
        + [ANY] * len(into),
        out_specs=[ANY] * len(shapes),
        out_shape=shapes,
        input_output_aliases={first_into + k: k for k in range(len(into))},
        scratch_shapes=[
            pltpu.VMEM((total, cols), BF),
            pltpu.SemaphoreType.DMA((steps * per_step,)),
        ],
        compiler_params=params(VMEM_MOST if most else VMEM_LIMIT),
        cost_estimate=cost(
            2 * tok * total * cols, 2 * tok * (total + cols) + 2 * total * cols
        ),
        name=name,
    )(me, *lefts, *rights, *into)


def norm_back(dn, x, gain):
    xhat, rstd = norm_parts(x)
    scaled = dn * gain
    mean_one = jnp.mean(scaled, axis=1, keepdims=True)
    mean_two = jnp.mean(scaled * xhat, axis=1, keepdims=True)
    return (scaled - mean_one - xhat * mean_two) * rstd, dn * xhat


def second_kernel(net, blk_w, blk, outs_n, me_ref, gh, normed, mixed, second, cot, vecs, *rest):
    np_ = n_pieces(net, 2)
    pieces, rest = rest[:np_], rest[np_:]
    gsec_ref, gmix_ref, ggain_ref, gshift_ref, gbout_ref = rest[:5]
    outs, rest = rest[5 : 5 + outs_n], rest[5 + outs_n :]
    w_up, sems_up, w_out, sems_out, acc_up, sems_a, acc_out, sems_b, gattn_all = rest
    step = pl.program_id(0)
    me = me_ref[0]
    width, ff = acc_up.shape
    first_steps, mid_steps = width // blk_w, gattn_all.shape[0] // blk
    if net.fast:
        up_outs, out_outs, out_col = outs, outs, ff
    else:
        up_outs, out_outs, out_col = outs[:1], outs[1:], 0
    per_step = sems_a.shape[0] // first_steps

    def stores(acc, targets, col, sems, s):
        return store_copies(net, me, acc, s * blk_w, blk_w, width, targets, col, sems, s * per_step)

    def loads():
        copies = load_list(net, me, pieces, w_up, sems_up, 1, width)
        return copies + load_list(net, me, pieces, w_out, sems_out, 0, 0)

    @pl.when(step == 0)
    def _():
        for copy in loads():
            copy.start()

    for s in range(first_steps):

        @pl.when(step == s)
        def _():
            left = normed[...].T
            for at in range(0, ff, 1024):
                part = slice(at, at + 1024)
                acc_up[s * blk_w : (s + 1) * blk_w, part] = dot(left, gh[:, part]).astype(BF)
            for copy in stores(acc_up, up_outs, 0, sems_a, s):
                copy.start()

    @pl.when(step == first_steps)
    def _():
        for copy in loads():
            copy.wait()

    row = step - first_steps

    @pl.when((row >= 0) & (row < mid_steps))
    def _():
        here = pl.ds(pl.multiple_of(row * blk, blk), blk)
        dn = dot_t(gh[here, :], w_up[...])
        pulled, dx = norm_back(dn, second[...], vec_row(vecs, GAIN2))
        gsec = cot[...].astype(F32) + pulled
        gsec_ref[...] = gsec
        gattn = gsec.astype(BF)
        gattn_all[here, :] = gattn
        gmix_ref[...] = dot_t(gattn, w_out[...]).astype(BF)
        add_to(ggain_ref, sums(dx), row)
        add_to(gshift_ref, sums(dn), row)
        add_to(gbout_ref, sums(gattn.astype(F32)), row)

    for s in range(first_steps):

        @pl.when(row - mid_steps == s)
        def _():
            left = mixed[...].T
            acc_out[s * blk_w : (s + 1) * blk_w, :] = dot(left, gattn_all[...]).astype(BF)
            for copy in stores(acc_out, out_outs, out_col, sems_b, s):
                copy.start()

    @pl.when(row - mid_steps == first_steps - 1)
    def _():
        for s in range(first_steps):
            for copy in stores(acc_up, up_outs, 0, sems_a, s):
                copy.wait()
            for copy in stores(acc_out, out_outs, out_col, sems_b, s):
                copy.wait()


def second_back(net, me, gh, normed, mixed, second, cot, pieces, vecs):
    tok, width = second.shape
    ff = gh.shape[1]
    blk, blk_w = min(256, tok), 512
    first_steps, mid_steps = width // blk_w, tok // blk
    per_step = blk_w // (width // net.size) if net.fast else 1
    if net.fast:
        shard = (net.size // 2, width // net.size, ff + width)
        shapes = [jax.ShapeDtypeStruct(shard, BF)] * 2
    else:
        shapes = [jax.ShapeDtypeStruct((1, width, c), BF) for c in (ff, width)]

    def rows(i):
        return (jnp.clip(i - first_steps, 0, mid_steps - 1), 0)

    def left(start):
        return pl.BlockSpec(
            (tok, blk_w), lambda i: (0, jnp.clip(i - start, 0, first_steps - 1))
        )

    row_spec = pl.BlockSpec((blk, width), rows)
    vec = pl.BlockSpec((1, width), lambda i: (0, 0))
    vec_shape = jax.ShapeDtypeStruct((1, width), F32)
    sems = pltpu.SemaphoreType.DMA((first_steps * per_step,))
    return pl.pallas_call(
        functools.partial(second_kernel, net, blk_w, blk, len(shapes)),
        grid=(2 * first_steps + mid_steps,),
        in_specs=[
            SMEM,
            pl.BlockSpec((tok, ff), lambda i: (0, 0), pipeline_mode=pl.Buffered(1)),
            left(0),
            left(first_steps + mid_steps),
            row_spec,
            row_spec,
            pl.BlockSpec((16, width), lambda i: (0, 0)),
        ]
        + [ANY] * len(pieces),
        out_specs=[row_spec, row_spec, vec, vec, vec] + [ANY] * len(shapes),
        out_shape=[
            jax.ShapeDtypeStruct((tok, width), F32),
            jax.ShapeDtypeStruct((tok, width), BF),
            vec_shape,
            vec_shape,
            vec_shape,
        ]
        + shapes,
        scratch_shapes=weight_scratch(net, (width, ff), (width, width))
        + [
            pltpu.VMEM((width, ff), BF),
            sems,
            pltpu.VMEM((width, width), BF),
            sems,
            pltpu.VMEM((tok, width), BF),
        ],
        compiler_params=params(VMEM_MOST),
        cost_estimate=cost(
            4 * tok * width * (width + ff), tok * (width * 14 + ff * 2) + 4 * width * (width + ff)
        ),
        name="second_back",
    )(me, gh, normed, mixed, second, cot, vecs, *pieces)


def first_kernel(net, me_ref, gq, gk, gv, raw, gsec, vecs, *rest):
    np_ = n_pieces(net)
    pieces, rest = rest[:np_], rest[np_:]
    gfirst_ref, ggain_ref, gshift_ref, gbskip_ref, gbq_ref, gbv_ref, w, sems = rest
    step = pl.program_id(0)

    @pl.when(step == 0)
    def _():
        for copy in load_start(net, me_ref[0], pieces, w, sems):
            copy.wait()

    width = gq.shape[1]
    dn = dot_t(gq[...], w[:, :width])
    dn = dn + dot_t(gk[...], w[:, width : 2 * width])
    dn = dn + dot_t(gv[...], w[:, 2 * width :])
    pulled, dx = norm_back(dn, raw[...] + vec_row(vecs, BSKIP), vec_row(vecs, GAIN1))
    gfirst = (gsec[...] + pulled).astype(BF)
    gfirst_ref[...] = gfirst
    add_to(ggain_ref, sums(dx), step)
    add_to(gshift_ref, sums(dn), step)
    add_to(gbskip_ref, sums(gfirst.astype(F32)), step)
    add_to(gbq_ref, sums(gq[...].astype(F32)), step)
    add_to(gbv_ref, sums(gv[...].astype(F32)), step)


def first_back(net, me, gq, gk, gv, raw, gsec, pieces, vecs):
    tok, width = raw.shape
    blk = row_block(tok)
    rows = pl.BlockSpec((blk, width), lambda i: (i, 0))
    vec = pl.BlockSpec((1, width), lambda i: (0, 0))
    vec_shape = jax.ShapeDtypeStruct((1, width), F32)
    return pl.pallas_call(
        functools.partial(first_kernel, net),
        grid=(tok // blk,),
        in_specs=[SMEM, rows, rows, rows, rows, rows, pl.BlockSpec((16, width), lambda i: (0, 0))]
        + [ANY] * len(pieces),
        out_specs=[rows] + [vec] * 5,
        out_shape=[jax.ShapeDtypeStruct((tok, width), BF)] + [vec_shape] * 5,
        scratch_shapes=weight_scratch(net, (width, 3 * width)),
        compiler_params=params(VMEM_MOST),
        cost_estimate=cost(6 * tok * width * width, tok * width * 16 + 6 * width * width),
        name="first_back",
    )(me, gq, gk, gv, raw, gsec, vecs, *pieces)


def joined_kernel(net, me_ref, gfirst, *rest):
    np_ = n_pieces(net)
    pieces, (gframes_ref, gskip_ref, w, sems) = rest[:np_], rest[np_:]

    @pl.when(pl.program_id(0) == 0)
    def _():
        for copy in load_start(net, me_ref[0], pieces, w, sems):
            copy.wait()

    width = gframes_ref.shape[1]
    gframes_ref[...] = dot_t(gfirst[...], w[:width, :]).astype(BF)
    gskip_ref[...] = dot_t(gfirst[...], w[width:, :]).astype(BF)


def joined_back(net, me, gfirst, pieces):
    tok, width = gfirst.shape
    blk = row_block(tok)
    rows = pl.BlockSpec((blk, width), lambda i: (i, 0))
    out = jax.ShapeDtypeStruct((tok, width), BF)
    return pl.pallas_call(
        functools.partial(joined_kernel, net),
        grid=(tok // blk,),
        in_specs=[SMEM, rows] + [ANY] * len(pieces),
        out_specs=[rows, rows],
        out_shape=[out, out],
        scratch_shapes=weight_scratch(net, (2 * width, width)),
        compiler_params=params(),
        cost_estimate=cost(4 * tok * width * width, tok * width * 6 + 4 * width * width),
        name="joined_back",
    )(me, gfirst, *pieces)


def far_apart(row_tag, col_tag, row_at):
    shape = (row_tag.shape[0], col_tag.shape[1])
    i = row_at + lax.broadcasted_iota(jnp.int32, shape, 0)
    j = lax.broadcasted_iota(jnp.int32, shape, 1)
    ok = (row_tag == col_tag) | (i == j)
    return jnp.where(ok, jnp.abs(i - j).astype(F32), FAR)


def head_slope(head):
    return jnp.exp2((jnp.full((1, 1), head, jnp.int32).astype(F32) + 1.0) * (-8.0 / HEADS))


def far_kernel(blk, tag_q, tag_k, out_ref):
    out_ref[...] = far_apart(tag_q[...], tag_k[...], pl.program_id(0) * blk)


def far_matrix(row_tag, col_tag):
    tok = row_tag.shape[0]
    blk = min(256, tok)
    return pl.pallas_call(
        functools.partial(far_kernel, blk),
        grid=(tok // blk,),
        in_specs=[pl.BlockSpec((blk, 1), lambda i: (i, 0)), pl.BlockSpec((1, tok), lambda i: (0, 0))],
        out_specs=pl.BlockSpec((blk, tok), lambda i: (i, 0)),
        out_shape=jax.ShapeDtypeStruct((tok, tok), F32),
        compiler_params=params(),
        cost_estimate=cost(8 * tok * tok, 4 * tok * tok),
        name="far_matrix",
    )(row_tag.reshape(tok, 1), col_tag.reshape(1, tok))


def transposed(x):
    return x.astype(F32).T.astype(BF)


def attend_kernel(size, blk, first_pair, q, k, v, far, *rest):
    out_ref, lse_ref, columns = rest[-3:]
    pair = first_pair + pl.program_id(0)
    tok = q.shape[0]
    lane = lax.broadcasted_iota(jnp.int32, (1, 2 * size), 1)

    def score(i, h):
        at = slice(i * blk, (i + 1) * blk)
        mine = (lane >= h * size) & (lane < (h + 1) * size)
        q_h = jnp.where(mine, q[at, :] * size**-0.5, 0)
        scores = dot_t(q_h, k[...]) - head_slope(2 * pair + h) * far[at, :]
        return scores, jnp.max(scores, axis=1, keepdims=True)

    steps = [(i, h) for i in range(tok // blk) for h in range(2)]
    coming = score(*steps[0])
    for n, (i, h) in enumerate(steps):
        scores, top = coming
        if n + 1 < len(steps):
            coming = score(*steps[n + 1])
        expo = jnp.exp(scores - top)
        denom = jnp.sum(expo, axis=1, keepdims=True)
        out, lse = dot(expo.astype(BF), v[...]) / denom, top + jnp.log(denom)
        if h == 0:
            before = out, lse
        else:
            at = slice(i * blk, (i + 1) * blk)
            out_ref[at, :] = jnp.where(lane < size, before[0], out).astype(BF)
            columns[at, :] = jnp.where(lane < size, before[1], lse)
    rows = columns[...].T
    lse_ref[0, 0:1, :] = rows[0:1, :]
    lse_ref[0, 1:2, :] = rows[size : size + 1, :]


def attend(qkv, far, heads, part, parts, before=()):
    tok = qkv.shape[0]
    width = qkv.shape[1] // 3
    size = width // heads
    pairs = heads // 2
    here = pairs // parts
    start = part * here
    blk = min(512, tok)

    def cols(k):
        return pl.BlockSpec((tok, 2 * size), lambda p: (0, k * pairs + start + p))

    return pl.pallas_call(
        functools.partial(attend_kernel, size, blk, start),
        grid=(here,),
        in_specs=[
            cols(0),
            cols(1),
            cols(2),
            pl.BlockSpec((tok, tok), lambda p: (0, 0), pipeline_mode=pl.Buffered(1)),
        ]
        + [ANY] * len(before),
        out_specs=[cols(0), pl.BlockSpec((1, 8, tok), lambda p: (start + p, 0, 0))],
        out_shape=[
            jax.ShapeDtypeStruct((tok, width), BF),
            jax.ShapeDtypeStruct((pairs, 8, tok), F32),
        ],
        input_output_aliases={4 + k: k for k in range(len(before))},
        scratch_shapes=[pltpu.VMEM((tok, 2 * size), F32)],
        compiler_params=params(),
        cost_estimate=cost(
            16 * here * 2 * tok * tok * size, tok * width * 8 // parts, here * 2 * tok * tok
        ),
        name="attend",
    )(qkv, qkv, qkv, far, *before)


def attend_back_kernel(size, blk, first_pair, q, k, v, g, o, lse, far, *rest):
    gq_ref, gk_ref, gv_ref = rest[-3:]
    pair = first_pair + pl.program_id(0)
    tok = q.shape[0]
    lane = lax.broadcasted_iota(jnp.int32, (1, 2 * size), 1)
    scale = size**-0.5
    q_all = q[...] * scale
    g_all = g[...]
    products = (g_all.astype(F32) * o[...].astype(F32)).T
    k_t = transposed(k[...] * scale)
    grads_q = []
    for h in range(2):
        mine = (lane >= h * size) & (lane < (h + 1) * size)
        q_h = jnp.where(mine, q_all, 0)
        g_h = jnp.where(mine, g_all, 0)
        delta = jnp.sum(products[h * size : (h + 1) * size, :], axis=0, keepdims=True)
        norm = lse[0, h : h + 1, :]
        slope = head_slope(2 * pair + h)
        grad_q = jnp.zeros((size, tok), F32)
        for i in range(tok // blk):
            at = slice(i * blk, (i + 1) * blk)
            scores = dot_t(k[at, :], q_h) - slope * far[at, :]
            probs = jnp.exp(scores - norm)
            pulled = dot_t(v[at, :], g_h)
            ds = (probs * (pulled - delta)).astype(BF)
            gv = dot(probs.astype(BF), g_all)
            gk = dot(ds, q_all)
            grad_q = grad_q + dot(k_t[h * size : (h + 1) * size, at], ds)
            if h == 0:
                gv_ref[at, :] = gv.astype(BF)
                gk_ref[at, :] = gk.astype(BF)
            else:
                gv_ref[at, :] = jnp.where(mine, gv.astype(BF), gv_ref[at, :])
                gk_ref[at, :] = jnp.where(mine, gk.astype(BF), gk_ref[at, :])
        grads_q.append(grad_q)
    gq_ref[...] = jnp.concatenate(grads_q, axis=0).T.astype(BF)


def attend_back(qkv, grad_mixed, mixed, lse, far, heads, part, parts, before=(), count=1):
    tok = qkv.shape[0]
    width = qkv.shape[1] // 3
    size = width // heads
    pairs = heads // 2
    here = pairs // parts * count
    start = part * (pairs // parts)
    blk = min(512, tok)

    def cols(k):
        return pl.BlockSpec((tok, 2 * size), lambda p: (0, k * pairs + start + p))

    out = jax.ShapeDtypeStruct((tok, width), BF)
    return pl.pallas_call(
        functools.partial(attend_back_kernel, size, blk, start),
        grid=(here,),
        in_specs=[
            cols(0),
            cols(1),
            cols(2),
            cols(0),
            cols(0),
            pl.BlockSpec((1, 8, tok), lambda p: (start + p, 0, 0)),
            pl.BlockSpec((tok, tok), lambda p: (0, 0), pipeline_mode=pl.Buffered(1)),
        ]
        + [ANY] * len(before),
        out_specs=[cols(0)] * 3,
        out_shape=[out] * 3,
        input_output_aliases={7 + k: k for k in range(len(before))},
        compiler_params=params(),
        cost_estimate=cost(
            40 * here * 2 * tok * tok * size, tok * width * 16 // parts, here * 2 * tok * tok
        ),
        name="attend_back",
    )(qkv, qkv, qkv, grad_mixed, mixed, lse, far, *before)


def tags(length_row, mask_row, tok):
    order = jnp.arange(length_row.shape[0])
    ends = jnp.sum(jnp.where(order[:, None] <= order[None, :], length_row[:, None], 0), axis=0)
    slots = jnp.arange(tok, dtype=jnp.int32)
    segment = jnp.sum((slots[:, None] >= ends[None, :]).astype(jnp.int32), axis=1)
    used = slots < jnp.sum(length_row)
    return jnp.where(used, segment, -1), jnp.where(used & (mask_row == 1), segment, -2)


def body(size, frames, skip, lengths, key_mask, cotangent, *weights):
    (
        w_skip, b_skip, pre_attn_gain, pre_attn_bias, w_qkv, b_query, b_value, w_out, b_out,
        pre_ffn_gain, pre_ffn_bias, w_up, b_up, w_down, b_down,
    ) = weights
    tok, width = frames.shape
    net = Net(
        size,
        min(w.shape[0] for w in (w_skip, w_qkv, w_out, w_up, w_down)),
        (b_skip.shape[0], b_up.shape[0]),
    )
    index = lax.axis_index(AXES).astype(jnp.int32)
    me = index.reshape(1)
    narrow = (
        b_skip, pre_attn_gain, pre_attn_bias, b_query, b_value, b_out, pre_ffn_gain, pre_ffn_bias, b_down,
    )

    def stacked(arrays):
        return jnp.stack(arrays) if net.fast else arrays[0]

    flow = Flow(net)
    flow.own("s", w_skip)
    flow.z("s", 1, 2, 3)
    w_two, w_three = w_qkv, [w_out, w_up]
    if net.fast:
        w_two = jnp.concatenate([w_qkv, packed_vectors(narrow, b_up, w_qkv.shape[0])], axis=1)
        w_three = [jnp.concatenate(w_three, axis=1)]
    w_two, w_three, w_down = flow.end((w_two, w_three, w_down), "s")
    flow.own("q", w_two)
    flow.own("u", w_three[-1])
    flow.own("o", w_three[0])
    flow.own("d", w_down)
    flow.near("s")
    flow.z("q", 2)
    tag_q, tag_k = tags(lengths[0], key_mask, tok)
    tag_q, tag_k = flow.end((tag_q, tag_k), "s", "q")
    flow.far("s")
    flow.core("s", 0, 1)
    flow.z("q", 1, 3)
    far_t = far_matrix(tag_k, tag_q)
    frames, far_t, tag_q = flow.end((frames, far_t, tag_q), "s", "q", "u")
    flow.core("s", 2, 3)
    flow.near("q")
    flow.z("u", 2)
    frames = flow.end(frames, "s")
    flow.core("q", 0)
    flow.z("u", 1)
    pieces_s = flow.pieces("s")
    raw = skip_forward(net, me, frames, skip, pieces_s)
    raw, tag_q = flow.end((raw, tag_q), "q", "u")
    flow.far("q")
    flow.core("q", 1, 2)
    flow.z("u", 3)
    far = far_matrix(tag_q, tag_k)
    raw, far = flow.end((raw, far), "q", "u")
    flow.core("q", 3)
    raw = flow.end(raw, "q")
    flow.near("u")
    pieces_q = flow.pieces("q")
    if net.fast:
        vecs, bup = unpack_vectors(net, me, pieces_q, 3 * width)
    else:
        every = [lax.all_gather(v, AXES, axis=0, tiled=True).astype(F32) for v in (*narrow, b_up)]
        vecs, bup = jnp.pad(jnp.stack(every[:-1]), ((0, 16 - len(narrow)), (0, 0))), every[-1][None]
    normed, qkv = qkv_forward(net, me, raw, vecs, pieces_q)
    qkv = flow.end(qkv, "d")
    flow.z("d", 1, 2)
    attended = attend(qkv, far, HEADS, 0, 2)
    attended = flow.end(attended, "u", "d")
    flow.far("u")
    flow.core("u", 0, 1, 2)
    flow.z("d", 3)
    attended = attend(qkv, far, HEADS, 1, 2, attended)
    attended = flow.end(attended, "u", "d")
    flow.core("u", 3)
    attended = flow.end(attended, "u", "d")
    flow.near("d")
    mixed, lse = attended
    pieces_u = ([] if net.fast else flow.pieces("o")) + flow.pieces("u")
    second, normed2, act, pull = up_forward(net, me, raw, mixed, pieces_u, vecs, bup)
    act = flow.end(act, "d")
    flow.far("d")
    flow.core("d", 0, 1, 2)
    down = Scatter(net, weight_grad(net, me, [act], [cotangent], "grad_down"))
    down.keep, down.send = flow.end((down.keep, down.send), "d")
    flow.core("d", 3)
    pieces_d = flow.pieces("d")

    down.keep, down.send, pieces_d = bar(down.keep, down.send, pieces_d)
    down_got = down.core()
    gh, gbup, gbdown = hidden_back(net, me, pull, cotangent, pieces_d)
    gh, down_got = bar(gh, down_got)
    down_got = down.b(down_got)
    gsec, gmixed, ggain2, gshift2, gbout, *up_parts = second_back(
        net, me, gh, normed2, mixed, second, cotangent, pieces_u, vecs
    )
    gmixed, down_got, up_parts = bar(gmixed, down_got, up_parts)
    down_got = down.a(down_got)
    if net.fast:
        up = Scatter(net, up_parts)
    else:
        up, out = Scatter(net, up_parts[:1]), Scatter(net, up_parts[1:])
    gmixed, up.keep, up.send = bar(gmixed, up.keep, up.send)
    up_got = up.core()
    back = (qkv, gmixed, mixed, lse, far_t, HEADS)
    grads = attend_back(*back, 0, 4)
    grads, down_got, up_got = bar(grads, down_got, up_got)
    down_got = down.z(down_got, 1, 2, 3)
    up_got = up.b(up_got)
    grads = attend_back(*back, 1, 4, grads, 2)
    grads, down_got, up_got = bar(grads, down_got, up_got)
    up_got = up.a(up_got)
    grads = attend_back(*back, 3, 4, grads)
    (gq, gk, gv), up_got = bar(grads, up_got)
    up_got = up.z(up_got, 1, 2)
    gqkv = Scatter(net, weight_grad(net, me, [normed], [gq, gk, gv], "grad_qkv", most=True))
    gq, gqkv.keep, gqkv.send, up_got, up.keep = bar(gq, gqkv.keep, gqkv.send, up_got, up.keep)
    qkv_got = gqkv.core()
    up_got += up.z(None, 3)
    gfirst, ggain1, gshift1, gbskip, gbq, gbv = first_back(
        net, me, gq, gk, gv, raw, gsec, pieces_q, vecs
    )
    gfirst, qkv_got, ggain1, up_got = bar(gfirst, qkv_got, ggain1, up_got)
    qkv_got = gqkv.b(qkv_got)
    rows = [gbskip, ggain1, gshift1, gbq, gbv, gbout, ggain2, gshift2, gbdown, gbup.reshape(-1, width)]
    rows = sum_vectors(net, jnp.concatenate(rows, axis=0), 0, 1)
    gskip_w = Scatter(net, weight_grad(net, me, [frames, skip], [gfirst], "grad_skip", most=True))
    gfirst, gskip_w.keep, gskip_w.send, rows, qkv_got = bar(
        gfirst, gskip_w.keep, gskip_w.send, rows, qkv_got
    )
    qkv_got = gqkv.a(qkv_got)
    skip_got = gskip_w.core()
    rows = sum_vectors(net, rows, 1, 2)
    gframes, gskip = joined_back(net, me, gfirst, pieces_s)
    gframes, qkv_got, skip_got, second, rows = bar(gframes, qkv_got, skip_got, second, rows)
    skip_got = gskip_w.b(skip_got)
    qkv_got = gqkv.z(qkv_got, 1, 2)
    rows = sum_vectors(net, rows, 2, 3)
    layer_out = down_forward(net, me, second, act, pieces_d, vecs, 0, 2)
    layer_out, qkv_got, skip_got, rows, gqkv.keep = bar(layer_out, qkv_got, skip_got, rows, gqkv.keep)
    skip_got = gskip_w.a(skip_got)
    qkv_got += gqkv.z(None, 3)
    rows = sum_vectors(net, rows, 3, 4)
    layer_out = down_forward(net, me, second, act, pieces_d, vecs, 1, 2, [layer_out])
    layer_out, qkv_got, skip_got, rows = bar(layer_out, qkv_got, skip_got, rows)
    skip_got = gskip_w.z(skip_got, 1, 2, 3)
    rows = sum_vectors(net, rows, 4, net.bits)

    def mine(row):
        each = width // size
        return lax.dynamic_slice(rows[row], (index * each,), (each,))

    wide = rows[9:].reshape(-1)
    each = wide.shape[0] // size
    o_bup = lax.dynamic_slice(wide, (index * each,), (each,))
    up_out = up.done(up_got, slice(0, 4 * width) if net.fast else slice(None))
    if net.fast:
        out_out = up.done(up_got, slice(4 * width, 5 * width))
    else:
        out_out = out.core()
    return (
        layer_out,
        gframes,
        gskip,
        gskip_w.done(skip_got),
        mine(0),
        mine(1),
        mine(2),
        gqkv.done(qkv_got),
        mine(3),
        mine(4),
        out_out,
        mine(5),
        mine(6),
        mine(7),
        up_out,
        o_bup,
        down.done(down_got),
        mine(8),
    )


def solution(mesh):
    mat, vec = P(AXES, None), P(AXES)
    size = math.prod(mesh.shape.values())
    return jax.shard_map(
        functools.partial(body, size),
        mesh=mesh,
        in_specs=(
            mat, mat, mat, vec, mat,
            mat, vec, vec, vec, mat, vec, vec, mat, vec, vec, vec, mat, vec, mat, vec,
        ),
        out_specs=(
            mat, mat, mat,
            mat, vec, vec, vec, mat, vec, vec, mat, vec, vec, vec, mat, vec, mat, vec,
        ),
        check_vma=False,
    )
```

```python
import functools
import math

import jax
import jax.numpy as jnp
from jax import lax
from jax.experimental import pallas as pl
from jax.experimental.pallas import tpu as pltpu
from jax.sharding import PartitionSpec as P

HEADS = 16
EPSILON = 1e-05
FAR = 1e32
AXES = ("wide", "narrow")
BF = jnp.bfloat16
F32 = jnp.float32
VMEM_LIMIT = 36 * 1024 * 1024
VMEM_MOST = 58 * 1024 * 1024

ANY = pl.BlockSpec(memory_space=pl.ANY)
SMEM = pl.BlockSpec(memory_space=pltpu.SMEM)


def params(limit=VMEM_LIMIT):
    return pltpu.CompilerParams(vmem_limit_bytes=limit)


def cost(flops, nbytes, trans=0):
    return pl.CostEstimate(flops=int(flops), bytes_accessed=int(nbytes), transcendentals=int(trans))


class Net:
    def __init__(self, size, rows_min, vec_rows):
        self.size = size
        self.bits = size.bit_length() - 1
        self.high = self.bits - 3
        self.groups = 1 << self.high
        self.fast = size == 1 << self.bits and self.bits >= 3 and rows_min % 16 == 0 and vec_rows == (32, 128)
        self.shards = size if self.fast else 1

    def pp(self, x, mask):
        if not self.fast:
            return x
        pairs = [(d, d ^ mask(d & 1)) for d in range(self.size)]
        return lax.ppermute(x, AXES, pairs)


def first_bit(core):
    return 2 + 2 * core


def second_bit(core):
    return 4 - 2 * core


def other_core(core):
    return 1


def piece_masks(core):
    a, b = first_bit(core), second_bit(core)
    return [0, a, b, 6, 1, 1 ^ b, 1 ^ a, 7]


def bar(*values):
    return lax.optimization_barrier(values)


class Flow:
    def __init__(self, net):
        self.net, self.data = net, {}

    def end(self, values, *prefixes):
        names = [n for n in self.data if n.startswith(prefixes)] if prefixes else []
        values, arrays = bar(values, [self.data[n] for n in names])
        self.data.update(zip(names, arrays))
        return values

    def send(self, name, x, mask):
        self.data[name] = self.net.pp(x, mask)

    def own(self, p, shard):
        if self.net.fast:
            self.data[p + "z0"] = shard
        else:
            self.data[p + "m0"] = lax.all_gather(shard, AXES, axis=0, tiled=True)

    def z(self, p, *steps):
        if self.net.fast:
            for j in steps:
                self.send(f"{p}z{j}", self.data[p + "z0"], lambda c, j=j: j << 3)

    def near(self, p):
        if not self.net.fast:
            return
        block = jnp.stack([self.data.pop(f"{p}z{j}") for j in range(self.net.groups)])
        self.data[p + "m0"] = block
        self.send(p + "m1", block, first_bit)
        self.send(p + "m2", block, second_bit)

    def far(self, p):
        if self.net.fast:
            self.send(p + "m3", self.data[p + "m1"], second_bit)

    def core(self, p, *which):
        if self.net.fast:
            for i in which:
                self.send(f"{p}o{i}", self.data[f"{p}m{i}"], other_core)

    def pieces(self, p):
        if not self.net.fast:
            return [self.data.pop(p + "m0")]
        return [self.data.pop(p + k + str(i)) for k in "mo" for i in range(4)]


BSKIP, GAIN1, SHIFT1, BQUERY, BVALUE, BOUT, GAIN2, SHIFT2, BDOWN = range(9)


def packed_vectors(vectors, wide, rows):
    narrow = jnp.pad(jnp.stack(vectors), ((0, 0), (0, 128 - vectors[0].shape[0])))
    return jnp.pad(
        jnp.concatenate([narrow, wide.reshape(1, 128)], axis=0),
        ((0, rows - len(vectors) - 1), (0, 0)),
    )


def unpack_kernel(net, col, me_ref, *rest):
    pieces, (rows_ref, wide_ref, held, sems) = rest[:8], rest[8:]
    me = me_ref[0]
    masks = piece_masks(me & 1)
    copies = []
    for i, piece in enumerate(pieces):
        for j in range(net.groups):
            source = me ^ (masks[i] ^ (j << 3))
            copies.append(
                pltpu.make_async_copy(
                    piece.at[j, pl.ds(0, 16), pl.ds(col, 128)], held.at[source], sems.at[len(copies)]
                )
            )
    for copy in copies:
        copy.start()
    for copy in copies:
        copy.wait()
    for d in range(0, net.size, 4):
        tile = held[d].astype(F32)
        for k in range(1, 4):
            tile = tile + pltpu.roll(held[d + k].astype(F32), 32 * k, 1)
        rows_ref[:, 32 * d : 32 * d + 128] = tile
    for d in range(net.size):
        wide_ref[:, 128 * d : 128 * d + 128] = held[d].astype(F32)[9:10, :]


def unpack_vectors(net, me, pieces, col):
    return pl.pallas_call(
        functools.partial(unpack_kernel, net, col),
        in_specs=[SMEM] + [ANY] * len(pieces),
        out_shape=[
            jax.ShapeDtypeStruct((16, 32 * net.size), F32),
            jax.ShapeDtypeStruct((1, 128 * net.size), F32),
        ],
        scratch_shapes=[pltpu.VMEM((net.size, 16, 128), BF), pltpu.SemaphoreType.DMA((net.size,))],
        compiler_params=params(),
        cost_estimate=cost(1000, 200000),
        name="unpack_vectors",
    )(me, *pieces)


def sum_vectors(net, rows, start, stop):
    if not net.fast:
        return rows if start else lax.psum(rows, AXES)
    for bit in range(start, stop):
        rows = rows + net.pp(rows, lambda c: 1 << bit)
    return rows


class Scatter:
    def __init__(self, net, parts):
        self.net, self.keep, self.got = net, parts[0], []
        self.send = parts[-1]

    def summed(self, lo, hi, cols=slice(None)):
        total = self.keep[lo:hi, :, cols].astype(F32)
        for at, arr in self.got:
            if at <= lo and hi <= at + arr.shape[0]:
                total = total + arr[lo - at : hi - at, :, cols].astype(F32)
        return total

    def take(self, got, at=0):
        if got is not None:
            self.got.append((at, got))

    def core(self):
        if not self.net.fast:
            total = self.keep[0].astype(F32)
            return lax.psum_scatter(total, AXES, scatter_dimension=0, tiled=True)
        return self.net.pp(self.send, other_core)

    def next(self, got, mask, lo, at=0):
        self.take(got, at)
        if not self.net.fast:
            return got
        return self.net.pp(self.summed(lo, 2 * lo).astype(BF), mask)

    def b(self, got):
        return self.next(got, second_bit, 2 * self.net.groups)

    def a(self, got, at=0):
        return self.next(got, first_bit, self.net.groups, at)

    def z(self, got, *steps):
        self.take(got)
        if not self.net.fast:
            return [] if got is None else [got]
        return [
            self.net.pp(self.summed(j, j + 1)[0].astype(BF), lambda c, j=j: j << 3) for j in steps
        ]

    def done(self, last, cols=slice(None)):
        if not self.net.fast:
            return last[0][:, cols]
        total = self.summed(0, 1, cols)[0]
        for arr in last:
            total = total + arr[:, cols].astype(F32)
        return total


def load_list(net, me, pieces, dst, sems, which=0, col=0):
    copies = []
    if not net.fast:
        copies.append(pltpu.make_async_copy(pieces[which], dst, sems.at[0]))
    else:
        masks = piece_masks(me & 1)
        rows, cols = dst.shape[0] // net.size, dst.shape[1]
        for i, piece in enumerate(pieces):
            for j in range(net.groups):
                source = me ^ (masks[i] ^ (j << 3))
                at = pl.multiple_of(source * rows, rows)
                copies.append(
                    pltpu.make_async_copy(
                        piece.at[j, :, pl.ds(col, cols)],
                        dst.at[pl.ds(at, rows), :],
                        sems.at[len(copies)],
                    )
                )
    return copies


def load_start(*args):
    copies = load_list(*args)
    for copy in copies:
        copy.start()
    return copies


def relative(net, rel, core):
    bit_one, bit_two, group = (rel >> 1) & 1, (rel >> 2) & 1, rel >> 3
    top = jnp.where(core == 0, bit_two, bit_one)
    low = jnp.where(core == 0, bit_one, bit_two)
    return (top << (net.high + 1)) | (low << net.high) | group


def store_copies(net, me, src, base, rows, total_rows, outs, col, sems, first_sem):
    cols = pl.ds(col, src.shape[1])
    if not net.fast:
        rows = pl.ds(base, rows)
        return [
            pltpu.make_async_copy(
                src.at[rows, :], outs[0].at[0, rows, cols], sems.at[first_sem]
            )
        ]
    copies = []
    shard = total_rows // net.size
    core = me & 1
    for i in range(0, rows // shard, 2):
        even = base // shard + i
        for k, out in enumerate(outs):
            owner_core = core if k == 0 else 1 - core
            target = even | owner_core
            rel = (me if k == 0 else me ^ 1) ^ target
            at = pl.multiple_of(target * shard, shard)
            copies.append(
                pltpu.make_async_copy(
                    src.at[pl.ds(at, shard), :],
                    out.at[relative(net, rel, owner_core), :, cols],
                    sems.at[first_sem + i + k],
                )
            )
    return copies


def dot(a, b):
    return jnp.dot(a, b, preferred_element_type=F32)


def dot_t(a, b):
    return lax.dot_general(a, b, (((1,), (1,)), ((), ())), preferred_element_type=F32)


def norm_parts(x):
    center = x - jnp.mean(x, axis=1, keepdims=True)
    spread = jnp.mean(center * center, axis=1, keepdims=True)
    rstd = lax.rsqrt(spread + EPSILON)
    return center * rstd, rstd


def sums(x):
    return jnp.sum(x, axis=0, keepdims=True)


def add_to(ref, value, step):
    @pl.when(step == 0)
    def _():
        ref[...] = value

    @pl.when(step > 0)
    def _():
        ref[...] += value


def row_block(tok):
    return min(512, tok)


def weight_scratch(net, *shapes):
    out = []
    for shape in shapes:
        out += [pltpu.VMEM(shape, BF), pltpu.SemaphoreType.DMA((net.shards,))]
    return out


def n_pieces(net, whole=1):
    return 8 if net.fast else whole


def skip_kernel(net, me_ref, frames, skip, *rest):
    np_ = n_pieces(net)
    pieces, (raw_ref, w, sems) = rest[:np_], rest[np_:]

    @pl.when(pl.program_id(0) == 0)
    def _():
        for copy in load_start(net, me_ref[0], pieces, w, sems):
            copy.wait()

    width = frames.shape[1]
    raw_ref[...] = dot(frames[...], w[:width, :]) + dot(skip[...], w[width:, :])


def skip_forward(net, me, frames, skip, pieces):
    tok, width = frames.shape
    blk = row_block(tok)
    rows = pl.BlockSpec((blk, width), lambda i: (i, 0))
    return pl.pallas_call(
        functools.partial(skip_kernel, net),
        grid=(tok // blk,),
        in_specs=[SMEM, rows, rows] + [ANY] * len(pieces),
        out_specs=rows,
        out_shape=jax.ShapeDtypeStruct((tok, width), F32),
        scratch_shapes=weight_scratch(net, (2 * width, width)),
        compiler_params=params(),
        cost_estimate=cost(4 * tok * width * width, tok * width * 8 + 4 * width * width),
        name="skip_forward",
    )(me, frames, skip, *pieces)


def vec_row(vecs, k):
    return vecs[k : k + 1, :]


def qkv_kernel(net, me_ref, raw, vecs, *rest):
    np_ = n_pieces(net)
    pieces, (normed_ref, out_ref, w, sems) = rest[:np_], rest[np_:]

    @pl.when(pl.program_id(0) == 0)
    def _():
        copies = load_start(net, me_ref[0], pieces, w, sems)
        for copy in copies:
            copy.wait()

    xhat, _ = norm_parts(raw[...] + vec_row(vecs, BSKIP))
    normed = (xhat * vec_row(vecs, GAIN1) + vec_row(vecs, SHIFT1)).astype(BF)
    normed_ref[...] = normed
    width = raw.shape[1]
    out_ref[:, :width] = (dot(normed, w[:, :width]) + vec_row(vecs, BQUERY)).astype(BF)
    out_ref[:, width : 2 * width] = dot(normed, w[:, width : 2 * width]).astype(BF)
    out_ref[:, 2 * width :] = (dot(normed, w[:, 2 * width :]) + vec_row(vecs, BVALUE)).astype(BF)


def qkv_forward(net, me, raw, vecs, pieces):
    tok, width = raw.shape
    cols = 3 * width
    blk = row_block(tok)
    return pl.pallas_call(
        functools.partial(qkv_kernel, net),
        grid=(tok // blk,),
        in_specs=[
            SMEM,
            pl.BlockSpec((blk, width), lambda i: (i, 0)),
            pl.BlockSpec((16, width), lambda i: (0, 0)),
        ]
        + [ANY] * len(pieces),
        out_specs=[
            pl.BlockSpec((blk, width), lambda i: (i, 0)),
            pl.BlockSpec((blk, cols), lambda i: (i, 0)),
        ],
        out_shape=[jax.ShapeDtypeStruct((tok, width), BF), jax.ShapeDtypeStruct((tok, cols), BF)],
        scratch_shapes=weight_scratch(net, (width, cols)),
        compiler_params=params(),
        cost_estimate=cost(2 * tok * width * cols, tok * width * 12 + 6 * width * width),
        name="qkv_forward",
    )(me, raw, vecs, *pieces)


def gelu_both(v):
    lead, cubic = 0.7978845608, 0.7978845608 * 0.044715
    square = v * v
    half = 0.5 + 0.5 * jnp.tanh(v * (lead + cubic * square))
    slope = half + (half - half * half) * (v * (2 * lead + (6 * cubic) * square))
    return v * half, slope


def up_kernel(net, me_ref, raw, mixed, vecs, b_up, *rest):
    np_ = n_pieces(net, 2)
    pieces, rest = rest[:np_], rest[np_:]
    second_ref, normed_ref, act_ref, pull_ref, w_out, sems_out, w_up, sems_up = rest

    @pl.when(pl.program_id(0) == 0)
    def _():
        copies = load_start(net, me_ref[0], pieces, w_out, sems_out, 0, 0)
        copies += load_start(net, me_ref[0], pieces, w_up, sems_up, 1, w_out.shape[1])
        for copy in copies:
            copy.wait()

    bias = vec_row(vecs, BSKIP) + vec_row(vecs, BOUT)
    second = raw[...] + dot(mixed[...], w_out[...]) + bias
    second_ref[...] = second
    xhat, _ = norm_parts(second)
    normed = (xhat * vec_row(vecs, GAIN2) + vec_row(vecs, SHIFT2)).astype(BF)
    normed_ref[...] = normed
    chunk = 1024
    for at in range(0, w_up.shape[1], chunk):
        part = slice(at, at + chunk)
        hidden = dot(normed, w_up[:, part]) + b_up[:, part]
        act, pull = gelu_both(hidden)
        act_ref[:, part] = act.astype(BF)
        pull_ref[:, part] = pull.astype(BF)


def up_forward(net, me, raw, mixed, pieces, vecs, b_up):
    tok, width = raw.shape
    ff = b_up.shape[1]
    blk = min(256, tok)
    rows = pl.BlockSpec((blk, width), lambda i: (i, 0))
    wide = pl.BlockSpec((blk, ff), lambda i: (i, 0))
    vec = pl.BlockSpec((16, width), lambda i: (0, 0))
    vec_ff = pl.BlockSpec((1, ff), lambda i: (0, 0))
    return pl.pallas_call(
        functools.partial(up_kernel, net),
        grid=(tok // blk,),
        in_specs=[SMEM, rows, rows, vec, vec_ff] + [ANY] * len(pieces),
        out_specs=[rows, rows, wide, wide],
        out_shape=[
            jax.ShapeDtypeStruct((tok, width), F32),
            jax.ShapeDtypeStruct((tok, width), BF),
            jax.ShapeDtypeStruct((tok, ff), BF),
            jax.ShapeDtypeStruct((tok, ff), BF),
        ],
        scratch_shapes=weight_scratch(net, (width, width), (width, ff)),
        compiler_params=params(),
        cost_estimate=cost(
            2 * tok * width * (width + ff), tok * (width * 12 + ff * 4) + 2 * width * (width + ff)
        ),
        name="up_forward",
    )(me, raw, mixed, vecs, b_up, *pieces)


def down_kernel(net, me_ref, second, act, vecs, *rest):
    pieces, (out_ref, w, sems) = rest[: n_pieces(net)], rest[-3:]

    @pl.when(pl.program_id(0) == 0)
    def _():
        for copy in load_start(net, me_ref[0], pieces, w, sems):
            copy.wait()

    out_ref[...] = (second[...] + dot(act[...], w[...]) + vec_row(vecs, BDOWN)).astype(BF)


def down_forward(net, me, second, act, pieces, vecs, part, parts, before=()):
    tok, width = second.shape
    ff = act.shape[1]
    blk = min(256, tok)
    steps = tok // blk // parts
    start = part * steps
    rows = pl.BlockSpec((blk, width), lambda i: (start + i, 0))
    wide = pl.BlockSpec((blk, ff), lambda i: (start + i, 0))
    vec = pl.BlockSpec((16, width), lambda i: (0, 0))
    return pl.pallas_call(
        functools.partial(down_kernel, net),
        grid=(steps,),
        in_specs=[SMEM, rows, wide, vec] + [ANY] * (len(pieces) + len(before)),
        out_specs=rows,
        out_shape=jax.ShapeDtypeStruct((tok, width), BF),
        input_output_aliases={4 + len(pieces): 0} if before else {},
        scratch_shapes=weight_scratch(net, (ff, width)),
        compiler_params=params(),
        cost_estimate=cost(
            2 * tok * width * ff // parts, tok * (width * 6 + ff * 2) // parts + 2 * width * ff
        ),
        name="down_forward",
    )(me, second, act, vecs, *pieces, *before)


def hidden_kernel(net, me_ref, pull, cot, *rest):
    np_ = n_pieces(net)
    pieces, (gh_ref, bsum_ref, csum_ref, w, sems) = rest[:np_], rest[np_:]
    step = pl.program_id(0)

    @pl.when(step == 0)
    def _():
        for copy in load_start(net, me_ref[0], pieces, w, sems):
            copy.wait()

    chunk = 1024
    for at in range(0, w.shape[0], chunk):
        part = slice(at, at + chunk)
        gh = (dot_t(cot[...], w[part, :]) * pull[:, part].astype(F32)).astype(BF)
        gh_ref[:, part] = gh
        add_to(bsum_ref.at[:, part], sums(gh.astype(F32)), step)
    add_to(csum_ref, sums(cot[...].astype(F32)), step)


def hidden_back(net, me, pull, cot, pieces):
    tok, width = cot.shape
    ff = pull.shape[1]
    blk = row_block(tok)
    rows = pl.BlockSpec((blk, width), lambda i: (i, 0))
    wide = pl.BlockSpec((blk, ff), lambda i: (i, 0))
    vec = pl.BlockSpec((1, width), lambda i: (0, 0))
    vec_ff = pl.BlockSpec((1, ff), lambda i: (0, 0))
    return pl.pallas_call(
        functools.partial(hidden_kernel, net),
        grid=(tok // blk,),
        in_specs=[SMEM, wide, rows] + [ANY] * len(pieces),
        out_specs=[wide, vec_ff, vec],
        out_shape=[
            jax.ShapeDtypeStruct((tok, ff), BF),
            jax.ShapeDtypeStruct((1, ff), F32),
            jax.ShapeDtypeStruct((1, width), F32),
        ],
        scratch_shapes=weight_scratch(net, (ff, width)),
        compiler_params=params(),
        cost_estimate=cost(2 * tok * width * ff, tok * (width * 2 + ff * 4) + 2 * width * ff),
        name="hidden_back",
    )(me, pull, cot, *pieces)


def grad_kernel(net, lefts, rights, blk, col, outs_n, into_n, me_ref, *rest):
    left_refs, right_refs = rest[:lefts], rest[lefts : lefts + rights]
    rest = rest[lefts + rights + into_n :]
    outs, (acc, sems) = rest[:outs_n], rest[outs_n:]
    step = pl.program_id(0)
    total, cols = acc.shape
    steps = total // blk
    per_left = steps // lefts
    per_step = sems.shape[0] // steps
    for s in range(steps):

        @pl.when(step == s)
        def _():
            left = left_refs[s // per_left][...].T
            at = 0
            for right in right_refs:
                chunk = min(1024, right.shape[1])
                for i in range(0, right.shape[1], chunk):
                    acc[s * blk : (s + 1) * blk, at : at + chunk] = dot(
                        left, right[:, i : i + chunk]
                    ).astype(BF)
                    at += chunk
            for copy in store_copies(
                net, me_ref[0], acc, s * blk, blk, total, outs, col, sems, s * per_step
            ):
                copy.start()

    @pl.when(step == steps - 1)
    def _():
        for s in range(steps):
            for copy in store_copies(
                net, me_ref[0], acc, s * blk, blk, total, outs, col, sems, s * per_step
            ):
                copy.wait()


def weight_grad(net, me, lefts, rights, name, into=(), col=0, all_cols=0, most=False):
    tok = lefts[0].shape[0]
    cols = sum(right.shape[1] for right in rights)
    each = lefts[0].shape[1]
    total = each * len(lefts)
    blk = min(512, each)
    per_left = each // blk
    steps = total // blk
    all_cols = all_cols or cols
    if net.fast:
        per_step = blk // (total // net.size)
        shapes = [jax.ShapeDtypeStruct((net.size // 2, total // net.size, all_cols), BF)] * 2
    else:
        per_step = 1
        shapes = [jax.ShapeDtypeStruct((1, total, all_cols), BF)]

    def index(k):
        return lambda i: (0, jnp.clip(i - k * per_left, 0, per_left - 1))

    first_into = 1 + len(lefts) + len(rights)
    return pl.pallas_call(
        functools.partial(
            grad_kernel, net, len(lefts), len(rights), blk, col, len(shapes), len(into)
        ),
        grid=(steps,),
        in_specs=[SMEM]
        + [pl.BlockSpec((tok, blk), index(k)) for k in range(len(lefts))]
        + [
            pl.BlockSpec(right.shape, lambda i: (0, 0), pipeline_mode=pl.Buffered(1))
            for right in rights
        ]
        + [ANY] * len(into),
        out_specs=[ANY] * len(shapes),
        out_shape=shapes,
        input_output_aliases={first_into + k: k for k in range(len(into))},
        scratch_shapes=[
            pltpu.VMEM((total, cols), BF),
            pltpu.SemaphoreType.DMA((steps * per_step,)),
        ],
        compiler_params=params(VMEM_MOST if most else VMEM_LIMIT),
        cost_estimate=cost(
            2 * tok * total * cols, 2 * tok * (total + cols) + 2 * total * cols
        ),
        name=name,
    )(me, *lefts, *rights, *into)


def norm_back(dn, x, gain):
    xhat, rstd = norm_parts(x)
    scaled = dn * gain
    mean_one = jnp.mean(scaled, axis=1, keepdims=True)
    mean_two = jnp.mean(scaled * xhat, axis=1, keepdims=True)
    return (scaled - mean_one - xhat * mean_two) * rstd, dn * xhat


def second_kernel(net, blk_w, blk, outs_n, me_ref, gh, normed, mixed, second, cot, vecs, *rest):
    np_ = n_pieces(net, 2)
    pieces, rest = rest[:np_], rest[np_:]
    gsec_ref, gmix_ref, ggain_ref, gshift_ref, gbout_ref = rest[:5]
    outs, rest = rest[5 : 5 + outs_n], rest[5 + outs_n :]
    w_up, sems_up, w_out, sems_out, acc_up, sems_a, acc_out, sems_b, gattn_all = rest
    step = pl.program_id(0)
    me = me_ref[0]
    width, ff = acc_up.shape
    first_steps, mid_steps = width // blk_w, gattn_all.shape[0] // blk
    if net.fast:
        up_outs, out_outs, out_col = outs, outs, ff
    else:
        up_outs, out_outs, out_col = outs[:1], outs[1:], 0
    per_step = sems_a.shape[0] // first_steps

    def stores(acc, targets, col, sems, s):
        return store_copies(net, me, acc, s * blk_w, blk_w, width, targets, col, sems, s * per_step)

    def loads():
        copies = load_list(net, me, pieces, w_up, sems_up, 1, width)
        return copies + load_list(net, me, pieces, w_out, sems_out, 0, 0)

    @pl.when(step == 0)
    def _():
        for copy in loads():
            copy.start()

    for s in range(first_steps):

        @pl.when(step == s)
        def _():
            left = normed[...].T
            for at in range(0, ff, 1024):
                part = slice(at, at + 1024)
                acc_up[s * blk_w : (s + 1) * blk_w, part] = dot(left, gh[:, part]).astype(BF)
            for copy in stores(acc_up, up_outs, 0, sems_a, s):
                copy.start()

    @pl.when(step == first_steps)
    def _():
        for copy in loads():
            copy.wait()

    row = step - first_steps

    @pl.when((row >= 0) & (row < mid_steps))
    def _():
        here = pl.ds(pl.multiple_of(row * blk, blk), blk)
        dn = dot_t(gh[here, :], w_up[...])
        pulled, dx = norm_back(dn, second[...], vec_row(vecs, GAIN2))
        gsec = cot[...].astype(F32) + pulled
        gsec_ref[...] = gsec
        gattn = gsec.astype(BF)
        gattn_all[here, :] = gattn
        gmix_ref[...] = dot_t(gattn, w_out[...]).astype(BF)
        add_to(ggain_ref, sums(dx), row)
        add_to(gshift_ref, sums(dn), row)
        add_to(gbout_ref, sums(gattn.astype(F32)), row)

    for s in range(first_steps):

        @pl.when(row - mid_steps == s)
        def _():
            left = mixed[...].T
            acc_out[s * blk_w : (s + 1) * blk_w, :] = dot(left, gattn_all[...]).astype(BF)
            for copy in stores(acc_out, out_outs, out_col, sems_b, s):
                copy.start()

    @pl.when(row - mid_steps == first_steps - 1)
    def _():
        for s in range(first_steps):
            for copy in stores(acc_up, up_outs, 0, sems_a, s):
                copy.wait()
            for copy in stores(acc_out, out_outs, out_col, sems_b, s):
                copy.wait()


def second_back(net, me, gh, normed, mixed, second, cot, pieces, vecs):
    tok, width = second.shape
    ff = gh.shape[1]
    blk, blk_w = min(256, tok), 512
    first_steps, mid_steps = width // blk_w, tok // blk
    per_step = blk_w // (width // net.size) if net.fast else 1
    if net.fast:
        shard = (net.size // 2, width // net.size, ff + width)
        shapes = [jax.ShapeDtypeStruct(shard, BF)] * 2
    else:
        shapes = [jax.ShapeDtypeStruct((1, width, c), BF) for c in (ff, width)]

    def rows(i):
        return (jnp.clip(i - first_steps, 0, mid_steps - 1), 0)

    def left(start):
        return pl.BlockSpec(
            (tok, blk_w), lambda i: (0, jnp.clip(i - start, 0, first_steps - 1))
        )

    row_spec = pl.BlockSpec((blk, width), rows)
    vec = pl.BlockSpec((1, width), lambda i: (0, 0))
    vec_shape = jax.ShapeDtypeStruct((1, width), F32)
    sems = pltpu.SemaphoreType.DMA((first_steps * per_step,))
    return pl.pallas_call(
        functools.partial(second_kernel, net, blk_w, blk, len(shapes)),
        grid=(2 * first_steps + mid_steps,),
        in_specs=[
            SMEM,
            pl.BlockSpec((tok, ff), lambda i: (0, 0), pipeline_mode=pl.Buffered(1)),
            left(0),
            left(first_steps + mid_steps),
            row_spec,
            row_spec,
            pl.BlockSpec((16, width), lambda i: (0, 0)),
        ]
        + [ANY] * len(pieces),
        out_specs=[row_spec, row_spec, vec, vec, vec] + [ANY] * len(shapes),
        out_shape=[
            jax.ShapeDtypeStruct((tok, width), F32),
            jax.ShapeDtypeStruct((tok, width), BF),
            vec_shape,
            vec_shape,
            vec_shape,
        ]
        + shapes,
        scratch_shapes=weight_scratch(net, (width, ff), (width, width))
        + [
            pltpu.VMEM((width, ff), BF),
            sems,
            pltpu.VMEM((width, width), BF),
            sems,
            pltpu.VMEM((tok, width), BF),
        ],
        compiler_params=params(VMEM_MOST),
        cost_estimate=cost(
            4 * tok * width * (width + ff), tok * (width * 14 + ff * 2) + 4 * width * (width + ff)
        ),
        name="second_back",
    )(me, gh, normed, mixed, second, cot, vecs, *pieces)


def first_kernel(net, me_ref, gq, gk, gv, raw, gsec, vecs, *rest):
    np_ = n_pieces(net)
    pieces, rest = rest[:np_], rest[np_:]
    gfirst_ref, ggain_ref, gshift_ref, gbskip_ref, gbq_ref, gbv_ref, w, sems = rest
    step = pl.program_id(0)

    @pl.when(step == 0)
    def _():
        for copy in load_start(net, me_ref[0], pieces, w, sems):
            copy.wait()

    width = gq.shape[1]
    dn = dot_t(gq[...], w[:, :width])
    dn = dn + dot_t(gk[...], w[:, width : 2 * width])
    dn = dn + dot_t(gv[...], w[:, 2 * width :])
    pulled, dx = norm_back(dn, raw[...] + vec_row(vecs, BSKIP), vec_row(vecs, GAIN1))
    gfirst = (gsec[...] + pulled).astype(BF)
    gfirst_ref[...] = gfirst
    add_to(ggain_ref, sums(dx), step)
    add_to(gshift_ref, sums(dn), step)
    add_to(gbskip_ref, sums(gfirst.astype(F32)), step)
    add_to(gbq_ref, sums(gq[...].astype(F32)), step)
    add_to(gbv_ref, sums(gv[...].astype(F32)), step)


def first_back(net, me, gq, gk, gv, raw, gsec, pieces, vecs):
    tok, width = raw.shape
    blk = row_block(tok)
    rows = pl.BlockSpec((blk, width), lambda i: (i, 0))
    vec = pl.BlockSpec((1, width), lambda i: (0, 0))
    vec_shape = jax.ShapeDtypeStruct((1, width), F32)
    return pl.pallas_call(
        functools.partial(first_kernel, net),
        grid=(tok // blk,),
        in_specs=[SMEM, rows, rows, rows, rows, rows, pl.BlockSpec((16, width), lambda i: (0, 0))]
        + [ANY] * len(pieces),
        out_specs=[rows] + [vec] * 5,
        out_shape=[jax.ShapeDtypeStruct((tok, width), BF)] + [vec_shape] * 5,
        scratch_shapes=weight_scratch(net, (width, 3 * width)),
        compiler_params=params(VMEM_MOST),
        cost_estimate=cost(6 * tok * width * width, tok * width * 16 + 6 * width * width),
        name="first_back",
    )(me, gq, gk, gv, raw, gsec, vecs, *pieces)


def joined_kernel(net, me_ref, gfirst, *rest):
    np_ = n_pieces(net)
    pieces, (gframes_ref, gskip_ref, w, sems) = rest[:np_], rest[np_:]

    @pl.when(pl.program_id(0) == 0)
    def _():
        for copy in load_start(net, me_ref[0], pieces, w, sems):
            copy.wait()

    width = gframes_ref.shape[1]
    gframes_ref[...] = dot_t(gfirst[...], w[:width, :]).astype(BF)
    gskip_ref[...] = dot_t(gfirst[...], w[width:, :]).astype(BF)


def joined_back(net, me, gfirst, pieces):
    tok, width = gfirst.shape
    blk = row_block(tok)
    rows = pl.BlockSpec((blk, width), lambda i: (i, 0))
    out = jax.ShapeDtypeStruct((tok, width), BF)
    return pl.pallas_call(
        functools.partial(joined_kernel, net),
        grid=(tok // blk,),
        in_specs=[SMEM, rows] + [ANY] * len(pieces),
        out_specs=[rows, rows],
        out_shape=[out, out],
        scratch_shapes=weight_scratch(net, (2 * width, width)),
        compiler_params=params(),
        cost_estimate=cost(4 * tok * width * width, tok * width * 6 + 4 * width * width),
        name="joined_back",
    )(me, gfirst, *pieces)


def far_apart(row_tag, col_tag, row_at):
    shape = (row_tag.shape[0], col_tag.shape[1])
    i = row_at + lax.broadcasted_iota(jnp.int32, shape, 0)
    j = lax.broadcasted_iota(jnp.int32, shape, 1)
    ok = (row_tag == col_tag) | (i == j)
    return jnp.where(ok, jnp.abs(i - j).astype(F32), FAR)


def head_slope(head):
    return jnp.exp2((jnp.full((1, 1), head, jnp.int32).astype(F32) + 1.0) * (-8.0 / HEADS))


def far_kernel(blk, tag_q, tag_k, out_ref):
    out_ref[...] = far_apart(tag_q[...], tag_k[...], pl.program_id(0) * blk)


def far_matrix(row_tag, col_tag):
    tok = row_tag.shape[0]
    blk = min(256, tok)
    return pl.pallas_call(
        functools.partial(far_kernel, blk),
        grid=(tok // blk,),
        in_specs=[pl.BlockSpec((blk, 1), lambda i: (i, 0)), pl.BlockSpec((1, tok), lambda i: (0, 0))],
        out_specs=pl.BlockSpec((blk, tok), lambda i: (i, 0)),
        out_shape=jax.ShapeDtypeStruct((tok, tok), F32),
        compiler_params=params(),
        cost_estimate=cost(8 * tok * tok, 4 * tok * tok),
        name="far_matrix",
    )(row_tag.reshape(tok, 1), col_tag.reshape(1, tok))


def transposed(x):
    return x.astype(F32).T.astype(BF)


def attend_kernel(size, blk, first_pair, q, k, v, far, *rest):
    out_ref, lse_ref, columns = rest[-3:]
    pair = first_pair + pl.program_id(0)
    tok = q.shape[0]
    lane = lax.broadcasted_iota(jnp.int32, (1, 2 * size), 1)

    def score(i, h):
        at = slice(i * blk, (i + 1) * blk)
        mine = (lane >= h * size) & (lane < (h + 1) * size)
        q_h = jnp.where(mine, q[at, :] * size**-0.5, 0)
        scores = dot_t(q_h, k[...]) - head_slope(2 * pair + h) * far[at, :]
        return scores, jnp.max(scores, axis=1, keepdims=True)

    steps = [(i, h) for i in range(tok // blk) for h in range(2)]
    coming = score(*steps[0])
    for n, (i, h) in enumerate(steps):
        scores, top = coming
        if n + 1 < len(steps):
            coming = score(*steps[n + 1])
        expo = jnp.exp(scores - top)
        denom = jnp.sum(expo, axis=1, keepdims=True)
        out, lse = dot(expo.astype(BF), v[...]) / denom, top + jnp.log(denom)
        if h == 0:
            before = out, lse
        else:
            at = slice(i * blk, (i + 1) * blk)
            out_ref[at, :] = jnp.where(lane < size, before[0], out).astype(BF)
            columns[at, :] = jnp.where(lane < size, before[1], lse)
    rows = columns[...].T
    lse_ref[0, 0:1, :] = rows[0:1, :]
    lse_ref[0, 1:2, :] = rows[size : size + 1, :]


def attend(qkv, far, heads, part, parts, before=()):
    tok = qkv.shape[0]
    width = qkv.shape[1] // 3
    size = width // heads
    pairs = heads // 2
    here = pairs // parts
    start = part * here
    blk = min(512, tok)

    def cols(k):
        return pl.BlockSpec((tok, 2 * size), lambda p: (0, k * pairs + start + p))

    return pl.pallas_call(
        functools.partial(attend_kernel, size, blk, start),
        grid=(here,),
        in_specs=[
            cols(0),
            cols(1),
            cols(2),
            pl.BlockSpec((tok, tok), lambda p: (0, 0), pipeline_mode=pl.Buffered(1)),
        ]
        + [ANY] * len(before),
        out_specs=[cols(0), pl.BlockSpec((1, 8, tok), lambda p: (start + p, 0, 0))],
        out_shape=[
            jax.ShapeDtypeStruct((tok, width), BF),
            jax.ShapeDtypeStruct((pairs, 8, tok), F32),
        ],
        input_output_aliases={4 + k: k for k in range(len(before))},
        scratch_shapes=[pltpu.VMEM((tok, 2 * size), F32)],
        compiler_params=params(),
        cost_estimate=cost(
            16 * here * 2 * tok * tok * size, tok * width * 8 // parts, here * 2 * tok * tok
        ),
        name="attend",
    )(qkv, qkv, qkv, far, *before)


def attend_back_kernel(size, blk, first_pair, q, k, v, g, o, lse, far, *rest):
    gq_ref, gk_ref, gv_ref = rest[-3:]
    pair = first_pair + pl.program_id(0)
    tok = q.shape[0]
    lane = lax.broadcasted_iota(jnp.int32, (1, 2 * size), 1)
    scale = size**-0.5
    q_all = q[...] * scale
    g_all = g[...]
    products = (g_all.astype(F32) * o[...].astype(F32)).T
    k_t = transposed(k[...] * scale)
    grads_q = []
    for h in range(2):
        mine = (lane >= h * size) & (lane < (h + 1) * size)
        q_h = jnp.where(mine, q_all, 0)
        g_h = jnp.where(mine, g_all, 0)
        delta = jnp.sum(products[h * size : (h + 1) * size, :], axis=0, keepdims=True)
        norm = lse[0, h : h + 1, :]
        slope = head_slope(2 * pair + h)
        grad_q = jnp.zeros((size, tok), F32)
        for i in range(tok // blk):
            at = slice(i * blk, (i + 1) * blk)
            scores = dot_t(k[at, :], q_h) - slope * far[at, :]
            probs = jnp.exp(scores - norm)
            pulled = dot_t(v[at, :], g_h)
            ds = (probs * (pulled - delta)).astype(BF)
            gv = dot(probs.astype(BF), g_all)
            gk = dot(ds, q_all)
            grad_q = grad_q + dot(k_t[h * size : (h + 1) * size, at], ds)
            if h == 0:
                gv_ref[at, :] = gv.astype(BF)
                gk_ref[at, :] = gk.astype(BF)
            else:
                gv_ref[at, :] = jnp.where(mine, gv.astype(BF), gv_ref[at, :])
                gk_ref[at, :] = jnp.where(mine, gk.astype(BF), gk_ref[at, :])
        grads_q.append(grad_q)
    gq_ref[...] = jnp.concatenate(grads_q, axis=0).T.astype(BF)


def attend_back(qkv, grad_mixed, mixed, lse, far, heads, part, parts, before=(), count=1):
    tok = qkv.shape[0]
    width = qkv.shape[1] // 3
    size = width // heads
    pairs = heads // 2
    here = pairs // parts * count
    start = part * (pairs // parts)
    blk = min(512, tok)

    def cols(k):
        return pl.BlockSpec((tok, 2 * size), lambda p: (0, k * pairs + start + p))

    out = jax.ShapeDtypeStruct((tok, width), BF)
    return pl.pallas_call(
        functools.partial(attend_back_kernel, size, blk, start),
        grid=(here,),
        in_specs=[
            cols(0),
            cols(1),
            cols(2),
            cols(0),
            cols(0),
            pl.BlockSpec((1, 8, tok), lambda p: (start + p, 0, 0)),
            pl.BlockSpec((tok, tok), lambda p: (0, 0), pipeline_mode=pl.Buffered(1)),
        ]
        + [ANY] * len(before),
        out_specs=[cols(0)] * 3,
        out_shape=[out] * 3,
        input_output_aliases={7 + k: k for k in range(len(before))},
        compiler_params=params(),
        cost_estimate=cost(
            40 * here * 2 * tok * tok * size, tok * width * 16 // parts, here * 2 * tok * tok
        ),
        name="attend_back",
    )(qkv, qkv, qkv, grad_mixed, mixed, lse, far, *before)


def tags(length_row, mask_row, tok):
    order = jnp.arange(length_row.shape[0])
    ends = jnp.sum(jnp.where(order[:, None] <= order[None, :], length_row[:, None], 0), axis=0)
    slots = jnp.arange(tok, dtype=jnp.int32)
    segment = jnp.sum((slots[:, None] >= ends[None, :]).astype(jnp.int32), axis=1)
    used = slots < jnp.sum(length_row)
    return jnp.where(used, segment, -1), jnp.where(used & (mask_row == 1), segment, -2)


def body(size, frames, skip, lengths, key_mask, cotangent, *weights):
    (
        w_skip, b_skip, pre_attn_gain, pre_attn_bias, w_qkv, b_query, b_value, w_out, b_out,
        pre_ffn_gain, pre_ffn_bias, w_up, b_up, w_down, b_down,
    ) = weights
    tok, width = frames.shape
    net = Net(
        size,
        min(w.shape[0] for w in (w_skip, w_qkv, w_out, w_up, w_down)),
        (b_skip.shape[0], b_up.shape[0]),
    )
    index = lax.axis_index(AXES).astype(jnp.int32)
    me = index.reshape(1)
    narrow = (
        b_skip, pre_attn_gain, pre_attn_bias, b_query, b_value, b_out, pre_ffn_gain, pre_ffn_bias, b_down,
    )

    def stacked(arrays):
        return jnp.stack(arrays) if net.fast else arrays[0]

    flow = Flow(net)
    flow.own("s", w_skip)
    flow.z("s", 1, 2, 3)
    w_two, w_three = w_qkv, [w_out, w_up]
    if net.fast:
        w_two = jnp.concatenate([w_qkv, packed_vectors(narrow, b_up, w_qkv.shape[0])], axis=1)
        w_three = [jnp.concatenate(w_three, axis=1)]
    w_two, w_three, w_down = flow.end((w_two, w_three, w_down), "s")
    flow.own("q", w_two)
    flow.own("u", w_three[-1])
    flow.own("o", w_three[0])
    flow.own("d", w_down)
    flow.near("s")
    flow.z("q", 2)
    tag_q, tag_k = tags(lengths[0], key_mask, tok)
    tag_q, tag_k = flow.end((tag_q, tag_k), "s", "q")
    flow.far("s")
    flow.core("s", 0, 1)
    flow.z("q", 1, 3)
    far_t = far_matrix(tag_k, tag_q)
    frames, far_t, tag_q = flow.end((frames, far_t, tag_q), "s", "q", "u")
    flow.core("s", 2, 3)
    flow.near("q")
    flow.z("u", 2)
    frames = flow.end(frames, "s")
    flow.core("q", 0)
    flow.z("u", 1)
    pieces_s = flow.pieces("s")
    raw = skip_forward(net, me, frames, skip, pieces_s)
    raw, tag_q = flow.end((raw, tag_q), "q", "u")
    flow.far("q")
    flow.core("q", 1, 2)
    flow.z("u", 3)
    far = far_matrix(tag_q, tag_k)
    raw, far = flow.end((raw, far), "q", "u")
    flow.core("q", 3)
    raw = flow.end(raw, "q")
    flow.near("u")
    pieces_q = flow.pieces("q")
    if net.fast:
        vecs, bup = unpack_vectors(net, me, pieces_q, 3 * width)
    else:
        every = [lax.all_gather(v, AXES, axis=0, tiled=True).astype(F32) for v in (*narrow, b_up)]
        vecs, bup = jnp.pad(jnp.stack(every[:-1]), ((0, 16 - len(narrow)), (0, 0))), every[-1][None]
    normed, qkv = qkv_forward(net, me, raw, vecs, pieces_q)
    qkv = flow.end(qkv, "d")
    flow.z("d", 1, 2)
    attended = attend(qkv, far, HEADS, 0, 2)
    attended = flow.end(attended, "u", "d")
    flow.far("u")
    flow.core("u", 0, 1, 2)
    flow.z("d", 3)
    attended = attend(qkv, far, HEADS, 1, 2, attended)
    attended = flow.end(attended, "u", "d")
    flow.core("u", 3)
    attended = flow.end(attended, "u", "d")
    flow.near("d")
    mixed, lse = attended
    pieces_u = ([] if net.fast else flow.pieces("o")) + flow.pieces("u")
    second, normed2, act, pull = up_forward(net, me, raw, mixed, pieces_u, vecs, bup)
    act = flow.end(act, "d")
    flow.far("d")
    flow.core("d", 0, 1, 2)
    down = Scatter(net, weight_grad(net, me, [act], [cotangent], "grad_down"))
    down.keep, down.send = flow.end((down.keep, down.send), "d")
    flow.core("d", 3)
    pieces_d = flow.pieces("d")

    down.keep, down.send, pieces_d = bar(down.keep, down.send, pieces_d)
    down_got = down.core()
    gh, gbup, gbdown = hidden_back(net, me, pull, cotangent, pieces_d)
    gh, down_got = bar(gh, down_got)
    down_got = down.b(down_got)
    gsec, gmixed, ggain2, gshift2, gbout, *up_parts = second_back(
        net, me, gh, normed2, mixed, second, cotangent, pieces_u, vecs
    )
    gmixed, down_got, up_parts = bar(gmixed, down_got, up_parts)
    down_got = down.a(down_got)
    if net.fast:
        up = Scatter(net, up_parts)
    else:
        up, out = Scatter(net, up_parts[:1]), Scatter(net, up_parts[1:])
    gmixed, up.keep, up.send = bar(gmixed, up.keep, up.send)
    up_got = up.core()
    back = (qkv, gmixed, mixed, lse, far_t, HEADS)
    grads = attend_back(*back, 0, 4)
    grads, down_got, up_got = bar(grads, down_got, up_got)
    down_got = down.z(down_got, 1, 2, 3)
    up_got = up.b(up_got)
    grads = attend_back(*back, 1, 4, grads, 2)
    grads, down_got, up_got = bar(grads, down_got, up_got)
    up_got = up.a(up_got)
    grads = attend_back(*back, 3, 4, grads)
    (gq, gk, gv), up_got = bar(grads, up_got)
    up_got = up.z(up_got, 1, 2)
    gqkv = Scatter(net, weight_grad(net, me, [normed], [gq, gk, gv], "grad_qkv", most=True))
    gq, gqkv.keep, gqkv.send, up_got, up.keep = bar(gq, gqkv.keep, gqkv.send, up_got, up.keep)
    qkv_got = gqkv.core()
    up_got += up.z(None, 3)
    gfirst, ggain1, gshift1, gbskip, gbq, gbv = first_back(
        net, me, gq, gk, gv, raw, gsec, pieces_q, vecs
    )
    gfirst, qkv_got, ggain1, up_got = bar(gfirst, qkv_got, ggain1, up_got)
    qkv_got = gqkv.b(qkv_got)
    rows = [gbskip, ggain1, gshift1, gbq, gbv, gbout, ggain2, gshift2, gbdown, gbup.reshape(-1, width)]
    rows = sum_vectors(net, jnp.concatenate(rows, axis=0), 0, 1)
    gskip_w = Scatter(net, weight_grad(net, me, [frames, skip], [gfirst], "grad_skip", most=True))
    up_out = up.done(up_got, slice(0, 4 * width) if net.fast else slice(None))
    if net.fast:
        out_out = up.done(up_got, slice(4 * width, 5 * width))
    else:
        out_out = out.core()
    gfirst, gskip_w.keep, gskip_w.send, rows, qkv_got, up_out, out_out = bar(
        gfirst, gskip_w.keep, gskip_w.send, rows, qkv_got, up_out, out_out
    )
    qkv_got = gqkv.a(qkv_got)
    skip_got = gskip_w.core()
    rows = sum_vectors(net, rows, 1, 2)
    gframes, gskip = joined_back(net, me, gfirst, pieces_s)
    gframes, qkv_got, skip_got, second, rows = bar(gframes, qkv_got, skip_got, second, rows)
    skip_got = gskip_w.b(skip_got)
    qkv_got = gqkv.z(qkv_got, 1, 2)
    rows = sum_vectors(net, rows, 2, 3)
    layer_out = down_forward(net, me, second, act, pieces_d, vecs, 0, 2)
    layer_out, qkv_got, skip_got, rows, gqkv.keep = bar(layer_out, qkv_got, skip_got, rows, gqkv.keep)
    skip_got = gskip_w.a(skip_got)
    qkv_got += gqkv.z(None, 3)
    rows = sum_vectors(net, rows, 3, 4)
    layer_out = down_forward(net, me, second, act, pieces_d, vecs, 1, 2, [layer_out])
    layer_out, qkv_got, skip_got, rows, down.keep, down_got = bar(
        layer_out, qkv_got, skip_got, rows, down.keep, down_got
    )
    skip_got = gskip_w.z(skip_got, 1, 2, 3)
    rows = sum_vectors(net, rows, 4, net.bits)

    def mine(row):
        each = width // size
        return lax.dynamic_slice(rows[row], (index * each,), (each,))

    wide = rows[9:].reshape(-1)
    each = wide.shape[0] // size
    o_bup = lax.dynamic_slice(wide, (index * each,), (each,))
    return (
        layer_out,
        gframes,
        gskip,
        gskip_w.done(skip_got),
        mine(0),
        mine(1),
        mine(2),
        gqkv.done(qkv_got),
        mine(3),
        mine(4),
        out_out,
        mine(5),
        mine(6),
        mine(7),
        up_out,
        o_bup,
        down.done(down_got),
        mine(8),
    )


def solution(mesh):
    mat, vec = P(AXES, None), P(AXES)
    size = math.prod(mesh.shape.values())
    return jax.shard_map(
        functools.partial(body, size),
        mesh=mesh,
        in_specs=(
            mat, mat, mat, vec, mat,
            mat, vec, vec, vec, mat, vec, vec, mat, vec, vec, vec, mat, vec, mat, vec,
        ),
        out_specs=(
            mat, mat, mat,
            mat, vec, vec, vec, mat, vec, vec, mat, vec, vec, vec, mat, vec, mat, vec,
        ),
        check_vma=False,
    )
```
